32 devices in a mesh: gx: 4 (over x, core), gy: 8 (over z, y).
Axes of the slice: x: 2, y: 2, z: 4, core: 2. Of those that a mesh axis runs over, the one named last changes fastest.
Arguments:
- xy_noisy: bfloat16 [256, 128, 128], P('gx', 'gy'), may hold values from -6 to 6
- xz_plane: bfloat16 [256, 64, 128], P('gy'), may hold values from -6 to 6
- yz_plane: bfloat16 [128, 64, 128], P('gx'), may hold values from -6 to 6
- labels: int32 [256, 128, 4], P('gx', 'gy'), may hold values from 0 to 19
- timestep: int32 [1], replicated, may hold values from 0 to 999
- conv1_weight: bfloat16 [3, 3, 128, 128], replicated, may hold values from -0.1875 to 0.1875
- conv2_weight: bfloat16 [3, 3, 128, 128], replicated, may hold values from -0.1875 to 0.1875
- time_weight: bfloat16 [128, 128], replicated, may hold values from -0.5 to 0.5
- w1: bfloat16 [128, 256], replicated, may hold values from -0.5 to 0.5
- w2: bfloat16 [256, 256], replicated, may hold values from -0.375 to 0.375
- w3: bfloat16 [256, 20], replicated, may hold values from -0.375 to 0.375
Outputs:
- grad_conv1: float32 [3, 3, 128, 128], replicated
- grad_conv2: float32 [3, 3, 128, 128], replicated
- grad_time: float32 [128, 128], replicated
- grad_w1: float32 [128, 256], replicated
- grad_w2: float32 [256, 256], replicated
- grad_w3: float32 [256, 20], replicated
- grad_xz: float32 [256, 4, 128], P('gy')
- grad_yz: float32 [128, 4, 128], P('gx')
The draws below stay inside these ranges and needn't reach their ends.
All inputs are finite; a program needn't handle non-finite values.
Results may differ from the reference program's by a relative error of at most 0.014.
Values may be sent and summed in bfloat16 or wider, within the bound.
No kernel may reach another device: no remote copies, remote signals or barrier semaphores. Data moves between devices by JAX's collectives and lax.ppermute only.
A program may use at most 64 MiB of HBM per device.

```python
import math
import jax
import jax.numpy as jnp
from jax import lax

C = 128
HID = 256
CLS = 20
Z = 64
SLAB = 4
TX = 64
X = 256
Y = 128


def with_ends(drawn, key, least, high):
    longest = drawn.shape.index(max(drawn.shape))
    spots = []
    for shift in (0, 1):
        where = [jax.random.randint(jax.random.fold_in(key, axis), (), 0, length) for axis, length in enumerate(drawn.shape)]
        where[longest] = (where[longest] + shift) % drawn.shape[longest]
        spots.append(tuple(where))
    return drawn.at[spots[0]].set(least).at[spots[1]].set(high)


def level_of(rng, extent, split, smallest, largest):
    def one(position, blocks):
        draws = jax.random.uniform(jax.random.fold_in(jax.random.fold_in(rng, 6), position), (blocks,), jnp.float32, smallest / len(split), largest / len(split))
        return jnp.repeat(jnp.exp(draws), extent[position] // blocks).reshape((-1,) + (1,) * (len(extent) - position - 1))

    level = one(*split[0])
    for cut in split[1:]:
        level = level * one(*cut)
    return level


def bell_draw(rng, dims, deviation, bound, shards=(), kind=jnp.bfloat16):
    factor_of = level_of(rng, dims, shards, -0.22, 0.18) if shards else 1.0
    values = jax.random.normal(rng, dims, jnp.float32) * deviation * factor_of
    return jnp.minimum(jnp.maximum(values, -bound), bound).astype(kind)


def setup_inputs(seed: int = 0) -> dict:
    seeds = jax.random.split(jax.random.key(seed), 12)
    xy_noisy = bell_draw(seeds[0], (X, Y, C), 1.0, 6.0, ((0, 4), (1, 8)))
    xz_plane = bell_draw(seeds[1], (X, Z, C), 1.0, 6.0, ((0, 8),))
    yz_plane = bell_draw(seeds[2], (Y, Z, C), 1.0, 6.0, ((0, 4),))
    labels = with_ends(jax.random.randint(seeds[3], (X, Y, SLAB), 0, CLS), jax.random.fold_in(seeds[3], 1), 0, CLS - 1).astype(jnp.int32)
    timestep = jax.random.randint(seeds[4], (1,), 0, 1000).astype(jnp.int32)
    conv1_weight = bell_draw(seeds[5], (3, 3, C, C), (9 * C) ** -0.5, 0.1875)
    conv2_weight = bell_draw(seeds[6], (3, 3, C, C), (9 * C) ** -0.5, 0.1875)
    time_weight = bell_draw(seeds[7], (C, C), C ** -0.5, 0.5)
    w1 = bell_draw(seeds[8], (C, HID), C ** -0.5, 0.5)
    w2 = bell_draw(seeds[9], (HID, HID), HID ** -0.5, 0.375)
    w3 = bell_draw(seeds[10], (HID, CLS), HID ** -0.5, 0.375)
    return {"xy_noisy": xy_noisy, "xz_plane": xz_plane, "yz_plane": yz_plane, "labels": labels, "timestep": timestep, "conv1_weight": conv1_weight, "conv2_weight": conv2_weight, "time_weight": time_weight, "w1": w1, "w2": w2, "w3": w3}


loss_weight = 1.0 / 256.0

def silu_grad(value):
    sig = jax.nn.sigmoid(value)
    return sig * (1.0 + value * (1.0 - sig))

def patches(padded, nrows, ncols):
    taps = [padded[a:a + nrows, b:b + ncols] for a in range(3) for b in range(3)]
    return jnp.concatenate(taps, axis=-1).reshape(nrows * ncols, -1)

def time_embedding(timestep, width):
    half = width // 2
    freqs = jnp.exp(-math.log(10000.0) * jnp.arange(half, dtype=jnp.float32) / half)
    angle = timestep.astype(jnp.float32)[0] * freqs
    return jnp.concatenate([jnp.cos(angle), jnp.sin(angle)])

def decode(feat, label_flat, w1, w2, w3):
    u1 = jnp.dot(feat, w1, preferred_element_type=jnp.float32)
    g1 = jax.nn.silu(u1).astype(jnp.bfloat16)
    u2 = jnp.dot(g1, w2, preferred_element_type=jnp.float32)
    g2 = jax.nn.silu(u2).astype(jnp.bfloat16)
    logits = jnp.dot(g2, w3, preferred_element_type=jnp.float32)
    prob = jax.nn.softmax(logits, axis=-1)
    onehot = (label_flat[:, None] == jnp.arange(w3.shape[1], dtype=jnp.int32)[None, :]).astype(jnp.float32)
    dlogits = (loss_weight * (prob - onehot)).astype(jnp.bfloat16)
    dw3 = jnp.dot(g2.T, dlogits, preferred_element_type=jnp.float32)
    dg2 = jnp.dot(dlogits, w3.T, preferred_element_type=jnp.float32)
    du2 = (dg2 * silu_grad(u2)).astype(jnp.bfloat16)
    dw2 = jnp.dot(g1.T, du2, preferred_element_type=jnp.float32)
    dg1 = jnp.dot(du2, w2.T, preferred_element_type=jnp.float32)
    du1 = (dg1 * silu_grad(u1)).astype(jnp.bfloat16)
    dw1 = jnp.dot(feat.T, du1, preferred_element_type=jnp.float32)
    dfeat = jnp.dot(du1, w1.T, preferred_element_type=jnp.float32)
    return (dfeat, dw1, dw2, dw3)

def conv_full(padded, w_flat, block):
    nrows = padded.shape[0] - 2
    ncols = padded.shape[1] - 2

    def one_block(index):
        piece = lax.dynamic_slice_in_dim(padded, index * block, block + 2, 0)
        out = jnp.dot(patches(piece, block, ncols), w_flat, preferred_element_type=jnp.float32)
        return out.reshape(block, ncols, -1)
    result = lax.map(one_block, jnp.arange(nrows // block, dtype=jnp.int32))
    return result.reshape(nrows, ncols, -1)

def conv_weight_grad(padded, dout, block):
    nrows, ncols, width = dout.shape

    def step(total, index):
        piece = lax.dynamic_slice_in_dim(padded, index * block, block + 2, 0)
        grad_piece = lax.dynamic_slice_in_dim(dout, index * block, block, 0).reshape(block * ncols, width)
        return (total + jnp.dot(patches(piece, block, ncols).T, grad_piece, preferred_element_type=jnp.float32), None)
    total, _ = lax.scan(step, jnp.zeros((9 * padded.shape[2], width), jnp.float32), jnp.arange(nrows // block, dtype=jnp.int32))
    return total

def reference(xy_noisy, xz_plane, yz_plane, labels, timestep, conv1_weight, conv2_weight, time_weight, w1, w2, w3):
    width = xy_noisy.shape[2]
    emb = time_embedding(timestep, width)
    temb = jnp.dot(emb, time_weight.astype(jnp.float32), precision=lax.Precision.HIGHEST)
    spacing = ((1, 1), (1, 1), (0, 0))
    pad0 = jnp.pad(xy_noisy, spacing)
    h1 = conv_full(pad0, conv1_weight.reshape(9 * width, width), TX) + temb
    a1 = jax.nn.silu(h1).astype(jnp.bfloat16)
    pad1 = jnp.pad(a1, spacing)
    xyd = conv_full(pad1, conv2_weight.reshape(9 * width, width), TX).astype(jnp.bfloat16)
    start = (timestep[0] % (Z // SLAB) * SLAB).astype(jnp.int32)
    xz_slab = lax.dynamic_slice_in_dim(xz_plane, start, SLAB, 1).astype(jnp.float32)
    yz_slab = lax.dynamic_slice_in_dim(yz_plane, start, SLAB, 1).astype(jnp.float32)

    def mlp_step(carry, index):
        xy_rows = lax.dynamic_slice_in_dim(xyd, index * TX, TX, 0).astype(jnp.float32)
        xz_rows = lax.dynamic_slice_in_dim(xz_slab, index * TX, TX, 0)
        label_rows = lax.dynamic_slice_in_dim(labels, index * TX, TX, 0)
        feat = xy_rows[:, :, None, :] + xz_rows[:, None, :, :] + yz_slab[None, :, :, :]
        feat = feat.astype(jnp.bfloat16).reshape(-1, width)
        dfeat, dw1, dw2, dw3 = decode(feat, label_rows.reshape(-1), w1, w2, w3)
        dfeat = dfeat.reshape(TX, Y, SLAB, width)
        carry = (carry[0] + dw1, carry[1] + dw2, carry[2] + dw3, carry[3] + lax.optimization_barrier(jnp.sum(dfeat, axis=0)))
        return (carry, (lax.optimization_barrier(jnp.sum(dfeat, axis=1)), lax.optimization_barrier(jnp.sum(dfeat, axis=2)).astype(jnp.bfloat16)))
    start_carry = (jnp.zeros(w1.shape, jnp.float32), jnp.zeros(w2.shape, jnp.float32), jnp.zeros(w3.shape, jnp.float32), jnp.zeros((Y, SLAB, width), jnp.float32))
    carry, outs = lax.scan(mlp_step, start_carry, jnp.arange(X // TX, dtype=jnp.int32))
    grad_w1, grad_w2, grad_w3, grad_yz = carry
    grad_xz = outs[0].reshape(X, SLAB, width)
    dxyd = outs[1].reshape(X, Y, width)
    grad_conv2 = conv_weight_grad(pad1, dxyd, TX).reshape(3, 3, width, width)
    back_flat = jnp.transpose(conv2_weight[::-1, ::-1], (0, 1, 3, 2)).reshape(9 * width, width)
    da1 = conv_full(jnp.pad(dxyd, spacing), back_flat, TX)
    dh1 = (da1 * silu_grad(h1)).astype(jnp.bfloat16)
    grad_conv1 = conv_weight_grad(pad0, dh1, TX).reshape(3, 3, width, width)
    grad_time = jnp.outer(emb, lax.optimization_barrier(jnp.sum(dh1.astype(jnp.float32), axis=(0, 1))))
    return (grad_conv1, grad_conv2, grad_time, grad_w1, grad_w2, grad_w3, grad_xz, grad_yz)
```

```python
import math

import jax
import jax.numpy as jnp
from jax import lax
from jax.sharding import PartitionSpec as P

loss_weight = 1.0 / 256.0
BOTH = ("gx", "gy")
LANES = 128


def silu_grad(value):
    sig = jax.nn.sigmoid(value)
    return sig * (1.0 + value * (1.0 - sig))


def patches(padded, nrows, ncols):
    taps = [padded[a : a + nrows, b : b + ncols] for a in range(3) for b in range(3)]
    return jnp.concatenate(taps, axis=-1).reshape(nrows * ncols, -1)


def time_embedding(timestep, width):
    half = width // 2
    freqs = jnp.exp(-math.log(10000.0) * jnp.arange(half, dtype=jnp.float32) / half)
    angle = timestep.astype(jnp.float32)[0] * freqs
    return jnp.concatenate([jnp.cos(angle), jnp.sin(angle)])


class Grid:
    def __init__(self):
        self.nx, self.ny = lax.axis_size("gx"), lax.axis_size("gy")
        self.count = self.ny // self.nx
        self.ix, self.iy = lax.axis_index("gx"), lax.axis_index("gy")

    def move(self, array, target):
        pairs = []
        for i in range(self.nx):
            for j in range(self.ny):
                k, m = target(i, j)
                if 0 <= k < self.nx and 0 <= m < self.ny:
                    pairs.append((i * self.ny + j, k * self.ny + m))
        return lax.ppermute(array, BOTH, pairs)

    def turned(self, shift):
        count = self.count
        return lambda i, j: (j // count, count * i + (j % count + shift) % count)


def decode_forward(feat, label_flat, w1, w2, w3):
    u1 = jnp.dot(feat, w1, preferred_element_type=jnp.float32)
    g1 = jax.nn.silu(u1).astype(jnp.bfloat16)
    u2 = jnp.dot(g1, w2, preferred_element_type=jnp.float32)
    g2 = jax.nn.silu(u2).astype(jnp.bfloat16)
    logits = jnp.dot(g2, w3, preferred_element_type=jnp.float32)
    prob = jax.nn.softmax(logits, axis=-1)
    onehot = (label_flat[:, None] == jnp.arange(w3.shape[1], dtype=jnp.int32)[None, :]).astype(
        jnp.float32
    )
    dlogits = (loss_weight * (prob - onehot)).astype(jnp.bfloat16)
    dg2 = jnp.dot(dlogits, w3.T, preferred_element_type=jnp.float32)
    du2 = (dg2 * silu_grad(u2)).astype(jnp.bfloat16)
    dg1 = jnp.dot(du2, w2.T, preferred_element_type=jnp.float32)
    du1 = (dg1 * silu_grad(u1)).astype(jnp.bfloat16)
    dfeat = jnp.dot(du1, w1.T, preferred_element_type=jnp.float32)
    return g1, g2, dlogits, du2, du1, dfeat


def local(
    xy_noisy,
    xz_plane,
    yz_plane,
    labels,
    timestep,
    conv1_weight,
    conv2_weight,
    time_weight,
    w1,
    w2,
    w3,
):
    f32, bf16 = jnp.float32, jnp.bfloat16
    grid = Grid()
    nrows, ncols, width = xy_noisy.shape
    depth = labels.shape[2]
    count = grid.count
    side = grid.iy % count
    emb = time_embedding(timestep, width)
    temb = jnp.dot(emb, time_weight.astype(f32), precision=lax.Precision.HIGHEST)
    flat_one = conv1_weight.reshape(9 * width, width)
    flat_two = conv2_weight.reshape(9 * width, width)

    slab_count = xz_plane.shape[1] // depth
    start = timestep[0] % slab_count * depth
    xz_local = lax.dynamic_slice_in_dim(xz_plane, start, depth, 1)
    yz_local = lax.dynamic_slice_in_dim(yz_plane, start, depth, 1)
    share = xz_local.shape[0]
    yz_half = lax.dynamic_slice_in_dim(yz_local, side * ncols, ncols, 0)

    label_bf = labels.astype(bf16)
    up = lambda i, j: (i + 1, j)
    down = lambda i, j: (i - 1, j)
    left = lambda i, j: (i, j - 1)
    right = lambda i, j: (i, j + 1)
    reach = 3

    def pack(parts):
        flat = []
        for part in parts:
            part = part.reshape(-1)
            flat.append(jnp.pad(part, (0, -part.size % LANES)).reshape(-1, LANES))
        return jnp.concatenate(flat, axis=0)

    def unpack(packed, shapes):
        out, at = [], 0
        for shape in shapes:
            size = math.prod(shape)
            rows = -(-size // LANES)
            out.append(packed[at : at + rows].reshape(-1)[:size].reshape(shape))
            at += rows
        return out

    row_shapes = ((reach, ncols, width), (1, ncols, depth))
    above, label_above = unpack(
        grid.move(pack([xy_noisy[nrows - reach :], label_bf[nrows - 1 :]]), up), row_shapes
    )
    below, label_below = unpack(
        grid.move(pack([xy_noisy[:reach], label_bf[:1]]), down), row_shapes
    )
    first = grid.move(pack([yz_half, xz_local]), grid.turned(0))
    second = grid.move(xz_local, grid.turned(1))
    yz_cols, xz_same = unpack(first, ((ncols, depth, width), (share, depth, width)))
    xz_rows = jnp.where(
        side == 0,
        jnp.concatenate([xz_same, second], axis=0),
        jnp.concatenate([second, xz_same], axis=0),
    )
    edge = jnp.where(side == 0, xz_local[:1], xz_local[share - 1 :])
    rim_a = grid.move(
        edge, lambda i, j: (j // count - 1, count * i + 1) if j % count == 0 else (j // count + 1, count * i)
    )
    rim_b = grid.move(
        edge, lambda i, j: (j // count - 1, count * i) if j % count == 0 else (j // count + 1, count * i + 1)
    )
    xz_above = jnp.where(side == 0, rim_a, rim_b)
    xz_below = jnp.where(side == 0, rim_b, rim_a)

    tall = jnp.concatenate([above, xy_noisy, below], axis=0)
    label_tall = jnp.concatenate([label_above, label_bf, label_below], axis=0)
    col_shapes = ((nrows + 2 * reach, reach, width), (nrows + 2, 1, depth), (1, depth, width))
    before, label_before, yz_before = unpack(
        grid.move(pack([tall[:, ncols - reach :], label_tall[:, ncols - 1 :], yz_cols[ncols - 1 :]]), right),
        col_shapes,
    )
    after, label_after, yz_after = unpack(
        grid.move(pack([tall[:, :reach], label_tall[:, :1], yz_cols[:1]]), left), col_shapes
    )
    wide = jnp.concatenate([before, tall, after], axis=1)

    def inside(margin):
        rows = jnp.arange(-margin, nrows + margin) + grid.ix * nrows
        cols = jnp.arange(-margin, ncols + margin) + grid.iy * ncols
        row_ok = (rows >= 0) & (rows < nrows * grid.nx)
        col_ok = (cols >= 0) & (cols < ncols * grid.ny)
        return (row_ok[:, None] & col_ok[None, :])[:, :, None]

    h1 = (
        jnp.dot(patches(wide, nrows + 4, ncols + 4), flat_one, preferred_element_type=f32).reshape(
            nrows + 4, ncols + 4, width
        )
        + temb
    )
    a1 = jnp.where(inside(2), jax.nn.silu(h1), 0.0).astype(bf16)
    xyd = jnp.dot(patches(a1, nrows + 2, ncols + 2), flat_two, preferred_element_type=f32)
    xyd = xyd.astype(bf16).reshape(nrows + 2, ncols + 2, width)

    xz_all = jnp.concatenate([xz_above, xz_rows, xz_below], axis=0).astype(f32)
    yz_all = jnp.concatenate([yz_before, yz_cols, yz_after], axis=0).astype(f32)
    label_all = jnp.concatenate([label_before, label_tall, label_after], axis=1).astype(jnp.int32)

    def features(rows, cols):
        tile = xyd[rows, cols].astype(f32)
        feat = tile[:, :, None, :] + xz_all[rows, None, :, :] + yz_all[None, cols, :, :]
        return feat.astype(bf16).reshape(-1, width), label_all[rows, cols].reshape(-1)

    mid_r, mid_c = slice(1, nrows + 1), slice(1, ncols + 1)
    feat, lab = features(mid_r, mid_c)
    g1, g2, dlogits, du2, du1, dfeat = decode_forward(feat, lab, w1, w2, w3)
    dw3 = jnp.dot(g2.T, dlogits, preferred_element_type=f32)
    dw2 = jnp.dot(g1.T, du2, preferred_element_type=f32)
    dw1 = jnp.dot(feat.T, du1, preferred_element_type=f32)
    dfeat = dfeat.reshape(nrows, ncols, depth, width)
    dxz = jnp.sum(dfeat, axis=1)
    dyz = jnp.sum(dfeat, axis=0)
    dxyd = jnp.sum(dfeat, axis=2).astype(bf16)

    rims = (
        (slice(0, 1), slice(0, ncols + 2)),
        (slice(nrows + 1, nrows + 2), slice(0, ncols + 2)),
        (mid_r, slice(0, 1)),
        (mid_r, slice(ncols + 1, ncols + 2)),
    )
    rim_feat, rim_lab = zip(*[features(*r) for r in rims])
    *_, rim_dfeat = decode_forward(jnp.concatenate(rim_feat), jnp.concatenate(rim_lab), w1, w2, w3)
    rim_d = jnp.sum(rim_dfeat.reshape(-1, depth, width), axis=1).astype(bf16)
    n = ncols + 2
    top, bottom = rim_d[:n].reshape(1, n, width), rim_d[n : 2 * n].reshape(1, n, width)
    west = rim_d[2 * n : 2 * n + nrows].reshape(nrows, 1, width)
    east = rim_d[2 * n + nrows :].reshape(nrows, 1, width)
    dxyd_all = jnp.concatenate([top, jnp.concatenate([west, dxyd, east], axis=1), bottom], axis=0)
    dxyd_all = jnp.where(inside(1), dxyd_all, jnp.zeros_like(dxyd_all))

    grad_conv2 = jnp.dot(
        patches(a1[1:-1, 1:-1], nrows, ncols).T, dxyd.reshape(-1, width), preferred_element_type=f32
    )
    back_flat = jnp.transpose(conv2_weight[::-1, ::-1], (0, 1, 3, 2)).reshape(9 * width, width)
    da1 = jnp.dot(
        patches(dxyd_all, nrows, ncols), back_flat, preferred_element_type=f32
    ).reshape(nrows, ncols, width)
    dh1 = (da1 * silu_grad(h1[2:-2, 2:-2])).astype(bf16)
    grad_conv1 = jnp.dot(
        patches(wide[2:-2, 2:-2], nrows, ncols).T, dh1.reshape(-1, width), preferred_element_type=f32
    )
    time_total = jnp.sum(dh1.astype(f32), axis=(0, 1))

    def both(own, got):
        return own.astype(f32) + got.astype(f32)

    dxz = dxz.astype(bf16)
    low, high = dxz[:share], dxz[share:]
    keep = jnp.where(side == 0, low, high)
    give = jnp.where(side == 0, high, low)
    xz_sum = both(keep, grid.move(give, lambda i, j: (i, j ^ 1)))
    bit = 2
    while bit < grid.ny:
        own = xz_sum.astype(bf16)
        xz_sum = both(own, grid.move(own, lambda i, j, bit=bit: (i, j ^ bit)))
        bit *= 2
    grad_xz = grid.move(xz_sum.astype(bf16), grid.turned(0)).astype(f32)
    yz_sum = dyz
    bit = 1
    while bit < grid.nx:
        own = yz_sum.astype(bf16)
        yz_sum = both(own, grid.move(own, lambda i, j, bit=bit: (i ^ bit, j)))
        bit *= 2
    yz_sum = yz_sum.astype(bf16)
    yz_same = grid.move(yz_sum, grid.turned(0))
    yz_other = grid.move(yz_sum, grid.turned(1))
    grad_yz = jnp.where(
        side == 0,
        jnp.concatenate([yz_same, yz_other], axis=0),
        jnp.concatenate([yz_other, yz_same], axis=0),
    ).astype(f32)

    parts = (grad_conv1, grad_conv2, dw1, dw2, dw3, time_total)
    chips = grid.nx * grid.ny // 2
    rows = sum(-(-p.size // LANES) for p in parts)
    each = -(-rows // (2 * chips * 8)) * 8
    packed = pack(parts)
    packed = jnp.pad(packed, ((0, 2 * chips * each - rows), (0, 0))).reshape(2, chips, each, LANES)
    core = grid.ix % 2
    own = lax.dynamic_index_in_dim(packed, core, 0, keepdims=False)
    other = lax.dynamic_index_in_dim(packed, 1 - core, 0, keepdims=False).astype(bf16)
    own = own + grid.move(other, lambda i, j: (i ^ 1, j)).astype(f32)
    groups = [
        [i * grid.ny + j for i in range(c, grid.nx, 2) for j in range(grid.ny)] for c in range(2)
    ]
    pieces = lax.all_to_all(own.astype(bf16), BOTH, 0, 0, axis_index_groups=groups)
    total = jnp.sum(pieces.astype(f32), axis=0).astype(bf16)
    spread = jnp.broadcast_to(total[None], (chips, each, LANES))
    half = lax.all_to_all(spread, BOTH, 0, 0, axis_index_groups=groups)
    partner = grid.move(half, lambda i, j: (i ^ 1, j))
    whole = jnp.where(core == 0, jnp.stack([half, partner]), jnp.stack([partner, half]))
    whole = whole.reshape(-1, LANES)
    summed = [s.astype(f32) for s in unpack(whole, [p.shape for p in parts])]
    return (
        summed[0].reshape(3, 3, width, width),
        summed[1].reshape(3, 3, width, width),
        jnp.outer(emb, summed[5]),
        summed[2],
        summed[3],
        summed[4],
        grad_xz,
        grad_yz,
    )


def solution(mesh):
    placed = (
        P("gx", "gy", None),
        P("gy", None, None),
        P("gx", None, None),
        P("gx", "gy", None),
        P(),
        P(),
        P(),
        P(),
        P(),
        P(),
        P(),
    )
    return jax.shard_map(
        local,
        mesh=mesh,
        in_specs=placed,
        out_specs=(P(), P(), P(), P(), P(), P(), P("gy", None, None), P("gx", None, None)),
        check_vma=False,
    )
```

```python
import functools
import math

import jax
import jax.numpy as jnp
from jax import lax
from jax.experimental import pallas as pl
from jax.experimental.pallas import tpu as pltpu
from jax.sharding import PartitionSpec as P

loss_weight = 1.0 / 256.0
BOTH = ("gx", "gy")
LANES = 128
PITCH = 24
REACH = 3
CLASS_ROWS = 32
F32, BF16 = jnp.float32, jnp.bfloat16
VMEM_LIMIT = 48 * 1024 * 1024


def sigmoid(value):
    return 0.5 * jnp.tanh(0.5 * value) + 0.5


def silu_pair(value):
    sig = sigmoid(value)
    out = value * sig
    return out, sig + out - out * sig


def dot(a, b):
    return jnp.dot(a, b, preferred_element_type=F32)


def dot_nt(a, b):
    return lax.dot_general(a, b, (((1,), (1,)), ((), ())), preferred_element_type=F32)


def dot_tn(a, b):
    return lax.dot_general(a, b, (((0,), (0,)), ((), ())), preferred_element_type=F32)


def time_embedding(timestep, width):
    half = width // 2
    freqs = jnp.exp(-math.log(10000.0) * jnp.arange(half, dtype=jnp.float32) / half)
    angle = timestep.astype(jnp.float32)[0] * freqs
    return jnp.concatenate([jnp.cos(angle), jnp.sin(angle)])


class Grid:
    def __init__(self):
        self.nx, self.ny = lax.axis_size("gx"), lax.axis_size("gy")
        self.count = self.ny // self.nx
        self.ix, self.iy = lax.axis_index("gx"), lax.axis_index("gy")

    def move(self, array, target):
        pairs = []
        for i in range(self.nx):
            for j in range(self.ny):
                k, m = target(i, j)
                if 0 <= k < self.nx and 0 <= m < self.ny:
                    pairs.append((i * self.ny + j, k * self.ny + m))
        return lax.ppermute(array, BOTH, pairs)

    def turned(self, shift):
        count = self.count
        return lambda i, j: (j // count, count * i + (j % count + shift) % count)


def gradient_rows(width, hidden):
    sizes = (
        ("conv1", 9 * width),
        ("conv2", 9 * width),
        ("w1", width * hidden // LANES),
        ("w2", hidden * hidden // LANES),
        ("w3", CLASS_ROWS * hidden // LANES),
        ("time", 16),
    )
    at, total = {}, 0
    for name, rows in sizes:
        at[name] = total
        total += rows
    return at, total


def main_kernel(
    classes,
    place,
    xy,
    above,
    below,
    before,
    after,
    labels,
    xz_same,
    xz_second,
    xz_above,
    xz_below,
    yz_cols,
    temb,
    conv1,
    conv2,
    back,
    w1,
    w2,
    w3,
    packed,
    dxz_out,
    dyz_out,
    xs,
    hs,
    acts,
    xyds,
    dx,
    patch,
    xzs,
    dw1,
    dw2,
    dw3,
    dyz,
):
    nrows, ncols, width = xy.shape
    depth = labels.shape[2]
    hidden = w1.shape[1]
    share = xz_same.shape[1]
    at, _ = gradient_rows(width, hidden)
    side = place[0]
    open_up, open_down, open_left, open_right = (place[1] > 0, place[2] > 0, place[3] > 0, place[4] > 0)

    mid_r, mid_c = slice(REACH, REACH + nrows), slice(REACH, REACH + ncols)
    xs[...] = jnp.zeros_like(xs)
    xs[mid_r, mid_c] = xy[...].astype(F32)
    xs[0:REACH, mid_c] = above[0:REACH].astype(F32)
    xs[REACH + nrows : 2 * REACH + nrows, mid_c] = below[0:REACH].astype(F32)
    xs[:, 0:REACH] = before[...].astype(F32)[:, 0:REACH]
    xs[:, REACH + ncols : 2 * REACH + ncols] = after[...].astype(F32)[:, 0:REACH]

    def gather(source, row, col, rows, cols):
        count = rows * cols
        for a in range(3):
            for b in range(3):
                piece = source[row + a : row + a + rows, col + b : col + b + cols, :]
                tap = (3 * a + b) * width
                patch[0:count, tap : tap + width] = piece.reshape(count, width).astype(BF16)
        return count

    n1 = gather(xs, 0, 0, nrows + 4, PITCH)
    h1 = dot(patch[0:n1], conv1[...]) + temb[...]
    h1 = h1.reshape(nrows + 4, PITCH, width)
    hs[...] = h1
    row = lax.broadcasted_iota(jnp.int32, h1.shape, 0)
    col = lax.broadcasted_iota(jnp.int32, h1.shape, 1)
    low_r = jnp.where(open_up, 0, 2)
    high_r = jnp.where(open_down, nrows + 4, nrows + 2)
    low_c = jnp.where(open_left, 0, 2)
    high_c = jnp.where(open_right, ncols + 4, ncols + 2)
    inside = (row >= low_r) & (row < high_r) & (col >= low_c) & (col < high_c)
    a1 = jnp.where(inside, h1 * sigmoid(h1), 0.0)
    acts[...] = jnp.zeros_like(acts)
    acts[:, 0:PITCH] = a1.astype(BF16).astype(F32)
    n2 = gather(acts, 0, 0, nrows + 2, PITCH)
    xyd = dot(patch[0:n2], conv2[...])
    xyds[...] = xyd.astype(BF16).astype(F32).reshape(nrows + 2, PITCH, width)

    xzs[:, pl.ds(pl.multiple_of(side * share, share), share), :] = xz_same[...].astype(F32)
    xzs[:, pl.ds(pl.multiple_of((1 - side) * share, share), share), :] = xz_second[...].astype(F32)

    def decode(feat, label):
        u1 = dot(feat, w1[...])
        g1, s1 = silu_pair(u1)
        g1 = g1.astype(BF16)
        u2 = dot(g1, w2[...])
        g2, s2 = silu_pair(u2)
        g2 = g2.astype(BF16)
        logits = dot(g2, w3[...])
        lane = lax.broadcasted_iota(jnp.int32, logits.shape, 1)
        logits = jnp.where(lane < classes, logits, -jnp.inf)
        power = jnp.exp(logits - jnp.max(logits, axis=1, keepdims=True))
        prob = power / jnp.sum(power, axis=1, keepdims=True)
        onehot = jnp.where(lane == label, 1.0, 0.0)
        dlogits = (loss_weight * (prob - onehot)).astype(BF16)
        du2 = (dot_nt(dlogits, w3[...]) * s2).astype(BF16)
        du1 = (dot_nt(du2, w2[...]) * s1).astype(BF16)
        return g1, g2, dlogits, du2, du1, dot_nt(du1, w1[...])

    dw1[...] = jnp.zeros_like(dw1)
    dw2[...] = jnp.zeros_like(dw2)
    dw3[...] = jnp.zeros_like(dw3)
    dyz[...] = jnp.zeros_like(dyz)
    dx[...] = jnp.zeros_like(dx)
    chunk = 16
    size = chunk * ncols

    def step(index, carry):
        r0 = pl.multiple_of(index * chunk, chunk)
        tile = xyds[pl.ds(r0 + 1, chunk), 1 : ncols + 1, :]
        lab = labels[pl.ds(r0, chunk)].reshape(size, depth)
        feats, labs = [], []
        for k in range(depth):
            xz_k = xzs[k, pl.ds(r0, chunk), :]
            feat = tile + xz_k[:, None, :] + yz_cols[k].astype(F32)[None]
            feats.append(feat.reshape(size, width).astype(BF16))
            labs.append(jnp.broadcast_to(lab[:, k : k + 1], (size, LANES)))
        feat = jnp.concatenate(feats, axis=0)
        g1, g2, dlogits, du2, du1, dfeat = decode(feat, jnp.concatenate(labs, axis=0))
        dw3[...] += dot_tn(dlogits, g2)
        dw2[...] += dot_tn(g1, du2)
        dw1[...] += dot_tn(feat, du1)
        total = jnp.zeros((chunk, ncols, width), F32)
        for k in range(depth):
            piece = dfeat[k * size : (k + 1) * size].reshape(chunk, ncols, width)
            total = total + piece
            dxz_out[k, pl.ds(r0, chunk), :] = jnp.sum(piece, axis=1).astype(BF16)
            dyz[k] += jnp.sum(piece, axis=0)
        dx[pl.ds(r0 + 1, chunk), 1 : ncols + 1, :] = total.astype(BF16).astype(F32)
        return carry

    lax.fori_loop(0, nrows // chunk, step, 0)
    dyz_out[...] = dyz[...].astype(BF16)

    lab_before = before[2 : nrows + 4, 3, :].astype(F32).astype(jnp.int32)
    lab_after = after[2 : nrows + 4, 3, :].astype(F32).astype(jnp.int32)
    lab_up = above[3].astype(F32).astype(jnp.int32)
    lab_down = below[3].astype(F32).astype(jnp.int32)
    tail = jnp.zeros((PITCH - ncols - 2, LANES), jnp.int32)
    lab_rim = jnp.concatenate(
        [
            lab_before[0:1],
            lab_up,
            lab_after[0:1],
            tail,
            lab_before[nrows + 1 : nrows + 2],
            lab_down,
            lab_after[nrows + 1 : nrows + 2],
            tail,
            lab_before[1 : nrows + 1],
            lab_after[1 : nrows + 1],
        ],
        axis=0,
    )
    rim_at = (0, 1, nrows + 2 * REACH - 2, nrows + 2 * REACH - 1)
    feats, labs = [], []
    zero_tail = jnp.zeros((PITCH - ncols - 2, width), F32)
    for k in range(depth):
        yz_before = before[rim_at[k], 3:4, :].astype(F32)
        yz_after = after[rim_at[k], 3:4, :].astype(F32)
        yz_row = jnp.concatenate([yz_before, yz_cols[k].astype(F32), yz_after, zero_tail], axis=0)
        feats.append(xyds[0] + xz_above[k].astype(F32) + yz_row)
        feats.append(xyds[nrows + 1] + xz_below[k].astype(F32) + yz_row)
        feats.append(xyds[1 : nrows + 1, 0, :] + xzs[k] + yz_before)
        feats.append(xyds[1 : nrows + 1, ncols + 1, :] + xzs[k] + yz_after)
        labs.append(jnp.broadcast_to(lab_rim[:, k : k + 1], (2 * PITCH + 2 * nrows, LANES)))
    rim = decode(jnp.concatenate(feats, axis=0).astype(BF16), jnp.concatenate(labs, axis=0))[-1]
    span = 2 * PITCH + 2 * nrows
    rim_sum = rim[0:span]
    for k in range(1, depth):
        rim_sum = rim_sum + rim[k * span : (k + 1) * span]
    rim_sum = rim_sum.astype(BF16).astype(F32)
    rcol = lax.broadcasted_iota(jnp.int32, (PITCH, width), 0)
    keep = (rcol >= jnp.where(open_left, 0, 1)) & (rcol < jnp.where(open_right, ncols + 2, ncols + 1))
    dx[0] = jnp.where(keep & open_up, rim_sum[0:PITCH], 0.0)
    dx[nrows + 1] = jnp.where(keep & open_down, rim_sum[PITCH : 2 * PITCH], 0.0)
    west = rim_sum[2 * PITCH : 2 * PITCH + nrows]
    east = rim_sum[2 * PITCH + nrows : span]
    dx[1 : nrows + 1, 0, :] = jnp.where(open_left, west, 0.0)
    dx[1 : nrows + 1, ncols + 1, :] = jnp.where(open_right, east, 0.0)

    def weight_gradient(start, dout):
        grad = dot_tn(dout, patch[0 : nrows * ncols])
        for tap in range(9):
            block = grad[:, tap * width : (tap + 1) * width].T
            packed[start + tap * width : start + (tap + 1) * width, :] = block.astype(BF16)

    n3 = gather(acts, 1, 1, nrows, ncols)
    dxyd = dx[1 : nrows + 1, 1 : ncols + 1, :].reshape(n3, width).astype(BF16)
    weight_gradient(at["conv2"], dxyd)
    gather(dx, 0, 0, nrows, ncols)
    da1 = dot(patch[0:n3], back[...])
    _, slope = silu_pair(hs[2 : nrows + 2, 2 : ncols + 2, :].reshape(n3, width))
    dh1 = (da1 * slope).astype(BF16)
    gather(xs, 2, 2, nrows, ncols)
    weight_gradient(at["conv1"], dh1)

    parts = ((at["w1"], dw1, width), (at["w2"], dw2, hidden), (at["w3"], dw3, CLASS_ROWS))
    for start, ref, rows in parts:
        for half in range(hidden // LANES):
            packed[start + half * rows : start + (half + 1) * rows, :] = ref[
                0:rows, half * LANES : (half + 1) * LANES
            ].astype(BF16)
    time_row = jnp.sum(dh1.astype(F32), axis=0, keepdims=True)
    packed[at["time"] : at["time"] + 16, :] = jnp.broadcast_to(time_row, (16, LANES)).astype(BF16)
    used = at["time"] + 16
    if packed.shape[0] > used:
        packed[used:, :] = jnp.zeros((packed.shape[0] - used, LANES), BF16)


def last_kernel(hidden, classes, place, half, partner, emb, g1, g2, gt, gw1, gw2, gw3, whole):
    rows = half.shape[0]
    width = emb.shape[0]
    at, _ = gradient_rows(width, hidden)
    core = place[0]
    whole[pl.ds(pl.multiple_of(core * rows, rows), rows), :] = half[...]
    whole[pl.ds(pl.multiple_of((1 - core) * rows, rows), rows), :] = partner[...]
    g1[...] = whole[at["conv1"] : at["conv1"] + 9 * width, :].astype(F32).reshape(9, width, LANES)
    g2[...] = whole[at["conv2"] : at["conv2"] + 9 * width, :].astype(F32).reshape(9, width, LANES)
    gt[...] = emb[...] * whole[at["time"] : at["time"] + 16, :].astype(F32)[0:1]
    for half_index in range(hidden // LANES):
        lanes = slice(half_index * LANES, (half_index + 1) * LANES)
        for start, ref, size in ((at["w1"], gw1, width), (at["w2"], gw2, hidden)):
            begin = start + half_index * size
            ref[:, lanes] = whole[begin : begin + size, :].astype(F32)
        begin = at["w3"] + half_index * CLASS_ROWS
        block = whole[begin : begin + CLASS_ROWS, :].astype(F32)
        block = jnp.concatenate([block, jnp.zeros((LANES - CLASS_ROWS, LANES), F32)], axis=0).T
        gw3[lanes, :] = block[:, 0:classes]


def local(
    xy_noisy,
    xz_plane,
    yz_plane,
    labels,
    timestep,
    conv1_weight,
    conv2_weight,
    time_weight,
    w1,
    w2,
    w3,
):
    grid = Grid()
    nrows, ncols, width = xy_noisy.shape
    depth = labels.shape[2]
    hidden, classes = w3.shape
    count = grid.count
    side = grid.iy % count
    emb = time_embedding(timestep, width)
    temb = jnp.dot(emb, time_weight.astype(F32), precision=lax.Precision.HIGHEST)
    flat_one = conv1_weight.reshape(9 * width, width)
    flat_two = conv2_weight.reshape(9 * width, width)
    back_flat = jnp.transpose(conv2_weight[::-1, ::-1], (0, 1, 3, 2)).reshape(9 * width, width)
    w3_wide = jnp.pad(w3, ((0, 0), (0, LANES - classes)))

    up = lambda i, j: (i + 1, j)
    down = lambda i, j: (i - 1, j)
    left = lambda i, j: (i, j - 1)
    right = lambda i, j: (i, j + 1)

    def lab(part):
        return jnp.pad(part.astype(BF16), ((0, 0), (0, 0), (0, LANES - depth)))

    above = grid.move(jnp.concatenate([xy_noisy[nrows - REACH :], lab(labels[nrows - 1 :])]), up)
    below = grid.move(jnp.concatenate([xy_noisy[:REACH], lab(labels[:1])]), down)

    slab_count = xz_plane.shape[1] // depth
    start = timestep[0] % slab_count * depth
    xz_local = jnp.transpose(lax.dynamic_slice_in_dim(xz_plane, start, depth, 1), (1, 0, 2))
    yz_local = jnp.transpose(lax.dynamic_slice_in_dim(yz_plane, start, depth, 1), (1, 0, 2))
    share = xz_local.shape[1]
    yz_half = lax.dynamic_slice_in_dim(yz_local, side * ncols, ncols, 1)
    first = grid.move(jnp.concatenate([yz_half, xz_local], axis=1), grid.turned(0))
    xz_second = grid.move(xz_local, grid.turned(1))
    yz_cols, xz_same = first[:, :ncols], first[:, ncols:]
    edge = jnp.where(side == 0, xz_local[:, :1], xz_local[:, share - 1 :])
    rim_a = grid.move(
        edge,
        lambda i, j: (j // count - 1, count * i + 1) if j % count == 0 else (j // count + 1, count * i),
    )
    rim_b = grid.move(
        edge,
        lambda i, j: (j // count - 1, count * i) if j % count == 0 else (j // count + 1, count * i + 1),
    )
    xz_above = jnp.where(side == 0, rim_a, rim_b)
    xz_below = jnp.where(side == 0, rim_b, rim_a)

    def column(at, where):
        cols = jnp.concatenate(
            [above[:REACH, where], xy_noisy[:, where], below[:REACH, where]], axis=0
        )
        yz = yz_cols[:, at : at + 1]
        extra = jnp.concatenate(
            [yz[:2], above[3:, at : at + 1], lab(labels[:, at : at + 1]), below[3:, at : at + 1], yz[2:]],
            axis=0,
        )
        return jnp.concatenate([cols, extra], axis=1)

    before = grid.move(column(ncols - 1, slice(ncols - REACH, ncols)), right)
    after = grid.move(column(0, slice(0, REACH)), left)

    flags = jnp.stack(
        [side, grid.ix, grid.nx - 1 - grid.ix, grid.iy, grid.ny - 1 - grid.iy]
    ).astype(jnp.int32)
    chips = grid.nx * grid.ny // 2
    _, rows = gradient_rows(width, hidden)
    each = -(-rows // (2 * chips * 8)) * 8
    vmem = pl.BlockSpec(memory_space=pltpu.VMEM)
    smem = pl.BlockSpec(memory_space=pltpu.SMEM)
    packed, dxz, dyz = pl.pallas_call(
        functools.partial(main_kernel, classes),
        out_shape=(
            jax.ShapeDtypeStruct((2 * chips * each, LANES), BF16),
            jax.ShapeDtypeStruct((depth, nrows, width), BF16),
            jax.ShapeDtypeStruct((depth, ncols, width), BF16),
        ),
        in_specs=[smem] + [vmem] * 18,
        out_specs=(vmem, vmem, vmem),
        scratch_shapes=[
            pltpu.VMEM((nrows + 6, 32, width), F32),
            pltpu.VMEM((nrows + 4, PITCH, width), F32),
            pltpu.VMEM((nrows + 4, 32, width), F32),
            pltpu.VMEM((nrows + 2, PITCH, width), F32),
            pltpu.VMEM((nrows + 2, PITCH, width), F32),
            pltpu.VMEM(((nrows + 4) * PITCH, 9 * width), BF16),
            pltpu.VMEM((depth, nrows, width), F32),
            pltpu.VMEM((width, hidden), F32),
            pltpu.VMEM((hidden, hidden), F32),
            pltpu.VMEM((LANES, hidden), F32),
            pltpu.VMEM((depth, ncols, width), F32),
        ],
        compiler_params=pltpu.CompilerParams(vmem_limit_bytes=VMEM_LIMIT),
        name="tile",
    )(
        flags,
        xy_noisy,
        above,
        below,
        before,
        after,
        labels,
        xz_same,
        xz_second,
        xz_above,
        xz_below,
        yz_cols,
        temb.reshape(1, width),
        flat_one,
        flat_two,
        back_flat,
        w1,
        w2,
        w3_wide,
    )

    def both(own, got):
        return (own.astype(F32) + got.astype(F32)).astype(BF16)

    low, high = dxz[:, :share], dxz[:, share:]
    keep = jnp.where(side == 0, low, high)
    give = jnp.where(side == 0, high, low)
    xz_sum = both(keep, grid.move(give, lambda i, j: (i, j ^ 1)))
    bit = 2
    while bit < grid.ny:
        xz_sum = both(xz_sum, grid.move(xz_sum, lambda i, j, bit=bit: (i, j ^ bit)))
        bit *= 2
    grad_xz = jnp.transpose(grid.move(xz_sum, grid.turned(0)), (1, 0, 2)).astype(F32)
    yz_sum = dyz
    bit = 1
    while bit < grid.nx:
        yz_sum = both(yz_sum, grid.move(yz_sum, lambda i, j, bit=bit: (i ^ bit, j)))
        bit *= 2
    yz_same = grid.move(yz_sum, grid.turned(0))
    yz_other = grid.move(yz_sum, grid.turned(1))
    grad_yz = jnp.where(
        side == 0,
        jnp.concatenate([yz_same, yz_other], axis=1),
        jnp.concatenate([yz_other, yz_same], axis=1),
    )
    grad_yz = jnp.transpose(grad_yz, (1, 0, 2)).astype(F32)

    core = grid.ix % 2
    packed = packed.reshape(2, chips, each, LANES)
    own = lax.dynamic_index_in_dim(packed, core, 0, keepdims=False)
    other = lax.dynamic_index_in_dim(packed, 1 - core, 0, keepdims=False)
    own = both(own, grid.move(other, lambda i, j: (i ^ 1, j)))
    groups = [
        [i * grid.ny + j for i in range(c, grid.nx, 2) for j in range(grid.ny)] for c in range(2)
    ]
    pieces = lax.all_to_all(own, BOTH, 0, 0, axis_index_groups=groups)
    total = jnp.sum(pieces.astype(F32), axis=0).astype(BF16)
    spread = jnp.broadcast_to(total[None], (chips, each, LANES))
    half = lax.all_to_all(spread, BOTH, 0, 0, axis_index_groups=groups)
    partner = grid.move(half, lambda i, j: (i ^ 1, j))
    g1, g2, gt, gw1, gw2, gw3 = pl.pallas_call(
        functools.partial(last_kernel, hidden, classes),
        out_shape=(
            jax.ShapeDtypeStruct((9, width, width), F32),
            jax.ShapeDtypeStruct((9, width, width), F32),
            jax.ShapeDtypeStruct((width, width), F32),
            jax.ShapeDtypeStruct((width, hidden), F32),
            jax.ShapeDtypeStruct((hidden, hidden), F32),
            jax.ShapeDtypeStruct((hidden, classes), F32),
        ),
        in_specs=[smem, vmem, vmem, vmem],
        out_specs=(vmem,) * 6,
        scratch_shapes=[pltpu.VMEM((2 * chips * each, LANES), BF16)],
        compiler_params=pltpu.CompilerParams(vmem_limit_bytes=VMEM_LIMIT),
        name="spread",
    )(
        core.reshape(1).astype(jnp.int32),
        half.reshape(chips * each, LANES),
        partner.reshape(chips * each, LANES),
        emb.reshape(width, 1),
    )
    shape = (3, 3, width, width)
    return (g1.reshape(shape), g2.reshape(shape), gt, gw1, gw2, gw3, grad_xz, grad_yz)


def solution(mesh):
    placed = (
        P("gx", "gy", None),
        P("gy", None, None),
        P("gx", None, None),
        P("gx", "gy", None),
        P(),
        P(),
        P(),
        P(),
        P(),
        P(),
        P(),
    )
    return jax.shard_map(
        local,
        mesh=mesh,
        in_specs=placed,
        out_specs=(P(), P(), P(), P(), P(), P(), P("gy", None, None), P("gx", None, None)),
        check_vma=False,
    )
```

```python
import functools
import math

import jax
import jax.numpy as jnp
from jax import lax
from jax.experimental import pallas as pl
from jax.experimental.pallas import tpu as pltpu
from jax.sharding import PartitionSpec as P

loss_weight = 1.0 / 256.0
BOTH = ("gx", "gy")
LANES = 128
PITCH = 24
REACH = 3
CLASS_ROWS = 32
F32, BF16 = jnp.float32, jnp.bfloat16
VMEM_LIMIT = 48 * 1024 * 1024


def sigmoid(value):
    return 0.5 * jnp.tanh(0.5 * value) + 0.5


def silu_pair(value):
    sig = sigmoid(value)
    out = value * sig
    return out, sig + out - out * sig


def dot(a, b):
    return jnp.dot(a, b, preferred_element_type=F32)


def dot_nt(a, b):
    return lax.dot_general(a, b, (((1,), (1,)), ((), ())), preferred_element_type=F32)


def dot_tn(a, b):
    return lax.dot_general(a, b, (((0,), (0,)), ((), ())), preferred_element_type=F32)


def time_embedding(timestep, width):
    half = width // 2
    freqs = jnp.exp(-math.log(10000.0) * jnp.arange(half, dtype=jnp.float32) / half)
    angle = timestep.astype(jnp.float32)[0] * freqs
    return jnp.concatenate([jnp.cos(angle), jnp.sin(angle)])


class Grid:
    def __init__(self):
        self.nx, self.ny = lax.axis_size("gx"), lax.axis_size("gy")
        self.count = self.ny // self.nx
        self.ix, self.iy = lax.axis_index("gx"), lax.axis_index("gy")

    def move(self, array, target):
        pairs = []
        for i in range(self.nx):
            for j in range(self.ny):
                k, m = target(i, j)
                if 0 <= k < self.nx and 0 <= m < self.ny:
                    pairs.append((i * self.ny + j, k * self.ny + m))
        return lax.ppermute(array, BOTH, pairs)

    def turned(self, shift):
        count = self.count
        return lambda i, j: (j // count, count * i + (j % count + shift) % count)


class Shares:
    def __init__(self, chips, nrows, ncols, depth, width, hidden):
        sizes = (("conv1", 9 * width), ("conv2", 9 * width), ("w1", width * hidden // LANES), ("w2", hidden * hidden // LANES))
        self.at, total = {}, 0
        for name, rows in sizes:
            self.at[name] = total
            total += rows
        self.chips = chips
        self.each = -(-total // (2 * chips * 8)) * 8
        self.xz_rows = nrows * depth // chips
        self.yz_rows = max(1, ncols * depth // 2 // chips)
        self.yz_shares = ncols * depth // 2 // self.yz_rows
        self.xz = self.each
        self.small = self.xz + -(-self.xz_rows // 8) * 8
        self.yz = self.small + 2
        self.rows = -(-(self.yz + 4 * self.yz_rows) // 16) * 16

    def split(self, start, rows):
        done = 0
        while done < rows:
            share, row = divmod(start + done, self.each)
            step = min(rows - done, self.each - row)
            yield share // self.chips, share % self.chips, row, done, step
            done += step


def main_kernel(
    classes,
    shares,
    place,
    xy,
    above,
    below,
    before,
    after,
    labels,
    first,
    rim_row,
    temb,
    conv1,
    conv2,
    back,
    w1,
    w2,
    w3,
    own_out,
    other_out,
    xs,
    hs,
    acts,
    xyds,
    dx,
    patch,
    xzs,
    yzs,
    dw1,
    dw2,
    dw3,
    dxz,
    dyz,
    flat,
    packed,
):
    nrows, ncols, width = xy.shape
    depth = labels.shape[2]
    hidden = w1.shape[1]
    share = nrows // 2
    side, core = place[0], place[5]
    open_up, open_down, open_left, open_right = (place[1] > 0, place[2] > 0, place[3] > 0, place[4] > 0)
    tall = nrows + 2 * REACH

    mid_r, mid_c = slice(REACH, REACH + nrows), slice(REACH, REACH + ncols)
    xs[...] = jnp.zeros_like(xs)
    xs[mid_r, mid_c] = xy[...].astype(F32)
    xs[0:REACH, mid_c] = above[0:REACH].astype(F32)
    xs[REACH + nrows : 2 * REACH + nrows, mid_c] = below[0:REACH].astype(F32)
    xs[:, 0:REACH] = before[0:tall].astype(F32)[:, 0:REACH]
    xs[:, REACH + ncols : 2 * REACH + ncols] = after[0:tall].astype(F32)[:, 0:REACH]

    def gather(source, row, col, rows, cols):
        count = rows * cols
        for a in range(3):
            for b in range(3):
                piece = source[row + a : row + a + rows, col + b : col + b + cols, :]
                tap = (3 * a + b) * width
                patch[0:count, tap : tap + width] = piece.reshape(count, width).astype(BF16)
        return count

    n1 = gather(xs, 0, 0, nrows + 4, PITCH)
    h1 = dot(patch[0:n1], conv1[...]) + temb[...]
    h1 = h1.reshape(nrows + 4, PITCH, width)
    hs[...] = h1
    row = lax.broadcasted_iota(jnp.int32, h1.shape, 0)
    col = lax.broadcasted_iota(jnp.int32, h1.shape, 1)
    low_r = jnp.where(open_up, 0, 2)
    high_r = jnp.where(open_down, nrows + 4, nrows + 2)
    low_c = jnp.where(open_left, 0, 2)
    high_c = jnp.where(open_right, ncols + 4, ncols + 2)
    inside = (row >= low_r) & (row < high_r) & (col >= low_c) & (col < high_c)
    a1 = jnp.where(inside, h1 * sigmoid(h1), 0.0)
    acts[...] = jnp.zeros_like(acts)
    acts[:, 0:PITCH] = a1.astype(BF16).astype(F32)
    n2 = gather(acts, 0, 0, nrows + 2, PITCH)
    xyd = dot(patch[0:n2], conv2[...])
    xyds[...] = xyd.astype(BF16).astype(F32).reshape(nrows + 2, PITCH, width)

    rows_before = before[tall : tall + share + 1].astype(F32)
    rows_after = after[tall : tall + share + 1].astype(F32)
    mine = first[...].astype(F32)
    rim_mine = rim_row[...].astype(F32)
    same_at = pl.ds(pl.multiple_of(side * share, share), share)
    second_at = pl.ds(pl.multiple_of((1 - side) * share, share), share)
    xz_above, xz_below = [], []
    for k in range(depth):
        second = jnp.where(side == 0, rows_after[:, k, :], rows_before[:, k, :])
        yzs[k] = mine[0:ncols, k, :]
        xzs[k, same_at, :] = mine[ncols:, k, :]
        xzs[k, second_at, :] = second[0:share]
        rim_same, rim_second = rim_mine[:, k, :], second[share:]
        xz_above.append(jnp.where(side == 0, rim_same, rim_second))
        xz_below.append(jnp.where(side == 0, rim_second, rim_same))

    def decode(feat, label):
        u1 = dot(feat, w1[...])
        g1, s1 = silu_pair(u1)
        g1 = g1.astype(BF16)
        u2 = dot(g1, w2[...])
        g2, s2 = silu_pair(u2)
        g2 = g2.astype(BF16)
        logits = dot(g2, w3[...])
        lane = lax.broadcasted_iota(jnp.int32, logits.shape, 1)
        logits = jnp.where(lane < classes, logits, -jnp.inf)
        power = jnp.exp(logits - jnp.max(logits, axis=1, keepdims=True))
        prob = power / jnp.sum(power, axis=1, keepdims=True)
        onehot = jnp.where(lane == label, 1.0, 0.0)
        dlogits = (loss_weight * (prob - onehot)).astype(BF16)
        du2 = (dot_nt(dlogits, w3[...]) * s2).astype(BF16)
        du1 = (dot_nt(du2, w2[...]) * s1).astype(BF16)
        return g1, g2, dlogits, du2, du1, dot_nt(du1, w1[...])

    dw1[...] = jnp.zeros_like(dw1)
    dw2[...] = jnp.zeros_like(dw2)
    dw3[...] = jnp.zeros_like(dw3)
    dyz[...] = jnp.zeros_like(dyz)
    dx[...] = jnp.zeros_like(dx)
    chunk = 16
    size = chunk * ncols

    def step(index, carry):
        r0 = pl.multiple_of(index * chunk, chunk)
        tile = xyds[pl.ds(r0 + 1, chunk), 1 : ncols + 1, :]
        lab = labels[pl.ds(r0, chunk)].reshape(size, depth)
        feats, labs = [], []
        for k in range(depth):
            xz_k = xzs[k, pl.ds(r0, chunk), :]
            feat = tile + xz_k[:, None, :] + yzs[k][None]
            feats.append(feat.reshape(size, width).astype(BF16))
            labs.append(jnp.broadcast_to(lab[:, k : k + 1], (size, LANES)))
        feat = jnp.concatenate(feats, axis=0)
        g1, g2, dlogits, du2, du1, dfeat = decode(feat, jnp.concatenate(labs, axis=0))
        dw3[...] += dot_tn(dlogits, g2)
        dw2[...] += dot_tn(g1, du2)
        dw1[...] += dot_tn(feat, du1)
        total = jnp.zeros((chunk, ncols, width), F32)
        for k in range(depth):
            piece = dfeat[k * size : (k + 1) * size].reshape(chunk, ncols, width)
            total = total + piece
            dxz[k, pl.ds(r0, chunk), :] = jnp.sum(piece, axis=1)
            dyz[k] += jnp.sum(piece, axis=0)
        dx[pl.ds(r0 + 1, chunk), 1 : ncols + 1, :] = total.astype(BF16).astype(F32)
        return carry

    lax.fori_loop(0, nrows // chunk, step, 0)

    lab_before = before[2 : nrows + 4, 3, :].astype(F32).astype(jnp.int32)
    lab_after = after[2 : nrows + 4, 3, :].astype(F32).astype(jnp.int32)
    lab_up = above[3].astype(F32).astype(jnp.int32)
    lab_down = below[3].astype(F32).astype(jnp.int32)
    tail = jnp.zeros((PITCH - ncols - 2, LANES), jnp.int32)
    lab_rim = jnp.concatenate(
        [
            lab_before[0:1],
            lab_up,
            lab_after[0:1],
            tail,
            lab_before[nrows + 1 : nrows + 2],
            lab_down,
            lab_after[nrows + 1 : nrows + 2],
            tail,
            lab_before[1 : nrows + 1],
            lab_after[1 : nrows + 1],
        ],
        axis=0,
    )
    rim_at = (0, 1, nrows + 2 * REACH - 2, nrows + 2 * REACH - 1)
    feats, labs = [], []
    zero_tail = jnp.zeros((PITCH - ncols - 2, width), F32)
    for k in range(depth):
        yz_before = before[rim_at[k], 3:4, :].astype(F32)
        yz_after = after[rim_at[k], 3:4, :].astype(F32)
        yz_row = jnp.concatenate([yz_before, yzs[k], yz_after, zero_tail], axis=0)
        feats.append(xyds[0] + xz_above[k] + yz_row)
        feats.append(xyds[nrows + 1] + xz_below[k] + yz_row)
        feats.append(xyds[1 : nrows + 1, 0, :] + xzs[k] + yz_before)
        feats.append(xyds[1 : nrows + 1, ncols + 1, :] + xzs[k] + yz_after)
        labs.append(jnp.broadcast_to(lab_rim[:, k : k + 1], (2 * PITCH + 2 * nrows, LANES)))
    rim = decode(jnp.concatenate(feats, axis=0).astype(BF16), jnp.concatenate(labs, axis=0))[-1]
    span = 2 * PITCH + 2 * nrows
    rim_sum = rim[0:span]
    for k in range(1, depth):
        rim_sum = rim_sum + rim[k * span : (k + 1) * span]
    rim_sum = rim_sum.astype(BF16).astype(F32)
    rcol = lax.broadcasted_iota(jnp.int32, (PITCH, width), 0)
    keep = (rcol >= jnp.where(open_left, 0, 1)) & (rcol < jnp.where(open_right, ncols + 2, ncols + 1))
    dx[0] = jnp.where(keep & open_up, rim_sum[0:PITCH], 0.0)
    dx[nrows + 1] = jnp.where(keep & open_down, rim_sum[PITCH : 2 * PITCH], 0.0)
    west = rim_sum[2 * PITCH : 2 * PITCH + nrows]
    east = rim_sum[2 * PITCH + nrows : span]
    dx[1 : nrows + 1, 0, :] = jnp.where(open_left, west, 0.0)
    dx[1 : nrows + 1, ncols + 1, :] = jnp.where(open_right, east, 0.0)

    def put(start, block):
        for half, index, row, offset, rows in shares.split(start, block.shape[0]):
            packed[half, index, row : row + rows, :] = block[offset : offset + rows]

    def weight_gradient(start, dout):
        grad = dot_tn(dout, patch[0 : nrows * ncols])
        for tap in range(9):
            put(start + tap * width, grad[:, tap * width : (tap + 1) * width].T)

    packed[...] = jnp.zeros_like(packed)

    n3 = gather(acts, 1, 1, nrows, ncols)
    dxyd = dx[1 : nrows + 1, 1 : ncols + 1, :].reshape(n3, width).astype(BF16)
    weight_gradient(shares.at["conv2"], dxyd)
    gather(dx, 0, 0, nrows, ncols)
    da1 = dot(patch[0:n3], back[...])
    _, slope = silu_pair(hs[2 : nrows + 2, 2 : ncols + 2, :].reshape(n3, width))
    dh1 = (da1 * slope).astype(BF16)
    gather(xs, 2, 2, nrows, ncols)
    weight_gradient(shares.at["conv1"], dh1)

    for name, ref in (("w1", dw1), ("w2", dw2)):
        rows = ref.shape[0]
        for half in range(hidden // LANES):
            put(shares.at[name] + half * rows, ref[:, half * LANES : (half + 1) * LANES])
    for q in range(classes):
        where = packed.at[q // shares.chips, q % shares.chips]
        for half in range(hidden // LANES):
            row = shares.small + half
            where[row : row + 1, :] = dw3[q : q + 1, half * LANES : (half + 1) * LANES]
    time_row = jnp.sum(dh1.astype(F32), axis=0, keepdims=True)
    packed[classes // shares.chips, classes % shares.chips, shares.small : shares.small + 1, :] = time_row
    for k in range(depth):
        flat[pl.ds(k, ncols, stride=depth), :] = dyz[k]
    for half in range(2):
        for index in range(shares.yz_shares):
            begin = half * ncols * depth // 2 + index * shares.yz_rows
            packed[half, index, shares.yz : shares.yz + shares.yz_rows, :] = flat[begin : begin + shares.yz_rows]
    for k in range(depth):
        flat[pl.ds(k, nrows, stride=depth), :] = dxz[k]
    for index in range(shares.chips):
        begin = index * shares.xz_rows
        packed[core, index, shares.xz : shares.xz + shares.xz_rows, :] = flat[begin : begin + shares.xz_rows]
    own_out[...] = packed[core].astype(BF16)
    other_out[...] = packed[1 - core].astype(BF16)


def sum_kernel(shares, ny, pieces, out):
    chips = pieces.shape[0]
    nx = chips // ny
    cut, at_yz, yz_rows = shares.xz, shares.yz, shares.yz_rows
    total = pieces[0].astype(F32)
    for index in range(1, chips):
        total = total + pieces[index].astype(F32)
    common = total.astype(BF16)
    by_row, by_col = [], []
    for i in range(nx):
        part = pieces[i * ny, cut : shares.small].astype(F32)
        for j in range(1, ny):
            part = part + pieces[i * ny + j, cut : shares.small].astype(F32)
        by_row.append(part.astype(BF16))
    for j in range(ny):
        part = pieces[j, shares.small :].astype(F32)
        for i in range(1, nx):
            part = part + pieces[i * ny + j, shares.small :].astype(F32)
        by_col.append(part[at_yz - shares.small : at_yz - shares.small + yz_rows])
    pad = shares.rows - at_yz - 4 * yz_rows
    for i in range(nx):
        tail = [total[shares.small : at_yz]] + by_col[4 * i : 4 * i + 4]
        if pad:
            tail.append(jnp.zeros((pad, LANES), F32))
        tail = jnp.concatenate(tail, axis=0).astype(BF16)
        for j in range(ny):
            out[i * ny + j, 0:cut, :] = common[0:cut]
            out[i * ny + j, cut : shares.small, :] = by_row[j // 4]
            out[i * ny + j, shares.small :, :] = tail


def last_kernel(shares, classes, place, half, partner, emb, g1, g2, gt, gw1, gw2, gw3, gxz, gyz, whole, w3_rows):
    width, hidden = emb.shape[0], gw2.shape[0]
    core, row_core, row_side = place[0], place[1], place[2]
    whole[pl.ds(core, 1)] = half[...].astype(F32)[None]
    whole[pl.ds(1 - core, 1)] = partner[...].astype(F32)[None]

    def take(start, ref, lead, lanes):
        for side, index, row, offset, rows in shares.split(start, width if lead is not None else ref.shape[0]):
            block = whole[side, index, row : row + rows, :]
            if lead is not None:
                ref[lead, offset : offset + rows, :] = block
            else:
                ref[offset : offset + rows, lanes] = block

    for name, ref in (("conv1", g1), ("conv2", g2)):
        for tap in range(9):
            take(shares.at[name] + tap * width, ref, tap, None)
    for name, ref in (("w1", gw1), ("w2", gw2)):
        for part in range(hidden // LANES):
            take(shares.at[name] + part * ref.shape[0], ref, None, slice(part * LANES, (part + 1) * LANES))
    small = slice(shares.small, shares.small + 1)
    gt[...] = emb[...] * whole[classes // shares.chips, classes % shares.chips, small, :]
    for part in range(hidden // LANES):
        small = slice(shares.small + part, shares.small + part + 1)
        w3_rows[...] = jnp.zeros_like(w3_rows)
        for q in range(classes):
            w3_rows[q : q + 1, :] = whole[q // shares.chips, q % shares.chips, small, :]
        gw3[part * LANES : (part + 1) * LANES, :] = w3_rows[...].T[:, 0:classes]
    count = gxz.shape[0]
    begin = pl.multiple_of(row_side * count, count)
    gxz[...] = whole[row_core, pl.ds(begin, count), shares.xz : shares.xz + shares.xz_rows, :]
    size, per = shares.yz_rows, shares.yz_rows * shares.yz_shares
    for r in range(2):
        for side in range(2):
            for index in range(shares.yz_shares):
                even = whole[side, index, shares.yz + r * size : shares.yz + (r + 1) * size, :]
                odd = whole[side, index, shares.yz + (2 + r) * size : shares.yz + (3 + r) * size, :]
                to = (2 * r + side) * per + index * size
                gyz[to : to + size, :] = jnp.where(core == 0, even, odd)


def local(
    xy_noisy,
    xz_plane,
    yz_plane,
    labels,
    timestep,
    conv1_weight,
    conv2_weight,
    time_weight,
    w1,
    w2,
    w3,
):
    grid = Grid()
    nrows, ncols, width = xy_noisy.shape
    depth = labels.shape[2]
    hidden, classes = w3.shape
    count = grid.count
    side = grid.iy % count
    emb = time_embedding(timestep, width)
    temb = jnp.dot(emb, time_weight.astype(F32), precision=lax.Precision.HIGHEST)
    flat_one = conv1_weight.reshape(9 * width, width)
    flat_two = conv2_weight.reshape(9 * width, width)
    back_flat = jnp.transpose(conv2_weight[::-1, ::-1], (0, 1, 3, 2)).reshape(9 * width, width)
    w3_wide = jnp.pad(w3, ((0, 0), (0, LANES - classes)))

    up = lambda i, j: (i + 1, j)
    down = lambda i, j: (i - 1, j)
    left = lambda i, j: (i, j - 1)
    right = lambda i, j: (i, j + 1)

    def lab(part):
        return jnp.pad(part.astype(BF16), ((0, 0), (0, 0), (0, LANES - depth)))

    above = grid.move(jnp.concatenate([xy_noisy[nrows - REACH :], lab(labels[nrows - 1 :])]), up)
    below = grid.move(jnp.concatenate([xy_noisy[:REACH], lab(labels[:1])]), down)

    slab_count = xz_plane.shape[1] // depth
    start = timestep[0] % slab_count * depth
    xz_local = lax.dynamic_slice_in_dim(xz_plane, start, depth, 1)
    share = xz_local.shape[0]
    yz_half = lax.dynamic_slice(yz_plane, (side * ncols, start, 0), (ncols, depth, width))
    first = grid.move(jnp.concatenate([yz_half, xz_local], axis=0), grid.turned(0))
    rim_row = grid.move(
        jnp.where(side == 0, xz_local[:1], xz_local[share - 1 :]),
        lambda i, j: (j // count - 1, count * i + 1) if j % count == 0 else (j // count + 1, count * i),
    )

    def column(at, where):
        cols = jnp.concatenate(
            [above[:REACH, where], xy_noisy[:, where], below[:REACH, where]], axis=0
        )
        yz = first[at].reshape(depth, 1, width)
        extra = jnp.concatenate(
            [yz[:2], above[3:, at : at + 1], lab(labels[:, at : at + 1]), below[3:, at : at + 1], yz[2:]],
            axis=0,
        )
        return jnp.concatenate([jnp.concatenate([cols, extra], axis=1), first[ncols:], rim_row], axis=0)

    before = grid.move(column(ncols - 1, slice(ncols - REACH, ncols)), right)
    after = grid.move(column(0, slice(0, REACH)), left)

    core = grid.ix % 2
    flags = jnp.stack(
        [side, grid.ix, grid.nx - 1 - grid.ix, grid.iy, grid.ny - 1 - grid.iy, core]
    ).astype(jnp.int32)
    chips = grid.nx * grid.ny // 2
    shares = Shares(chips, nrows, ncols, depth, width, hidden)
    vmem = pl.BlockSpec(memory_space=pltpu.VMEM)
    smem = pl.BlockSpec(memory_space=pltpu.SMEM)
    params = pltpu.CompilerParams(vmem_limit_bytes=VMEM_LIMIT)
    buffer = jax.ShapeDtypeStruct((chips, shares.rows, LANES), BF16)
    own, other = pl.pallas_call(
        functools.partial(main_kernel, classes, shares),
        out_shape=(buffer, buffer),
        in_specs=[smem] + [vmem] * 15,
        out_specs=(vmem, vmem),
        scratch_shapes=[
            pltpu.VMEM((nrows + 6, 32, width), F32),
            pltpu.VMEM((nrows + 4, PITCH, width), F32),
            pltpu.VMEM((nrows + 4, 32, width), F32),
            pltpu.VMEM((nrows + 2, PITCH, width), F32),
            pltpu.VMEM((nrows + 2, PITCH, width), F32),
            pltpu.VMEM(((nrows + 4) * PITCH, 9 * width), BF16),
            pltpu.VMEM((depth, nrows, width), F32),
            pltpu.VMEM((depth, ncols, width), F32),
            pltpu.VMEM((width, hidden), F32),
            pltpu.VMEM((hidden, hidden), F32),
            pltpu.VMEM((LANES, hidden), F32),
            pltpu.VMEM((depth, nrows, width), F32),
            pltpu.VMEM((depth, ncols, width), F32),
            pltpu.VMEM((nrows * depth, width), F32),
            pltpu.VMEM((2, chips, shares.rows, LANES), F32),
        ],
        compiler_params=params,
        name="tile",
    )(
        flags,
        xy_noisy,
        above,
        below,
        before,
        after,
        labels,
        first,
        rim_row,
        temb.reshape(1, width),
        flat_one,
        flat_two,
        back_flat,
        w1,
        w2,
        w3_wide,
    )

    swap = lambda i, j: (i ^ 1, j)
    own = (own.astype(F32) + grid.move(other, swap).astype(F32)).astype(BF16)
    groups = [
        [i * grid.ny + j for i in range(c, grid.nx, 2) for j in range(grid.ny)] for c in range(2)
    ]
    pieces = lax.all_to_all(own, BOTH, 0, 0, axis_index_groups=groups)
    sums = pl.pallas_call(
        functools.partial(sum_kernel, shares, grid.ny),
        out_shape=buffer,
        in_specs=[vmem],
        out_specs=vmem,
        compiler_params=params,
        name="sums",
    )(pieces)
    half = lax.all_to_all(sums, BOTH, 0, 0, axis_index_groups=groups)
    partner = grid.move(half, swap)
    row_of = grid.iy // count
    g1, g2, gt, gw1, gw2, gw3, gxz, gyz = pl.pallas_call(
        functools.partial(last_kernel, shares, classes),
        out_shape=(
            jax.ShapeDtypeStruct((9, width, width), F32),
            jax.ShapeDtypeStruct((9, width, width), F32),
            jax.ShapeDtypeStruct((width, width), F32),
            jax.ShapeDtypeStruct((width, hidden), F32),
            jax.ShapeDtypeStruct((hidden, hidden), F32),
            jax.ShapeDtypeStruct((hidden, classes), F32),
            jax.ShapeDtypeStruct((chips // 2, shares.xz_rows, width), F32),
            jax.ShapeDtypeStruct((2 * ncols * depth, width), F32),
        ),
        in_specs=[smem, vmem, vmem, vmem],
        out_specs=(vmem,) * 8,
        scratch_shapes=[
            pltpu.VMEM((2, chips, shares.rows, LANES), F32),
            pltpu.VMEM((LANES, LANES), F32),
        ],
        compiler_params=params,
        name="spread",
    )(
        jnp.stack([core, row_of % 2, side]).astype(jnp.int32),
        half,
        partner,
        emb.reshape(width, 1),
    )
    shape = (3, 3, width, width)
    return (
        g1.reshape(shape),
        g2.reshape(shape),
        gt,
        gw1,
        gw2,
        gw3,
        gxz.reshape(share, depth, width),
        gyz.reshape(2 * ncols, depth, width),
    )


def solution(mesh):
    placed = (
        P("gx", "gy", None),
        P("gy", None, None),
        P("gx", None, None),
        P("gx", "gy", None),
        P(),
        P(),
        P(),
        P(),
        P(),
        P(),
        P(),
    )
    return jax.shard_map(
        local,
        mesh=mesh,
        in_specs=placed,
        out_specs=(P(), P(), P(), P(), P(), P(), P("gy", None, None), P("gx", None, None)),
        check_vma=False,
    )
```

```python
import functools
import math

import jax
import jax.numpy as jnp
from jax import lax
from jax.experimental import pallas as pl
from jax.experimental.pallas import tpu as pltpu
from jax.sharding import PartitionSpec as P

loss_weight = 1.0 / 256.0
BOTH = ("gx", "gy")
LANES = 128
PITCH = 24
REACH = 3
CLASS_ROWS = 32
F32, BF16 = jnp.float32, jnp.bfloat16
VMEM_LIMIT = 48 * 1024 * 1024


def sigmoid(value):
    return 0.5 * jnp.tanh(0.5 * value) + 0.5


def silu_pair(value):
    sig = sigmoid(value)
    out = value * sig
    return out, sig + out - out * sig


def dot(a, b):
    return jnp.dot(a, b, preferred_element_type=F32)


def dot_nt(a, b):
    return lax.dot_general(a, b, (((1,), (1,)), ((), ())), preferred_element_type=F32)


def dot_tn(a, b):
    return lax.dot_general(a, b, (((0,), (0,)), ((), ())), preferred_element_type=F32)


def time_embedding(timestep, width):
    half = width // 2
    freqs = jnp.exp(-math.log(10000.0) * jnp.arange(half, dtype=jnp.float32) / half)
    angle = timestep.astype(jnp.float32)[0] * freqs
    return jnp.concatenate([jnp.cos(angle), jnp.sin(angle)])


class Grid:
    def __init__(self):
        self.nx, self.ny = lax.axis_size("gx"), lax.axis_size("gy")
        self.count = self.ny // self.nx
        self.ix, self.iy = lax.axis_index("gx"), lax.axis_index("gy")

    def move(self, array, target):
        pairs = []
        for i in range(self.nx):
            for j in range(self.ny):
                k, m = target(i, j)
                if 0 <= k < self.nx and 0 <= m < self.ny:
                    pairs.append((i * self.ny + j, k * self.ny + m))
        return lax.ppermute(array, BOTH, pairs)

    def turned(self, shift):
        count = self.count
        return lambda i, j: (j // count, count * i + (j % count + shift) % count)


class Shares:
    def __init__(self, nx, ny, nrows, ncols, depth, width, hidden):
        sizes = (("conv1", 9 * width), ("conv2", 9 * width), ("w1", width * hidden // LANES), ("w2", hidden * hidden // LANES))
        self.at, total = {}, 0
        for name, rows in sizes:
            self.at[name] = total
            total += rows
        self.chips = chips = nx * ny // 2
        self.ranks, self.planes, self.layers = nx // 2, nx, ny // 2
        self.each = -(-total // (2 * chips * 8)) * 8
        self.xz_rows = nrows * depth // chips
        self.yz_rows = max(1, ncols * depth // 2 // chips)
        self.yz_shares = ncols * depth // 2 // self.yz_rows
        self.xz_slot = -(-self.xz_rows // 8) * 8
        even = lambda rows: -(-rows // 16) * 16
        self.xz = self.each
        self.small = self.xz + self.xz_slot
        self.yz = self.small + 2
        self.rows = even(self.yz + self.yz_rows)
        self.mid_small = self.xz + self.ranks * self.xz_slot
        self.mid_yz = self.mid_small + 2
        self.mid_rows = even(self.mid_yz + 2 * self.yz_rows)
        self.end_rows = even(self.yz + ny * self.yz_rows)

    def split(self, start, rows):
        done = 0
        while done < rows:
            share, row = divmod(start + done, self.each)
            step = min(rows - done, self.each - row)
            yield share // self.chips, share % self.chips, row, done, step
            done += step


def main_kernel(
    classes,
    shares,
    place,
    xy,
    above,
    below,
    before,
    after,
    labels,
    first,
    rim_row,
    temb,
    conv1,
    conv2,
    back,
    w1,
    w2,
    w3,
    own_out,
    other_out,
    xs,
    hs,
    acts,
    xyds,
    dx,
    patch,
    xzs,
    yzs,
    dw1,
    dw2,
    dw3,
    dxz,
    dyz,
    flat,
    packed,
):
    nrows, ncols, width = xy.shape
    depth = labels.shape[2]
    hidden = w1.shape[1]
    share = nrows // 2
    side, core = place[0], place[5]
    open_up, open_down, open_left, open_right = (place[1] > 0, place[2] > 0, place[3] > 0, place[4] > 0)
    tall = nrows + 2 * REACH

    mid_r, mid_c = slice(REACH, REACH + nrows), slice(REACH, REACH + ncols)
    xs[...] = jnp.zeros_like(xs)
    xs[mid_r, mid_c] = xy[...].astype(F32)
    xs[0:REACH, mid_c] = above[0:REACH].astype(F32)
    xs[REACH + nrows : 2 * REACH + nrows, mid_c] = below[0:REACH].astype(F32)
    xs[:, 0:REACH] = before[0:tall].astype(F32)[:, 0:REACH]
    xs[:, REACH + ncols : 2 * REACH + ncols] = after[0:tall].astype(F32)[:, 0:REACH]

    def gather(source, row, col, rows, cols):
        count = rows * cols
        for a in range(3):
            for b in range(3):
                piece = source[row + a : row + a + rows, col + b : col + b + cols, :]
                tap = (3 * a + b) * width
                patch[0:count, tap : tap + width] = piece.reshape(count, width).astype(BF16)
        return count

    n1 = gather(xs, 0, 0, nrows + 4, PITCH)
    h1 = dot(patch[0:n1], conv1[...]) + temb[...]
    h1 = h1.reshape(nrows + 4, PITCH, width)
    hs[...] = h1
    row = lax.broadcasted_iota(jnp.int32, h1.shape, 0)
    col = lax.broadcasted_iota(jnp.int32, h1.shape, 1)
    low_r = jnp.where(open_up, 0, 2)
    high_r = jnp.where(open_down, nrows + 4, nrows + 2)
    low_c = jnp.where(open_left, 0, 2)
    high_c = jnp.where(open_right, ncols + 4, ncols + 2)
    inside = (row >= low_r) & (row < high_r) & (col >= low_c) & (col < high_c)
    a1 = jnp.where(inside, h1 * sigmoid(h1), 0.0)
    acts[...] = jnp.zeros_like(acts)
    acts[:, 0:PITCH] = a1.astype(BF16).astype(F32)
    n2 = gather(acts, 0, 0, nrows + 2, PITCH)
    xyd = dot(patch[0:n2], conv2[...])
    xyds[...] = xyd.astype(BF16).astype(F32).reshape(nrows + 2, PITCH, width)

    rows_before = before[tall : tall + share + 1].astype(F32)
    rows_after = after[tall : tall + share + 1].astype(F32)
    mine = first[...].astype(F32)
    rim_mine = rim_row[...].astype(F32)
    same_at = pl.ds(pl.multiple_of(side * share, share), share)
    second_at = pl.ds(pl.multiple_of((1 - side) * share, share), share)
    xz_above, xz_below = [], []
    for k in range(depth):
        second = jnp.where(side == 0, rows_after[:, k, :], rows_before[:, k, :])
        yzs[k] = mine[0:ncols, k, :]
        xzs[k, same_at, :] = mine[ncols:, k, :]
        xzs[k, second_at, :] = second[0:share]
        rim_same, rim_second = rim_mine[:, k, :], second[share:]
        xz_above.append(jnp.where(side == 0, rim_same, rim_second))
        xz_below.append(jnp.where(side == 0, rim_second, rim_same))

    def decode(feat, label):
        u1 = dot(feat, w1[...])
        g1, s1 = silu_pair(u1)
        g1 = g1.astype(BF16)
        u2 = dot(g1, w2[...])
        g2, s2 = silu_pair(u2)
        g2 = g2.astype(BF16)
        logits = dot(g2, w3[...])
        lane = lax.broadcasted_iota(jnp.int32, logits.shape, 1)
        logits = jnp.where(lane < classes, logits, -jnp.inf)
        power = jnp.exp(logits - jnp.max(logits, axis=1, keepdims=True))
        prob = power / jnp.sum(power, axis=1, keepdims=True)
        onehot = jnp.where(lane == label, 1.0, 0.0)
        dlogits = (loss_weight * (prob - onehot)).astype(BF16)
        du2 = (dot_nt(dlogits, w3[...]) * s2).astype(BF16)
        du1 = (dot_nt(du2, w2[...]) * s1).astype(BF16)
        return g1, g2, dlogits, du2, du1, dot_nt(du1, w1[...])

    dw1[...] = jnp.zeros_like(dw1)
    dw2[...] = jnp.zeros_like(dw2)
    dw3[...] = jnp.zeros_like(dw3)
    dyz[...] = jnp.zeros_like(dyz)
    dx[...] = jnp.zeros_like(dx)
    chunk = 16
    size = chunk * ncols

    def step(index, carry):
        r0 = pl.multiple_of(index * chunk, chunk)
        tile = xyds[pl.ds(r0 + 1, chunk), 1 : ncols + 1, :]
        lab = labels[pl.ds(r0, chunk)].reshape(size, depth)
        feats, labs = [], []
        for k in range(depth):
            xz_k = xzs[k, pl.ds(r0, chunk), :]
            feat = tile + xz_k[:, None, :] + yzs[k][None]
            feats.append(feat.reshape(size, width).astype(BF16))
            labs.append(jnp.broadcast_to(lab[:, k : k + 1], (size, LANES)))
        feat = jnp.concatenate(feats, axis=0)
        g1, g2, dlogits, du2, du1, dfeat = decode(feat, jnp.concatenate(labs, axis=0))
        dw3[...] += dot_tn(dlogits, g2)
        dw2[...] += dot_tn(g1, du2)
        dw1[...] += dot_tn(feat, du1)
        total = jnp.zeros((chunk, ncols, width), F32)
        for k in range(depth):
            piece = dfeat[k * size : (k + 1) * size].reshape(chunk, ncols, width)
            total = total + piece
            dxz[k, pl.ds(r0, chunk), :] = jnp.sum(piece, axis=1)
            dyz[k] += jnp.sum(piece, axis=0)
        dx[pl.ds(r0 + 1, chunk), 1 : ncols + 1, :] = total.astype(BF16).astype(F32)
        return carry

    lax.fori_loop(0, nrows // chunk, step, 0)

    lab_before = before[2 : nrows + 4, 3, :].astype(F32).astype(jnp.int32)
    lab_after = after[2 : nrows + 4, 3, :].astype(F32).astype(jnp.int32)
    lab_up = above[3].astype(F32).astype(jnp.int32)
    lab_down = below[3].astype(F32).astype(jnp.int32)
    tail = jnp.zeros((PITCH - ncols - 2, LANES), jnp.int32)
    lab_rim = jnp.concatenate(
        [
            lab_before[0:1],
            lab_up,
            lab_after[0:1],
            tail,
            lab_before[nrows + 1 : nrows + 2],
            lab_down,
            lab_after[nrows + 1 : nrows + 2],
            tail,
            lab_before[1 : nrows + 1],
            lab_after[1 : nrows + 1],
        ],
        axis=0,
    )
    rim_at = (0, 1, nrows + 2 * REACH - 2, nrows + 2 * REACH - 1)
    feats, labs = [], []
    zero_tail = jnp.zeros((PITCH - ncols - 2, width), F32)
    for k in range(depth):
        yz_before = before[rim_at[k], 3:4, :].astype(F32)
        yz_after = after[rim_at[k], 3:4, :].astype(F32)
        yz_row = jnp.concatenate([yz_before, yzs[k], yz_after, zero_tail], axis=0)
        feats.append(xyds[0] + xz_above[k] + yz_row)
        feats.append(xyds[nrows + 1] + xz_below[k] + yz_row)
        feats.append(xyds[1 : nrows + 1, 0, :] + xzs[k] + yz_before)
        feats.append(xyds[1 : nrows + 1, ncols + 1, :] + xzs[k] + yz_after)
        labs.append(jnp.broadcast_to(lab_rim[:, k : k + 1], (2 * PITCH + 2 * nrows, LANES)))
    rim = decode(jnp.concatenate(feats, axis=0).astype(BF16), jnp.concatenate(labs, axis=0))[-1]
    span = 2 * PITCH + 2 * nrows
    rim_sum = rim[0:span]
    for k in range(1, depth):
        rim_sum = rim_sum + rim[k * span : (k + 1) * span]
    rim_sum = rim_sum.astype(BF16).astype(F32)
    rcol = lax.broadcasted_iota(jnp.int32, (PITCH, width), 0)
    keep = (rcol >= jnp.where(open_left, 0, 1)) & (rcol < jnp.where(open_right, ncols + 2, ncols + 1))
    dx[0] = jnp.where(keep & open_up, rim_sum[0:PITCH], 0.0)
    dx[nrows + 1] = jnp.where(keep & open_down, rim_sum[PITCH : 2 * PITCH], 0.0)
    west = rim_sum[2 * PITCH : 2 * PITCH + nrows]
    east = rim_sum[2 * PITCH + nrows : span]
    dx[1 : nrows + 1, 0, :] = jnp.where(open_left, west, 0.0)
    dx[1 : nrows + 1, ncols + 1, :] = jnp.where(open_right, east, 0.0)

    def put(start, block):
        for half, index, row, offset, rows in shares.split(start, block.shape[0]):
            packed[half, index, row : row + rows, :] = block[offset : offset + rows]

    def weight_gradient(start, dout):
        grad = dot_tn(dout, patch[0 : nrows * ncols])
        for tap in range(9):
            put(start + tap * width, grad[:, tap * width : (tap + 1) * width].T)

    packed[...] = jnp.zeros_like(packed)

    n3 = gather(acts, 1, 1, nrows, ncols)
    dxyd = dx[1 : nrows + 1, 1 : ncols + 1, :].reshape(n3, width).astype(BF16)
    weight_gradient(shares.at["conv2"], dxyd)
    gather(dx, 0, 0, nrows, ncols)
    da1 = dot(patch[0:n3], back[...])
    _, slope = silu_pair(hs[2 : nrows + 2, 2 : ncols + 2, :].reshape(n3, width))
    dh1 = (da1 * slope).astype(BF16)
    gather(xs, 2, 2, nrows, ncols)
    weight_gradient(shares.at["conv1"], dh1)

    for name, ref in (("w1", dw1), ("w2", dw2)):
        rows = ref.shape[0]
        for half in range(hidden // LANES):
            put(shares.at[name] + half * rows, ref[:, half * LANES : (half + 1) * LANES])
    for q in range(classes):
        where = packed.at[q // shares.chips, q % shares.chips]
        for half in range(hidden // LANES):
            row = shares.small + half
            where[row : row + 1, :] = dw3[q : q + 1, half * LANES : (half + 1) * LANES]
    time_row = jnp.sum(dh1.astype(F32), axis=0, keepdims=True)
    packed[classes // shares.chips, classes % shares.chips, shares.small : shares.small + 1, :] = time_row
    for k in range(depth):
        flat[pl.ds(k, ncols, stride=depth), :] = dyz[k]
    for half in range(2):
        for index in range(shares.yz_shares):
            begin = half * ncols * depth // 2 + index * shares.yz_rows
            packed[half, index, shares.yz : shares.yz + shares.yz_rows, :] = flat[begin : begin + shares.yz_rows]
    for k in range(depth):
        flat[pl.ds(k, nrows, stride=depth), :] = dxz[k]
    for index in range(shares.chips):
        begin = index * shares.xz_rows
        packed[core, index, shares.xz : shares.xz + shares.xz_rows, :] = flat[begin : begin + shares.xz_rows]
    plane, layer = place[6], place[7]
    for k in range(shares.planes):
        for t in range(shares.layers):
            index = (plane ^ k) * shares.layers + (layer ^ t)
            own_out[k, t] = packed[core, index].astype(BF16)
            other_out[k, t] = packed[1 - core, index].astype(BF16)


def core_kernel(own, other, *outs):
    for k, out in enumerate(outs):
        out[...] = (own[k].astype(F32) + other[k].astype(F32)).astype(BF16)


def plane_kernel(shares, *refs):
    blocks, outs = refs[: shares.planes], refs[shares.planes :]
    size = shares.yz_rows
    for t, out in enumerate(outs):
        got = [block[t].astype(F32) for block in blocks]
        total = sum(got[1:], got[0])
        pieces = [total[: shares.each]]
        for rank in range(shares.ranks):
            pair = got[2 * rank] + got[2 * rank + 1]
            pieces.append(pair[shares.xz : shares.small])
        pieces.append(total[shares.small : shares.yz])
        for column in range(2):
            part = sum(got[column + 2 :: 2], got[column])
            pieces.append(part[shares.yz : shares.yz + size])
        rest = shares.mid_rows - shares.mid_yz - 2 * size
        if rest:
            pieces.append(jnp.zeros((rest, LANES), F32))
        out[...] = jnp.concatenate(pieces, axis=0).astype(BF16)


def layer_kernel(shares, place, *refs):
    layers, size = shares.layers, shares.yz_rows
    blocks, outs = refs[:layers], refs[layers : 2 * layers]
    by_row, by_col, tail = refs[2 * layers :]
    plane, layer = place[6], place[7]
    rank, column = plane // 2, plane % 2
    got = [block[...].astype(F32) for block in blocks]
    total = sum(got[1:], got[0])
    for r in range(shares.ranks):
        begin = shares.xz + r * shares.xz_slot
        by_row[rank ^ r] = total[begin : begin + shares.xz_slot]
    for t in range(layers):
        for c in range(2):
            begin = shares.mid_yz + c * size
            by_col[2 * (layer ^ t) + (column ^ c), 0:size, :] = got[t][begin : begin + size]
    tail[...] = jnp.zeros_like(tail)
    tail[0:2, :] = total[shares.mid_small : shares.mid_yz]
    for j in range(2 * layers):
        tail[2 + j * size : 2 + (j + 1) * size, :] = by_col[j, 0:size, :]
    common = total[: shares.each].astype(BF16)
    for t, out in enumerate(outs):
        out[0 : shares.each, :] = common
        out[shares.each :, :] = jnp.concatenate([by_row[(layer ^ t) // 2], tail[...]], axis=0).astype(BF16)


def last_kernel(shares, classes, place, *refs):
    halves, refs = refs[: 2 * shares.planes], refs[2 * shares.planes :]
    emb, g1, g2, gt, gw1, gw2, gw3, gxz, gyz, whole, w3_rows = refs
    width, hidden = emb.shape[0], gw2.shape[0]
    core, plane, layer = place[5], place[6], place[7]
    row_core, row_side, rank = place[8], place[0], place[9]
    for k in range(shares.planes):
        for t in range(shares.layers):
            index = (plane ^ k) * shares.layers + (layer ^ t)
            whole[core, index] = halves[k][t].astype(F32)
            whole[1 - core, index] = halves[shares.planes + k][t].astype(F32)

    def take(start, ref, lead, lanes):
        for side, index, row, offset, rows in shares.split(start, width if lead is not None else ref.shape[0]):
            block = whole[side, index, row : row + rows, :]
            if lead is not None:
                ref[lead, offset : offset + rows, :] = block
            else:
                ref[offset : offset + rows, lanes] = block

    for name, ref in (("conv1", g1), ("conv2", g2)):
        for tap in range(9):
            take(shares.at[name] + tap * width, ref, tap, None)
    for name, ref in (("w1", gw1), ("w2", gw2)):
        for part in range(hidden // LANES):
            take(shares.at[name] + part * ref.shape[0], ref, None, slice(part * LANES, (part + 1) * LANES))
    small = slice(shares.small, shares.small + 1)
    gt[...] = emb[...] * whole[classes // shares.chips, classes % shares.chips, small, :]
    for part in range(hidden // LANES):
        small = slice(shares.small + part, shares.small + part + 1)
        w3_rows[...] = jnp.zeros_like(w3_rows)
        for q in range(classes):
            w3_rows[q : q + 1, :] = whole[q // shares.chips, q % shares.chips, small, :]
        gw3[part * LANES : (part + 1) * LANES, :] = w3_rows[...].T[:, 0:classes]
    count = gxz.shape[0]
    begin = pl.multiple_of(row_side * count, count)
    gxz[...] = whole[row_core, pl.ds(begin, count), shares.xz : shares.xz + shares.xz_rows, :]
    size, per = shares.yz_rows, shares.yz_rows * shares.yz_shares
    for r in range(2):
        for side in range(2):
            for index in range(shares.yz_shares):
                to = (2 * r + side) * per + index * size
                value = whole[side, index, shares.yz + r * size : shares.yz + (r + 1) * size, :]
                for i in range(1, shares.planes):
                    begin = shares.yz + (2 * i + r) * size
                    value = jnp.where(rank == i, whole[side, index, begin : begin + size, :], value)
                gyz[to : to + size, :] = value


def local(
    xy_noisy,
    xz_plane,
    yz_plane,
    labels,
    timestep,
    conv1_weight,
    conv2_weight,
    time_weight,
    w1,
    w2,
    w3,
):
    grid = Grid()
    nrows, ncols, width = xy_noisy.shape
    depth = labels.shape[2]
    hidden, classes = w3.shape
    count = grid.count
    side = grid.iy % count
    emb = time_embedding(timestep, width)
    temb = jnp.dot(emb, time_weight.astype(F32), precision=lax.Precision.HIGHEST)
    flat_one = conv1_weight.reshape(9 * width, width)
    flat_two = conv2_weight.reshape(9 * width, width)
    back_flat = jnp.transpose(conv2_weight[::-1, ::-1], (0, 1, 3, 2)).reshape(9 * width, width)
    w3_wide = jnp.pad(w3, ((0, 0), (0, LANES - classes)))

    up = lambda i, j: (i + 1, j)
    down = lambda i, j: (i - 1, j)
    left = lambda i, j: (i, j - 1)
    right = lambda i, j: (i, j + 1)

    def lab(part):
        return jnp.pad(part.astype(BF16), ((0, 0), (0, 0), (0, LANES - depth)))

    above = grid.move(jnp.concatenate([xy_noisy[nrows - REACH :], lab(labels[nrows - 1 :])]), up)
    below = grid.move(jnp.concatenate([xy_noisy[:REACH], lab(labels[:1])]), down)

    slab_count = xz_plane.shape[1] // depth
    start = timestep[0] % slab_count * depth
    xz_local = lax.dynamic_slice_in_dim(xz_plane, start, depth, 1)
    share = xz_local.shape[0]
    yz_half = lax.dynamic_slice(yz_plane, (side * ncols, start, 0), (ncols, depth, width))
    first = grid.move(jnp.concatenate([yz_half, xz_local], axis=0), grid.turned(0))
    rim_row = grid.move(
        jnp.where(side == 0, xz_local[:1], xz_local[share - 1 :]),
        lambda i, j: (j // count - 1, count * i + 1) if j % count == 0 else (j // count + 1, count * i),
    )

    def column(at, where):
        cols = jnp.concatenate(
            [above[:REACH, where], xy_noisy[:, where], below[:REACH, where]], axis=0
        )
        yz = first[at].reshape(depth, 1, width)
        extra = jnp.concatenate(
            [yz[:2], above[3:, at : at + 1], lab(labels[:, at : at + 1]), below[3:, at : at + 1], yz[2:]],
            axis=0,
        )
        return jnp.concatenate([jnp.concatenate([cols, extra], axis=1), first[ncols:], rim_row], axis=0)

    before = grid.move(column(ncols - 1, slice(ncols - REACH, ncols)), right)
    after = grid.move(column(0, slice(0, REACH)), left)

    core = grid.ix % 2
    flags = jnp.stack(
        [
            side,
            grid.ix,
            grid.nx - 1 - grid.ix,
            grid.iy,
            grid.ny - 1 - grid.iy,
            core,
            grid.ix // 2 * 2 + grid.iy % 2,
            grid.iy // 2,
            grid.iy // count % 2,
            grid.ix,
        ]
    ).astype(jnp.int32)
    shares = Shares(grid.nx, grid.ny, nrows, ncols, depth, width, hidden)
    planes, layers, chips = shares.planes, shares.layers, shares.chips
    vmem = pl.BlockSpec(memory_space=pltpu.VMEM)
    smem = pl.BlockSpec(memory_space=pltpu.SMEM)
    params = pltpu.CompilerParams(vmem_limit_bytes=VMEM_LIMIT)
    buffer = jax.ShapeDtypeStruct((planes, layers, shares.rows, LANES), BF16)
    own, other = pl.pallas_call(
        functools.partial(main_kernel, classes, shares),
        out_shape=(buffer, buffer),
        in_specs=[smem] + [vmem] * 15,
        out_specs=(vmem, vmem),
        scratch_shapes=[
            pltpu.VMEM((nrows + 6, 32, width), F32),
            pltpu.VMEM((nrows + 4, PITCH, width), F32),
            pltpu.VMEM((nrows + 4, 32, width), F32),
            pltpu.VMEM((nrows + 2, PITCH, width), F32),
            pltpu.VMEM((nrows + 2, PITCH, width), F32),
            pltpu.VMEM(((nrows + 4) * PITCH, 9 * width), BF16),
            pltpu.VMEM((depth, nrows, width), F32),
            pltpu.VMEM((depth, ncols, width), F32),
            pltpu.VMEM((width, hidden), F32),
            pltpu.VMEM((hidden, hidden), F32),
            pltpu.VMEM((LANES, hidden), F32),
            pltpu.VMEM((depth, nrows, width), F32),
            pltpu.VMEM((depth, ncols, width), F32),
            pltpu.VMEM((nrows * depth, width), F32),
            pltpu.VMEM((2, chips, shares.rows, LANES), F32),
        ],
        compiler_params=params,
        name="tile",
    )(
        flags,
        xy_noisy,
        above,
        below,
        before,
        after,
        labels,
        first,
        rim_row,
        temb.reshape(1, width),
        flat_one,
        flat_two,
        back_flat,
        w1,
        w2,
        w3_wide,
    )

    swap = lambda i, j: (i ^ 1, j)
    in_plane = lambda k: lambda i, j: (i ^ (k // 2 * 2), j ^ (k % 2))
    in_layer = lambda t: lambda i, j: (i, j ^ (2 * t))

    def kernel(body, count_in, shape, count_out, name, scratch=(), scalars=False):
        return pl.pallas_call(
            body,
            out_shape=(jax.ShapeDtypeStruct(shape, BF16),) * count_out,
            in_specs=[smem] * scalars + [vmem] * count_in,
            out_specs=(vmem,) * count_out,
            scratch_shapes=list(scratch),
            compiler_params=params,
            name=name,
        )

    swapped = grid.move(other, swap)
    blocks = kernel(core_kernel, 2, (layers, shares.rows, LANES), planes, "cores")(own, swapped)
    blocks = [blocks[0]] + [grid.move(blocks[k], in_plane(k)) for k in range(1, planes)]
    body = functools.partial(plane_kernel, shares)
    blocks = kernel(body, planes, (shares.mid_rows, LANES), layers, "planes")(*blocks)
    blocks = [blocks[0]] + [grid.move(blocks[t], in_layer(t)) for t in range(1, layers)]
    scratch = (
        pltpu.VMEM((shares.ranks, shares.xz_slot, LANES), F32),
        pltpu.VMEM((grid.ny, 8, LANES), F32),
        pltpu.VMEM((shares.end_rows - shares.small, LANES), F32),
    )
    body = functools.partial(layer_kernel, shares)
    blocks = kernel(body, layers, (shares.end_rows, LANES), layers, "layers", scratch, True)(flags, *blocks)
    blocks = [blocks[0]] + [grid.move(blocks[t], in_layer(t)) for t in range(1, layers)]
    mine = jnp.stack(blocks)
    halves = [mine] + [grid.move(mine, in_plane(k)) for k in range(1, planes)]
    halves = halves + [grid.move(half, swap) for half in halves]
    g1, g2, gt, gw1, gw2, gw3, gxz, gyz = pl.pallas_call(
        functools.partial(last_kernel, shares, classes),
        out_shape=(
            jax.ShapeDtypeStruct((9, width, width), F32),
            jax.ShapeDtypeStruct((9, width, width), F32),
            jax.ShapeDtypeStruct((width, width), F32),
            jax.ShapeDtypeStruct((width, hidden), F32),
            jax.ShapeDtypeStruct((hidden, hidden), F32),
            jax.ShapeDtypeStruct((hidden, classes), F32),
            jax.ShapeDtypeStruct((chips // 2, shares.xz_rows, width), F32),
            jax.ShapeDtypeStruct((2 * ncols * depth, width), F32),
        ),
        in_specs=[smem] + [vmem] * (2 * planes + 1),
        out_specs=(vmem,) * 8,
        scratch_shapes=[
            pltpu.VMEM((2, chips, shares.end_rows, LANES), F32),
            pltpu.VMEM((LANES, LANES), F32),
        ],
        compiler_params=params,
        name="spread",
    )(
        flags,
        *halves,
        emb.reshape(width, 1),
    )
    shape = (3, 3, width, width)
    return (
        g1.reshape(shape),
        g2.reshape(shape),
        gt,
        gw1,
        gw2,
        gw3,
        gxz.reshape(share, depth, width),
        gyz.reshape(2 * ncols, depth, width),
    )


def solution(mesh):
    placed = (
        P("gx", "gy", None),
        P("gy", None, None),
        P("gx", None, None),
        P("gx", "gy", None),
        P(),
        P(),
        P(),
        P(),
        P(),
        P(),
        P(),
    )
    return jax.shard_map(
        local,
        mesh=mesh,
        in_specs=placed,
        out_specs=(P(), P(), P(), P(), P(), P(), P("gy", None, None), P("gx", None, None)),
        check_vma=False,
    )
```

```python
import functools
import math

import jax
import jax.numpy as jnp
from jax import lax
from jax.experimental import pallas as pl
from jax.experimental.pallas import tpu as pltpu
from jax.sharding import PartitionSpec as P

loss_weight = 1.0 / 256.0
BOTH = ("gx", "gy")
LANES = 128
PITCH = 24
REACH = 3
CLASS_ROWS = 32
F32, BF16 = jnp.float32, jnp.bfloat16
VMEM_LIMIT = 48 * 1024 * 1024


def sigmoid(value):
    return 0.5 * jnp.tanh(0.5 * value) + 0.5


def silu_pair(value):
    sig = sigmoid(value)
    out = value * sig
    return out, sig + out - out * sig


def dot(a, b):
    return jnp.dot(a, b, preferred_element_type=F32)


def dot_nt(a, b):
    return lax.dot_general(a, b, (((1,), (1,)), ((), ())), preferred_element_type=F32)


def dot_tn(a, b):
    return lax.dot_general(a, b, (((0,), (0,)), ((), ())), preferred_element_type=F32)


def time_embedding(timestep, width):
    half = width // 2
    freqs = jnp.exp(-math.log(10000.0) * jnp.arange(half, dtype=jnp.float32) / half)
    angle = timestep.astype(jnp.float32)[0] * freqs
    return jnp.concatenate([jnp.cos(angle), jnp.sin(angle)])


class Grid:
    def __init__(self):
        self.nx, self.ny = lax.axis_size("gx"), lax.axis_size("gy")
        self.count = self.ny // self.nx
        self.ix, self.iy = lax.axis_index("gx"), lax.axis_index("gy")

    def move(self, array, target):
        pairs = []
        for i in range(self.nx):
            for j in range(self.ny):
                k, m = target(i, j)
                if 0 <= k < self.nx and 0 <= m < self.ny:
                    pairs.append((i * self.ny + j, k * self.ny + m))
        return lax.ppermute(array, BOTH, pairs)

    def turned(self, shift):
        count = self.count
        return lambda i, j: (j // count, count * i + (j % count + shift) % count)


class Shares:
    def __init__(self, nx, ny, nrows, ncols, depth, width, hidden):
        sizes = (("conv1", 9 * width), ("conv2", 9 * width), ("w1", width * hidden // LANES), ("w2", hidden * hidden // LANES))
        self.at, total = {}, 0
        for name, rows in sizes:
            self.at[name] = total
            total += rows
        self.chips = chips = nx * ny // 2
        self.ranks, self.planes, self.layers = nx // 2, nx, ny // 2
        self.each = -(-total // (2 * chips * 8)) * 8
        self.xz_rows = nrows * depth // chips
        self.yz_rows = max(1, ncols * depth // 2 // chips)
        self.yz_shares = ncols * depth // 2 // self.yz_rows
        self.xz_slot = -(-self.xz_rows // 8) * 8
        even = lambda rows: -(-rows // 16) * 16
        self.xz = self.each
        self.small = self.xz + self.xz_slot
        self.yz = self.small + 2
        self.rows = even(self.yz + self.yz_rows)
        self.mid_small = self.xz + self.ranks * self.xz_slot
        self.mid_yz = self.mid_small + 2
        self.mid_rows = even(self.mid_yz + 2 * self.yz_rows)
        self.end_rows = even(self.yz + ny * self.yz_rows)

    def split(self, start, rows):
        done = 0
        while done < rows:
            share, row = divmod(start + done, self.each)
            step = min(rows - done, self.each - row)
            yield share // self.chips, share % self.chips, row, done, step
            done += step


def main_kernel(
    classes,
    shares,
    place,
    xy,
    above,
    below,
    before,
    after,
    labels,
    first,
    rim_row,
    temb,
    conv1,
    conv2,
    back,
    w1,
    w2,
    w3,
    own_out,
    other_out,
    xs,
    hs,
    acts,
    xyds,
    dx,
    das,
    paired,
    patch,
    xzs,
    yzs,
    dw1,
    dw2,
    dw3,
    dxz,
    dyz,
    flat,
    packed,
):
    nrows, ncols, width = xy.shape
    depth = labels.shape[1]
    hidden = w1.shape[1]
    share = nrows // 2
    side, core = place[0], place[5]
    open_up, open_down, open_left, open_right = (place[1] > 0, place[2] > 0, place[3] > 0, place[4] > 0)
    tall = nrows + 2 * REACH

    mid_r, mid_c = slice(REACH, REACH + nrows), slice(REACH, REACH + ncols)
    xs[...] = jnp.zeros_like(xs)
    xs[mid_r, mid_c] = xy[...].astype(F32)
    xs[0:REACH, mid_c] = above[0:REACH].astype(F32)
    xs[REACH + nrows : 2 * REACH + nrows, mid_c] = below[0:REACH].astype(F32)
    xs[:, 0:REACH] = before[0:tall].astype(F32)[:, 0:REACH]
    xs[:, REACH + ncols : 2 * REACH + ncols] = after[0:tall].astype(F32)[:, 0:REACH]

    def gather(source, row, col, rows, cols):
        count = rows * cols
        for a in range(3):
            for b in range(3):
                piece = source[row + a : row + a + rows, col + b : col + b + cols, :]
                tap = (3 * a + b) * width
                patch[0:count, tap : tap + width] = piece.reshape(count, width).astype(BF16)
        return count

    def pair_rows(source, weight, out, rows, cols):
        span, inner = 3 * width, rows // 2
        count = inner * cols
        paired[0 : 3 * span, 0:width] = weight[...]
        paired[3 * span : 4 * span, 0:width] = jnp.zeros((span, width), BF16)
        paired[0:span, width : 2 * width] = jnp.zeros((span, width), BF16)
        paired[span : 4 * span, width : 2 * width] = weight[...]
        for a in range(4):
            for b in range(3):
                piece = source[pl.ds(a, inner, stride=2), b : b + cols, :]
                tap = (3 * a + b) * width
                patch[0:count, tap : tap + width] = piece.reshape(count, width).astype(BF16)
        both = dot(patch[0:count, 0 : 4 * span], paired[...])
        out[pl.ds(0, inner, stride=2)] = both[:, 0:width].reshape(inner, cols, width)
        out[pl.ds(1, inner, stride=2)] = both[:, width : 2 * width].reshape(inner, cols, width)

    pair_rows(xs, conv1, hs, nrows + 4, PITCH)
    h1 = hs[...] + temb[...][None]
    hs[...] = h1
    row = lax.broadcasted_iota(jnp.int32, h1.shape, 0)
    col = lax.broadcasted_iota(jnp.int32, h1.shape, 1)
    low_r = jnp.where(open_up, 0, 2)
    high_r = jnp.where(open_down, nrows + 4, nrows + 2)
    low_c = jnp.where(open_left, 0, 2)
    high_c = jnp.where(open_right, ncols + 4, ncols + 2)
    inside = (row >= low_r) & (row < high_r) & (col >= low_c) & (col < high_c)
    a1 = jnp.where(inside, h1 * sigmoid(h1), 0.0)
    acts[...] = jnp.zeros_like(acts)
    acts[:, 0:PITCH] = a1.astype(BF16).astype(F32)
    pair_rows(acts, conv2, xyds, nrows + 2, PITCH)
    xyds[...] = xyds[...].astype(BF16).astype(F32)

    rows_before = before[tall : tall + share + 1].astype(F32)
    rows_after = after[tall : tall + share + 1].astype(F32)
    mine = first[...].astype(F32)
    rim_mine = rim_row[...].astype(F32)
    same_at = pl.ds(pl.multiple_of(side * share, share), share)
    second_at = pl.ds(pl.multiple_of((1 - side) * share, share), share)
    xz_above, xz_below = [], []
    for k in range(depth):
        second = jnp.where(side == 0, rows_after[:, k, :], rows_before[:, k, :])
        yzs[k] = mine[0:ncols, k, :]
        xzs[k, same_at, :] = mine[ncols:, k, :]
        xzs[k, second_at, :] = second[0:share]
        rim_same, rim_second = rim_mine[:, k, :], second[share:]
        xz_above.append(jnp.where(side == 0, rim_same, rim_second))
        xz_below.append(jnp.where(side == 0, rim_second, rim_same))

    def decode(feat, label):
        pixels = feat.shape[0] // depth
        u1 = dot(feat, w1[...])
        g1, s1 = silu_pair(u1)
        g1 = g1.astype(BF16)
        u2 = dot(g1, w2[...])
        g2, s2 = silu_pair(u2)
        g2 = g2.astype(BF16)
        logits = dot(g2[0:pixels], w3[0])
        for k in range(1, depth):
            logits = logits + dot(g2[k * pixels : (k + 1) * pixels], w3[k])
        turned = logits.T
        outs = []
        for k in range(depth):
            part = turned[k * CLASS_ROWS : (k + 1) * CLASS_ROWS]
            lane = lax.broadcasted_iota(jnp.int32, part.shape, 0)
            part = jnp.where(lane < classes, part, -jnp.inf)
            power = jnp.exp(part - jnp.max(part, axis=0, keepdims=True))
            prob = power / jnp.sum(power, axis=0, keepdims=True)
            onehot = jnp.where(lane.astype(F32) == label[k : k + 1], 1.0, 0.0)
            outs.append(loss_weight * (prob - onehot))
        turned = jnp.concatenate(outs, axis=0)
        dlogits = turned.T.astype(BF16)
        dg2 = jnp.concatenate([dot_nt(dlogits, w3[k]) for k in range(depth)], axis=0)
        du2 = (dg2 * s2).astype(BF16)
        du1 = (dot_nt(du2, w2[...]) * s1).astype(BF16)
        return g1, g2, turned.astype(BF16), du2, du1, dot_nt(du1, w1[...])

    dw1[...] = jnp.zeros_like(dw1)
    dw2[...] = jnp.zeros_like(dw2)
    dw3[...] = jnp.zeros_like(dw3)
    dyz[...] = jnp.zeros_like(dyz)
    dx[...] = jnp.zeros_like(dx)
    chunk = nrows // labels.shape[0]
    size = chunk * ncols

    def step(index, carry):
        r0 = pl.multiple_of(index * chunk, chunk)
        tile = xyds[pl.ds(r0 + 1, chunk), 1 : ncols + 1, :]
        feats = []
        for k in range(depth):
            xz_k = xzs[k, pl.ds(r0, chunk), :]
            feat = tile + xz_k[:, None, :] + yzs[k][None]
            feats.append(feat.reshape(size, width).astype(BF16))
        feat = jnp.concatenate(feats, axis=0)
        g1, g2, dlogits, du2, du1, dfeat = decode(feat, labels[index])
        for k in range(depth):
            dw3[...] += dot(dlogits[k * CLASS_ROWS : (k + 1) * CLASS_ROWS], g2[k * size : (k + 1) * size])
        dw2[...] += dot_tn(g1, du2)
        dw1[...] += dot_tn(feat, du1)
        total = jnp.zeros((chunk, ncols, width), F32)
        for k in range(depth):
            piece = dfeat[k * size : (k + 1) * size].reshape(chunk, ncols, width)
            total = total + piece
            dxz[k, pl.ds(r0, chunk), :] = jnp.sum(piece, axis=1)
            dyz[k] += jnp.sum(piece, axis=0)
        dx[pl.ds(r0 + 1, chunk), 1 : ncols + 1, :] = total.astype(BF16).astype(F32)
        return carry

    lax.fori_loop(0, nrows // chunk, step, 0, unroll=True)

    lab_before = before[2 : nrows + 4, 3, :].astype(F32)
    lab_after = after[2 : nrows + 4, 3, :].astype(F32)
    lab_up = above[3].astype(F32)
    lab_down = below[3].astype(F32)
    tail = jnp.zeros((PITCH - ncols - 2, LANES), F32)
    span = 2 * PITCH + 2 * nrows
    fill = -span % LANES
    lab_rim = jnp.concatenate(
        [
            lab_before[0:1],
            lab_up,
            lab_after[0:1],
            tail,
            lab_before[nrows + 1 : nrows + 2],
            lab_down,
            lab_after[nrows + 1 : nrows + 2],
            tail,
            lab_before[1 : nrows + 1],
            lab_after[1 : nrows + 1],
            jnp.zeros((fill, LANES), F32),
        ],
        axis=0,
    )
    rim_at = (0, 1, nrows + 2 * REACH - 2, nrows + 2 * REACH - 1)
    feats = []
    zero_tail = jnp.zeros((PITCH - ncols - 2, width), F32)
    for k in range(depth):
        yz_before = before[rim_at[k], 3:4, :].astype(F32)
        yz_after = after[rim_at[k], 3:4, :].astype(F32)
        yz_row = jnp.concatenate([yz_before, yzs[k], yz_after, zero_tail], axis=0)
        feats.append(xyds[0] + xz_above[k] + yz_row)
        feats.append(xyds[nrows + 1] + xz_below[k] + yz_row)
        feats.append(xyds[1 : nrows + 1, 0, :] + xzs[k] + yz_before)
        feats.append(xyds[1 : nrows + 1, ncols + 1, :] + xzs[k] + yz_after)
        feats.append(jnp.zeros((fill, width), F32))
    rim = decode(jnp.concatenate(feats, axis=0).astype(BF16), lab_rim.T[0:8])[-1]
    whole_span = span + fill
    rim_sum = rim[0:span]
    for k in range(1, depth):
        rim_sum = rim_sum + rim[k * whole_span : k * whole_span + span]
    rim_sum = rim_sum.astype(BF16).astype(F32)
    rcol = lax.broadcasted_iota(jnp.int32, (PITCH, width), 0)
    keep = (rcol >= jnp.where(open_left, 0, 1)) & (rcol < jnp.where(open_right, ncols + 2, ncols + 1))
    dx[0] = jnp.where(keep & open_up, rim_sum[0:PITCH], 0.0)
    dx[nrows + 1] = jnp.where(keep & open_down, rim_sum[PITCH : 2 * PITCH], 0.0)
    west = rim_sum[2 * PITCH : 2 * PITCH + nrows]
    east = rim_sum[2 * PITCH + nrows : span]
    dx[1 : nrows + 1, 0, :] = jnp.where(open_left, west, 0.0)
    dx[1 : nrows + 1, ncols + 1, :] = jnp.where(open_right, east, 0.0)

    def put(start, block):
        for half, index, row, offset, rows in shares.split(start, block.shape[0]):
            packed[half, index, row : row + rows, :] = block[offset : offset + rows]

    def weight_gradient(start, dout):
        grad = dot_tn(dout, patch[0 : nrows * ncols])
        for tap in range(9):
            put(start + tap * width, grad[:, tap * width : (tap + 1) * width].T)

    packed[...] = jnp.zeros_like(packed)

    n3 = gather(acts, 1, 1, nrows, ncols)
    dxyd = dx[1 : nrows + 1, 1 : ncols + 1, :].reshape(n3, width).astype(BF16)
    weight_gradient(shares.at["conv2"], dxyd)
    pair_rows(dx, back, das, nrows, ncols)
    da1 = das[...].reshape(n3, width)
    _, slope = silu_pair(hs[2 : nrows + 2, 2 : ncols + 2, :].reshape(n3, width))
    dh1 = (da1 * slope).astype(BF16)
    gather(xs, 2, 2, nrows, ncols)
    weight_gradient(shares.at["conv1"], dh1)

    for name, ref in (("w1", dw1), ("w2", dw2)):
        rows = ref.shape[0]
        for half in range(hidden // LANES):
            put(shares.at[name] + half * rows, ref[:, half * LANES : (half + 1) * LANES])
    for q in range(classes):
        where = packed.at[q // shares.chips, q % shares.chips]
        for half in range(hidden // LANES):
            row = shares.small + half
            where[row : row + 1, :] = dw3[q : q + 1, half * LANES : (half + 1) * LANES]
    time_row = jnp.sum(dh1.astype(F32), axis=0, keepdims=True)
    packed[classes // shares.chips, classes % shares.chips, shares.small : shares.small + 1, :] = time_row
    for k in range(depth):
        flat[pl.ds(k, ncols, stride=depth), :] = dyz[k]
    for half in range(2):
        for index in range(shares.yz_shares):
            begin = half * ncols * depth // 2 + index * shares.yz_rows
            packed[half, index, shares.yz : shares.yz + shares.yz_rows, :] = flat[begin : begin + shares.yz_rows]
    for k in range(depth):
        flat[pl.ds(k, nrows, stride=depth), :] = dxz[k]
    for index in range(shares.chips):
        begin = index * shares.xz_rows
        packed[core, index, shares.xz : shares.xz + shares.xz_rows, :] = flat[begin : begin + shares.xz_rows]
    plane, layer = place[6], place[7]
    for k in range(shares.planes):
        for t in range(shares.layers):
            index = (plane ^ k) * shares.layers + (layer ^ t)
            own_out[k, t] = packed[core, index].astype(BF16)
            other_out[k, t] = packed[1 - core, index].astype(BF16)


def core_kernel(own, other, *outs):
    for k, out in enumerate(outs):
        out[...] = (own[k].astype(F32) + other[k].astype(F32)).astype(BF16)


def plane_kernel(shares, *refs):
    blocks, outs = refs[: shares.planes], refs[shares.planes :]
    size = shares.yz_rows
    for t, out in enumerate(outs):
        got = [block[t].astype(F32) for block in blocks]
        total = sum(got[1:], got[0])
        pieces = [total[: shares.each]]
        for rank in range(shares.ranks):
            pair = got[2 * rank] + got[2 * rank + 1]
            pieces.append(pair[shares.xz : shares.small])
        pieces.append(total[shares.small : shares.yz])
        for column in range(2):
            part = sum(got[column + 2 :: 2], got[column])
            pieces.append(part[shares.yz : shares.yz + size])
        rest = shares.mid_rows - shares.mid_yz - 2 * size
        if rest:
            pieces.append(jnp.zeros((rest, LANES), F32))
        out[...] = jnp.concatenate(pieces, axis=0).astype(BF16)


def layer_kernel(shares, place, *refs):
    layers, size = shares.layers, shares.yz_rows
    blocks, outs = refs[:layers], refs[layers : 2 * layers]
    by_row, by_col, tail = refs[2 * layers :]
    plane, layer = place[6], place[7]
    rank, column = plane // 2, plane % 2
    got = [block[...].astype(F32) for block in blocks]
    total = sum(got[1:], got[0])
    for r in range(shares.ranks):
        begin = shares.xz + r * shares.xz_slot
        by_row[rank ^ r] = total[begin : begin + shares.xz_slot]
    for t in range(layers):
        for c in range(2):
            begin = shares.mid_yz + c * size
            by_col[2 * (layer ^ t) + (column ^ c), 0:size, :] = got[t][begin : begin + size]
    tail[...] = jnp.zeros_like(tail)
    tail[0:2, :] = total[shares.mid_small : shares.mid_yz]
    for j in range(2 * layers):
        tail[2 + j * size : 2 + (j + 1) * size, :] = by_col[j, 0:size, :]
    common = total[: shares.each].astype(BF16)
    for t, out in enumerate(outs):
        out[0 : shares.each, :] = common
        out[shares.each :, :] = jnp.concatenate([by_row[(layer ^ t) // 2], tail[...]], axis=0).astype(BF16)


def last_kernel(shares, classes, place, *refs):
    halves, refs = refs[: 2 * shares.planes], refs[2 * shares.planes :]
    emb, g1, g2, gt, gw1, gw2, gw3, gxz, gyz, whole, w3_rows = refs
    width, hidden = emb.shape[0], gw2.shape[0]
    core, plane, layer = place[5], place[6], place[7]
    row_core, row_side, rank = place[8], place[0], place[9]
    for k in range(shares.planes):
        for t in range(shares.layers):
            index = (plane ^ k) * shares.layers + (layer ^ t)
            whole[core, index] = halves[k][t].astype(F32)
            whole[1 - core, index] = halves[shares.planes + k][t].astype(F32)

    def take(start, ref, lead, lanes):
        for side, index, row, offset, rows in shares.split(start, width if lead is not None else ref.shape[0]):
            block = whole[side, index, row : row + rows, :]
            if lead is not None:
                ref[lead, offset : offset + rows, :] = block
            else:
                ref[offset : offset + rows, lanes] = block

    for name, ref in (("conv1", g1), ("conv2", g2)):
        for tap in range(9):
            take(shares.at[name] + tap * width, ref, tap, None)
    for name, ref in (("w1", gw1), ("w2", gw2)):
        for part in range(hidden // LANES):
            take(shares.at[name] + part * ref.shape[0], ref, None, slice(part * LANES, (part + 1) * LANES))
    small = slice(shares.small, shares.small + 1)
    gt[...] = emb[...] * whole[classes // shares.chips, classes % shares.chips, small, :]
    for part in range(hidden // LANES):
        small = slice(shares.small + part, shares.small + part + 1)
        w3_rows[...] = jnp.zeros_like(w3_rows)
        for q in range(classes):
            w3_rows[q : q + 1, :] = whole[q // shares.chips, q % shares.chips, small, :]
        gw3[part * LANES : (part + 1) * LANES, :] = w3_rows[...].T[:, 0:classes]
    count = gxz.shape[0]
    begin = pl.multiple_of(row_side * count, count)
    gxz[...] = whole[row_core, pl.ds(begin, count), shares.xz : shares.xz + shares.xz_rows, :]
    size, per = shares.yz_rows, shares.yz_rows * shares.yz_shares
    for r in range(2):
        for side in range(2):
            for index in range(shares.yz_shares):
                to = (2 * r + side) * per + index * size
                value = whole[side, index, shares.yz + r * size : shares.yz + (r + 1) * size, :]
                for i in range(1, shares.planes):
                    begin = shares.yz + (2 * i + r) * size
                    value = jnp.where(rank == i, whole[side, index, begin : begin + size, :], value)
                gyz[to : to + size, :] = value


def local(
    xy_noisy,
    xz_plane,
    yz_plane,
    labels,
    timestep,
    conv1_weight,
    conv2_weight,
    time_weight,
    w1,
    w2,
    w3,
):
    grid = Grid()
    nrows, ncols, width = xy_noisy.shape
    depth = labels.shape[2]
    hidden, classes = w3.shape
    count = grid.count
    side = grid.iy % count
    emb = time_embedding(timestep, width)
    temb = jnp.dot(emb, time_weight.astype(F32), precision=lax.Precision.HIGHEST)
    flat_one = conv1_weight.reshape(9 * width, width)
    flat_two = conv2_weight.reshape(9 * width, width)
    back_flat = jnp.transpose(conv2_weight[::-1, ::-1], (0, 1, 3, 2)).reshape(9 * width, width)
    w3_wide = jnp.stack(
        [jnp.pad(w3, ((0, 0), (CLASS_ROWS * k, LANES - classes - CLASS_ROWS * k))) for k in range(depth)]
    )
    chunks = nrows // 16
    labels_by_depth = labels.astype(F32).reshape(chunks, -1, depth).transpose(0, 2, 1)

    up = lambda i, j: (i + 1, j)
    down = lambda i, j: (i - 1, j)
    left = lambda i, j: (i, j - 1)
    right = lambda i, j: (i, j + 1)

    def lab(part):
        return jnp.pad(part.astype(BF16), ((0, 0), (0, 0), (0, LANES - depth)))

    above = grid.move(jnp.concatenate([xy_noisy[nrows - REACH :], lab(labels[nrows - 1 :])]), up)
    below = grid.move(jnp.concatenate([xy_noisy[:REACH], lab(labels[:1])]), down)

    slab_count = xz_plane.shape[1] // depth
    start = timestep[0] % slab_count * depth
    xz_local = lax.dynamic_slice_in_dim(xz_plane, start, depth, 1)
    share = xz_local.shape[0]
    yz_half = lax.dynamic_slice(yz_plane, (side * ncols, start, 0), (ncols, depth, width))
    first = grid.move(jnp.concatenate([yz_half, xz_local], axis=0), grid.turned(0))
    rim_row = grid.move(
        jnp.where(side == 0, xz_local[:1], xz_local[share - 1 :]),
        lambda i, j: (j // count - 1, count * i + 1) if j % count == 0 else (j // count + 1, count * i),
    )

    def column(at, where):
        cols = jnp.concatenate(
            [above[:REACH, where], xy_noisy[:, where], below[:REACH, where]], axis=0
        )
        yz = first[at].reshape(depth, 1, width)
        extra = jnp.concatenate(
            [yz[:2], above[3:, at : at + 1], lab(labels[:, at : at + 1]), below[3:, at : at + 1], yz[2:]],
            axis=0,
        )
        return jnp.concatenate([jnp.concatenate([cols, extra], axis=1), first[ncols:], rim_row], axis=0)

    before = grid.move(column(ncols - 1, slice(ncols - REACH, ncols)), right)
    after = grid.move(column(0, slice(0, REACH)), left)

    core = grid.ix % 2
    flags = jnp.stack(
        [
            side,
            grid.ix,
            grid.nx - 1 - grid.ix,
            grid.iy,
            grid.ny - 1 - grid.iy,
            core,
            grid.ix // 2 * 2 + grid.iy % 2,
            grid.iy // 2,
            grid.iy // count % 2,
            grid.ix,
        ]
    ).astype(jnp.int32)
    shares = Shares(grid.nx, grid.ny, nrows, ncols, depth, width, hidden)
    planes, layers, chips = shares.planes, shares.layers, shares.chips
    vmem = pl.BlockSpec(memory_space=pltpu.VMEM)
    smem = pl.BlockSpec(memory_space=pltpu.SMEM)
    params = pltpu.CompilerParams(vmem_limit_bytes=VMEM_LIMIT)
    buffer = jax.ShapeDtypeStruct((planes, layers, shares.rows, LANES), BF16)
    own, other = pl.pallas_call(
        functools.partial(main_kernel, classes, shares),
        out_shape=(buffer, buffer),
        in_specs=[smem] + [vmem] * 15,
        out_specs=(vmem, vmem),
        scratch_shapes=[
            pltpu.VMEM((nrows + 6, 32, width), F32),
            pltpu.VMEM((nrows + 4, PITCH, width), F32),
            pltpu.VMEM((nrows + 4, 32, width), F32),
            pltpu.VMEM((nrows + 2, PITCH, width), F32),
            pltpu.VMEM((nrows + 2, PITCH, width), F32),
            pltpu.VMEM((nrows, ncols, width), F32),
            pltpu.VMEM((12 * width, 2 * width), BF16),
            pltpu.VMEM((nrows * ncols, 12 * width), BF16),
            pltpu.VMEM((depth, nrows, width), F32),
            pltpu.VMEM((depth, ncols, width), F32),
            pltpu.VMEM((width, hidden), F32),
            pltpu.VMEM((hidden, hidden), F32),
            pltpu.VMEM((CLASS_ROWS, hidden), F32),
            pltpu.VMEM((depth, nrows, width), F32),
            pltpu.VMEM((depth, ncols, width), F32),
            pltpu.VMEM((nrows * depth, width), F32),
            pltpu.VMEM((2, chips, shares.rows, LANES), F32),
        ],
        compiler_params=params,
        name="tile",
    )(
        flags,
        xy_noisy,
        above,
        below,
        before,
        after,
        labels_by_depth,
        first,
        rim_row,
        temb.reshape(1, width),
        flat_one,
        flat_two,
        back_flat,
        w1,
        w2,
        w3_wide,
    )

    swap = lambda i, j: (i ^ 1, j)
    in_plane = lambda k: lambda i, j: (i ^ (k // 2 * 2), j ^ (k % 2))
    in_layer = lambda t: lambda i, j: (i, j ^ (2 * t))

    def kernel(body, count_in, shape, count_out, name, scratch=(), scalars=False):
        return pl.pallas_call(
            body,
            out_shape=(jax.ShapeDtypeStruct(shape, BF16),) * count_out,
            in_specs=[smem] * scalars + [vmem] * count_in,
            out_specs=(vmem,) * count_out,
            scratch_shapes=list(scratch),
            compiler_params=params,
            name=name,
        )

    swapped = grid.move(other, swap)
    blocks = kernel(core_kernel, 2, (layers, shares.rows, LANES), planes, "cores")(own, swapped)
    blocks = [blocks[0]] + [grid.move(blocks[k], in_plane(k)) for k in range(1, planes)]
    body = functools.partial(plane_kernel, shares)
    blocks = kernel(body, planes, (shares.mid_rows, LANES), layers, "planes")(*blocks)
    blocks = [blocks[0]] + [grid.move(blocks[t], in_layer(t)) for t in range(1, layers)]
    scratch = (
        pltpu.VMEM((shares.ranks, shares.xz_slot, LANES), F32),
        pltpu.VMEM((grid.ny, 8, LANES), F32),
        pltpu.VMEM((shares.end_rows - shares.small, LANES), F32),
    )
    body = functools.partial(layer_kernel, shares)
    blocks = kernel(body, layers, (shares.end_rows, LANES), layers, "layers", scratch, True)(flags, *blocks)
    blocks = [blocks[0]] + [grid.move(blocks[t], in_layer(t)) for t in range(1, layers)]
    mine = jnp.stack(blocks)
    halves = [mine] + [grid.move(mine, in_plane(k)) for k in range(1, planes)]
    halves = halves + [grid.move(half, swap) for half in halves]
    g1, g2, gt, gw1, gw2, gw3, gxz, gyz = pl.pallas_call(
        functools.partial(last_kernel, shares, classes),
        out_shape=(
            jax.ShapeDtypeStruct((9, width, width), F32),
            jax.ShapeDtypeStruct((9, width, width), F32),
            jax.ShapeDtypeStruct((width, width), F32),
            jax.ShapeDtypeStruct((width, hidden), F32),
            jax.ShapeDtypeStruct((hidden, hidden), F32),
            jax.ShapeDtypeStruct((hidden, classes), F32),
            jax.ShapeDtypeStruct((chips // 2, shares.xz_rows, width), F32),
            jax.ShapeDtypeStruct((2 * ncols * depth, width), F32),
        ),
        in_specs=[smem] + [vmem] * (2 * planes + 1),
        out_specs=(vmem,) * 8,
        scratch_shapes=[
            pltpu.VMEM((2, chips, shares.end_rows, LANES), F32),
            pltpu.VMEM((LANES, LANES), F32),
        ],
        compiler_params=params,
        name="spread",
    )(
        flags,
        *halves,
        emb.reshape(width, 1),
    )
    shape = (3, 3, width, width)
    return (
        g1.reshape(shape),
        g2.reshape(shape),
        gt,
        gw1,
        gw2,
        gw3,
        gxz.reshape(share, depth, width),
        gyz.reshape(2 * ncols, depth, width),
    )


def solution(mesh):
    placed = (
        P("gx", "gy", None),
        P("gy", None, None),
        P("gx", None, None),
        P("gx", "gy", None),
        P(),
        P(),
        P(),
        P(),
        P(),
        P(),
        P(),
    )
    return jax.shard_map(
        local,
        mesh=mesh,
        in_specs=placed,
        out_specs=(P(), P(), P(), P(), P(), P(), P("gy", None, None), P("gx", None, None)),
        check_vma=False,
    )
```

```python
import functools
import math

import jax
import jax.numpy as jnp
from jax import lax
from jax.experimental import pallas as pl
from jax.experimental.pallas import tpu as pltpu
from jax.sharding import PartitionSpec as P

loss_weight = 1.0 / 256.0
BOTH = ("gx", "gy")
LANES = 128
PITCH = 24
REACH = 3
CLASS_ROWS = 32
F32, BF16 = jnp.float32, jnp.bfloat16
VMEM_LIMIT = 48 * 1024 * 1024


def sigmoid(value):
    return 0.5 * jnp.tanh(0.5 * value) + 0.5


def silu_pair(value):
    sig = sigmoid(value)
    out = value * sig
    return out, sig + out - out * sig


def dot(a, b):
    return jnp.dot(a, b, preferred_element_type=F32)


def dot_nt(a, b):
    return lax.dot_general(a, b, (((1,), (1,)), ((), ())), preferred_element_type=F32)


def dot_tn(a, b):
    return lax.dot_general(a, b, (((0,), (0,)), ((), ())), preferred_element_type=F32)


def time_embedding(timestep, width):
    half = width // 2
    freqs = jnp.exp(-math.log(10000.0) * jnp.arange(half, dtype=jnp.float32) / half)
    angle = timestep.astype(jnp.float32)[0] * freqs
    return jnp.concatenate([jnp.cos(angle), jnp.sin(angle)])


class Grid:
    def __init__(self):
        self.nx, self.ny = lax.axis_size("gx"), lax.axis_size("gy")
        self.count = self.ny // self.nx
        self.ix, self.iy = lax.axis_index("gx"), lax.axis_index("gy")

    def move(self, array, target):
        pairs = []
        for i in range(self.nx):
            for j in range(self.ny):
                k, m = target(i, j)
                if 0 <= k < self.nx and 0 <= m < self.ny:
                    pairs.append((i * self.ny + j, k * self.ny + m))
        return lax.ppermute(array, BOTH, pairs)

    def turned(self, shift):
        count = self.count
        return lambda i, j: (j // count, count * i + (j % count + shift) % count)


class Shares:
    def __init__(self, nx, ny, nrows, ncols, depth, width, hidden):
        sizes = (("conv1", 9 * width), ("conv2", 9 * width), ("w1", width * hidden // LANES), ("w2", hidden * hidden // LANES))
        self.at, total = {}, 0
        for name, rows in sizes:
            self.at[name] = total
            total += rows
        self.chips = chips = nx * ny // 2
        self.ranks, self.planes, self.layers = nx // 2, nx, ny // 2
        self.each = -(-total // (2 * chips * 8)) * 8
        self.xz_rows = nrows * depth // chips
        self.yz_rows = max(1, ncols * depth // 2 // chips)
        self.yz_shares = ncols * depth // 2 // self.yz_rows
        self.xz_slot = -(-self.xz_rows // 8) * 8
        even = lambda rows: -(-rows // 16) * 16
        self.xz = self.each
        self.small = self.xz + self.xz_slot
        self.yz = self.small + 2
        self.rows = even(self.yz + self.yz_rows)
        self.mid_small = self.xz + self.ranks * self.xz_slot
        self.mid_yz = self.mid_small + 2
        self.mid_rows = even(self.mid_yz + 2 * self.yz_rows)
        self.end_rows = even(self.yz + ny * self.yz_rows)

    def split(self, start, rows):
        done = 0
        while done < rows:
            share, row = divmod(start + done, self.each)
            step = min(rows - done, self.each - row)
            yield share // self.chips, share % self.chips, row, done, step
            done += step


def main_kernel(
    classes,
    shares,
    place,
    xy,
    above,
    below,
    before,
    after,
    labels,
    first,
    temb,
    conv1,
    conv2,
    back,
    w1,
    w2,
    w3,
    own_out,
    other_out,
    xs,
    hs,
    acts,
    xyds,
    dx,
    das,
    paired,
    patch,
    xzs,
    yzs,
    dw1,
    dw2,
    dw3,
    dxz,
    dyz,
    flat,
    packed,
):
    nrows, ncols, width = xy.shape
    depth = labels.shape[1]
    hidden = w1.shape[1]
    share = nrows // 2
    side, core = place[0], place[5]
    open_up, open_down, open_left, open_right = (place[1] > 0, place[2] > 0, place[3] > 0, place[4] > 0)
    tall = nrows + 2 * REACH

    mid_r, mid_c = slice(REACH, REACH + nrows), slice(REACH, REACH + ncols)
    xs[...] = jnp.zeros_like(xs)
    xs[mid_r, mid_c] = xy[...].astype(F32)
    xs[0:REACH, mid_c] = above[0:REACH].astype(F32)
    xs[REACH + nrows : 2 * REACH + nrows, mid_c] = below[0:REACH].astype(F32)
    xs[:, 0:REACH] = before[0:tall].astype(F32)[:, 0:REACH]
    xs[:, REACH + ncols : 2 * REACH + ncols] = after[0:tall].astype(F32)[:, 0:REACH]

    def gather(source, row, col, rows, cols):
        count = rows * cols
        for a in range(3):
            for b in range(3):
                piece = source[row + a : row + a + rows, col + b : col + b + cols, :]
                tap = (3 * a + b) * width
                patch[0:count, tap : tap + width] = piece.reshape(count, width).astype(BF16)
        return count

    def pair_rows(source, weight, out, rows, cols):
        span, inner = 3 * width, rows // 2
        count = inner * cols
        paired[0 : 3 * span, 0:width] = weight[...]
        paired[3 * span : 4 * span, 0:width] = jnp.zeros((span, width), BF16)
        paired[0:span, width : 2 * width] = jnp.zeros((span, width), BF16)
        paired[span : 4 * span, width : 2 * width] = weight[...]
        for a in range(4):
            for b in range(3):
                piece = source[pl.ds(a, inner, stride=2), b : b + cols, :]
                tap = (3 * a + b) * width
                patch[0:count, tap : tap + width] = piece.reshape(count, width).astype(BF16)
        both = dot(patch[0:count, 0 : 4 * span], paired[...])
        out[pl.ds(0, inner, stride=2)] = both[:, 0:width].reshape(inner, cols, width)
        out[pl.ds(1, inner, stride=2)] = both[:, width : 2 * width].reshape(inner, cols, width)

    pair_rows(xs, conv1, hs, nrows + 4, PITCH)
    h1 = hs[...] + temb[...][None]
    hs[...] = h1
    row = lax.broadcasted_iota(jnp.int32, h1.shape, 0)
    col = lax.broadcasted_iota(jnp.int32, h1.shape, 1)
    low_r = jnp.where(open_up, 0, 2)
    high_r = jnp.where(open_down, nrows + 4, nrows + 2)
    low_c = jnp.where(open_left, 0, 2)
    high_c = jnp.where(open_right, ncols + 4, ncols + 2)
    inside = (row >= low_r) & (row < high_r) & (col >= low_c) & (col < high_c)
    a1 = jnp.where(inside, h1 * sigmoid(h1), 0.0)
    acts[...] = jnp.zeros_like(acts)
    acts[:, 0:PITCH] = a1.astype(BF16).astype(F32)
    pair_rows(acts, conv2, xyds, nrows + 2, PITCH)
    xyds[...] = xyds[...].astype(BF16).astype(F32)

    rows_before = before[tall : tall + share + 1].astype(F32)
    rows_after = after[tall : tall + share + 1].astype(F32)
    mine = first[...].astype(F32)
    edge_above, edge_below = above[4].astype(F32), below[4].astype(F32)
    same_at = pl.ds(pl.multiple_of(side * share, share), share)
    second_at = pl.ds(pl.multiple_of((1 - side) * share, share), share)
    xz_above, xz_below = [], []
    for k in range(depth):
        second = jnp.where(side == 0, rows_after[:, k, :], rows_before[:, k, :])
        yzs[k] = mine[0:ncols, k, :]
        xzs[k, same_at, :] = mine[ncols:, k, :]
        xzs[k, second_at, :] = second[0:share]
        xz_above.append(jnp.where(side == 0, second[share:], edge_above[k : k + 1]))
        xz_below.append(jnp.where(side == 0, edge_below[k : k + 1], second[share:]))

    def decode(feat, label):
        pixels = feat.shape[0] // depth
        u1 = dot(feat, w1[...])
        g1, s1 = silu_pair(u1)
        g1 = g1.astype(BF16)
        u2 = dot(g1, w2[...])
        g2, s2 = silu_pair(u2)
        g2 = g2.astype(BF16)
        logits = dot(g2[0:pixels], w3[0])
        for k in range(1, depth):
            logits = logits + dot(g2[k * pixels : (k + 1) * pixels], w3[k])
        turned = logits.T
        outs = []
        for k in range(depth):
            part = turned[k * CLASS_ROWS : (k + 1) * CLASS_ROWS]
            lane = lax.broadcasted_iota(jnp.int32, part.shape, 0)
            part = jnp.where(lane < classes, part, -jnp.inf)
            power = jnp.exp(part - jnp.max(part, axis=0, keepdims=True))
            prob = power / jnp.sum(power, axis=0, keepdims=True)
            onehot = jnp.where(lane.astype(F32) == label[k : k + 1], 1.0, 0.0)
            outs.append(loss_weight * (prob - onehot))
        turned = jnp.concatenate(outs, axis=0)
        dlogits = turned.T.astype(BF16)
        dg2 = jnp.concatenate([dot_nt(dlogits, w3[k]) for k in range(depth)], axis=0)
        du2 = (dg2 * s2).astype(BF16)
        du1 = (dot_nt(du2, w2[...]) * s1).astype(BF16)
        return g1, g2, turned.astype(BF16), du2, du1, dot_nt(du1, w1[...])

    dw1[...] = jnp.zeros_like(dw1)
    dw2[...] = jnp.zeros_like(dw2)
    dw3[...] = jnp.zeros_like(dw3)
    dyz[...] = jnp.zeros_like(dyz)
    dx[...] = jnp.zeros_like(dx)
    chunk = nrows // labels.shape[0]
    size = chunk * ncols

    def step(index, carry):
        r0 = pl.multiple_of(index * chunk, chunk)
        tile = xyds[pl.ds(r0 + 1, chunk), 1 : ncols + 1, :]
        feats = []
        for k in range(depth):
            xz_k = xzs[k, pl.ds(r0, chunk), :]
            feat = tile + xz_k[:, None, :] + yzs[k][None]
            feats.append(feat.reshape(size, width).astype(BF16))
        feat = jnp.concatenate(feats, axis=0)
        g1, g2, dlogits, du2, du1, dfeat = decode(feat, labels[index])
        for k in range(depth):
            dw3[...] += dot(dlogits[k * CLASS_ROWS : (k + 1) * CLASS_ROWS], g2[k * size : (k + 1) * size])
        dw2[...] += dot_tn(g1, du2)
        dw1[...] += dot_tn(feat, du1)
        total = jnp.zeros((chunk, ncols, width), F32)
        for k in range(depth):
            piece = dfeat[k * size : (k + 1) * size].reshape(chunk, ncols, width)
            total = total + piece
            dxz[k, pl.ds(r0, chunk), :] = jnp.sum(piece, axis=1)
            dyz[k] += jnp.sum(piece, axis=0)
        dx[pl.ds(r0 + 1, chunk), 1 : ncols + 1, :] = total.astype(BF16).astype(F32)
        return carry

    lax.fori_loop(0, nrows // chunk, step, 0, unroll=True)

    lab_before = before[2 : nrows + 4, 3, :].astype(F32)
    lab_after = after[2 : nrows + 4, 3, :].astype(F32)
    lab_up = above[3].astype(F32)
    lab_down = below[3].astype(F32)
    tail = jnp.zeros((PITCH - ncols - 2, LANES), F32)
    span = 2 * PITCH + 2 * nrows
    fill = -span % LANES
    lab_rim = jnp.concatenate(
        [
            lab_before[0:1],
            lab_up,
            lab_after[0:1],
            tail,
            lab_before[nrows + 1 : nrows + 2],
            lab_down,
            lab_after[nrows + 1 : nrows + 2],
            tail,
            lab_before[1 : nrows + 1],
            lab_after[1 : nrows + 1],
            jnp.zeros((fill, LANES), F32),
        ],
        axis=0,
    )
    rim_at = (0, 1, nrows + 2 * REACH - 2, nrows + 2 * REACH - 1)
    feats = []
    zero_tail = jnp.zeros((PITCH - ncols - 2, width), F32)
    for k in range(depth):
        yz_before = before[rim_at[k], 3:4, :].astype(F32)
        yz_after = after[rim_at[k], 3:4, :].astype(F32)
        yz_row = jnp.concatenate([yz_before, yzs[k], yz_after, zero_tail], axis=0)
        feats.append(xyds[0] + xz_above[k] + yz_row)
        feats.append(xyds[nrows + 1] + xz_below[k] + yz_row)
        feats.append(xyds[1 : nrows + 1, 0, :] + xzs[k] + yz_before)
        feats.append(xyds[1 : nrows + 1, ncols + 1, :] + xzs[k] + yz_after)
        feats.append(jnp.zeros((fill, width), F32))
    rim = decode(jnp.concatenate(feats, axis=0).astype(BF16), lab_rim.T[0:8])[-1]
    whole_span = span + fill
    rim_sum = rim[0:span]
    for k in range(1, depth):
        rim_sum = rim_sum + rim[k * whole_span : k * whole_span + span]
    rim_sum = rim_sum.astype(BF16).astype(F32)
    rcol = lax.broadcasted_iota(jnp.int32, (PITCH, width), 0)
    keep = (rcol >= jnp.where(open_left, 0, 1)) & (rcol < jnp.where(open_right, ncols + 2, ncols + 1))
    dx[0] = jnp.where(keep & open_up, rim_sum[0:PITCH], 0.0)
    dx[nrows + 1] = jnp.where(keep & open_down, rim_sum[PITCH : 2 * PITCH], 0.0)
    west = rim_sum[2 * PITCH : 2 * PITCH + nrows]
    east = rim_sum[2 * PITCH + nrows : span]
    dx[1 : nrows + 1, 0, :] = jnp.where(open_left, west, 0.0)
    dx[1 : nrows + 1, ncols + 1, :] = jnp.where(open_right, east, 0.0)

    def put(start, block):
        for half, index, row, offset, rows in shares.split(start, block.shape[0]):
            packed[half, index, row : row + rows, :] = block[offset : offset + rows]

    def weight_gradient(start, dout):
        grad = dot_tn(dout, patch[0 : nrows * ncols])
        for tap in range(9):
            put(start + tap * width, grad[:, tap * width : (tap + 1) * width].T)

    packed[...] = jnp.zeros_like(packed)

    n3 = gather(acts, 1, 1, nrows, ncols)
    dxyd = dx[1 : nrows + 1, 1 : ncols + 1, :].reshape(n3, width).astype(BF16)
    weight_gradient(shares.at["conv2"], dxyd)
    pair_rows(dx, back, das, nrows, ncols)
    da1 = das[...].reshape(n3, width)
    _, slope = silu_pair(hs[2 : nrows + 2, 2 : ncols + 2, :].reshape(n3, width))
    dh1 = (da1 * slope).astype(BF16)
    gather(xs, 2, 2, nrows, ncols)
    weight_gradient(shares.at["conv1"], dh1)

    for name, ref in (("w1", dw1), ("w2", dw2)):
        rows = ref.shape[0]
        for half in range(hidden // LANES):
            put(shares.at[name] + half * rows, ref[:, half * LANES : (half + 1) * LANES])
    for q in range(classes):
        where = packed.at[q // shares.chips, q % shares.chips]
        for half in range(hidden // LANES):
            row = shares.small + half
            where[row : row + 1, :] = dw3[q : q + 1, half * LANES : (half + 1) * LANES]
    time_row = jnp.sum(dh1.astype(F32), axis=0, keepdims=True)
    packed[classes // shares.chips, classes % shares.chips, shares.small : shares.small + 1, :] = time_row
    for k in range(depth):
        flat[pl.ds(k, ncols, stride=depth), :] = dyz[k]
    for half in range(2):
        for index in range(shares.yz_shares):
            begin = half * ncols * depth // 2 + index * shares.yz_rows
            packed[half, index, shares.yz : shares.yz + shares.yz_rows, :] = flat[begin : begin + shares.yz_rows]
    for k in range(depth):
        flat[pl.ds(k, nrows, stride=depth), :] = dxz[k]
    for index in range(shares.chips):
        begin = index * shares.xz_rows
        packed[core, index, shares.xz : shares.xz + shares.xz_rows, :] = flat[begin : begin + shares.xz_rows]
    plane, layer = place[6], place[7]
    for k in range(shares.planes):
        for t in range(shares.layers):
            index = (plane ^ k) * shares.layers + (layer ^ t)
            own_out[k, t] = packed[core, index].astype(BF16)
            other_out[k, t] = packed[1 - core, index].astype(BF16)


def core_kernel(own, other, *outs):
    for k, out in enumerate(outs):
        out[...] = (own[k].astype(F32) + other[k].astype(F32)).astype(BF16)


def plane_kernel(shares, *refs):
    blocks, outs = refs[: shares.planes], refs[shares.planes :]
    size = shares.yz_rows
    for t, out in enumerate(outs):
        got = [block[t].astype(F32) for block in blocks]
        total = sum(got[1:], got[0])
        pieces = [total[: shares.each]]
        for rank in range(shares.ranks):
            pair = got[2 * rank] + got[2 * rank + 1]
            pieces.append(pair[shares.xz : shares.small])
        pieces.append(total[shares.small : shares.yz])
        for column in range(2):
            part = sum(got[column + 2 :: 2], got[column])
            pieces.append(part[shares.yz : shares.yz + size])
        rest = shares.mid_rows - shares.mid_yz - 2 * size
        if rest:
            pieces.append(jnp.zeros((rest, LANES), F32))
        out[...] = jnp.concatenate(pieces, axis=0).astype(BF16)


def layer_kernel(shares, place, *refs):
    layers, size = shares.layers, shares.yz_rows
    blocks, outs = refs[:layers], refs[layers : 2 * layers]
    by_row, by_col, tail = refs[2 * layers :]
    plane, layer = place[6], place[7]
    rank, column = plane // 2, plane % 2
    got = [block[...].astype(F32) for block in blocks]
    total = sum(got[1:], got[0])
    for r in range(shares.ranks):
        begin = shares.xz + r * shares.xz_slot
        by_row[rank ^ r] = total[begin : begin + shares.xz_slot]
    for t in range(layers):
        for c in range(2):
            begin = shares.mid_yz + c * size
            by_col[2 * (layer ^ t) + (column ^ c), 0:size, :] = got[t][begin : begin + size]
    tail[...] = jnp.zeros_like(tail)
    tail[0:2, :] = total[shares.mid_small : shares.mid_yz]
    for j in range(2 * layers):
        tail[2 + j * size : 2 + (j + 1) * size, :] = by_col[j, 0:size, :]
    common = total[: shares.each].astype(BF16)
    for t, out in enumerate(outs):
        out[0 : shares.each, :] = common
        out[shares.each :, :] = jnp.concatenate([by_row[(layer ^ t) // 2], tail[...]], axis=0).astype(BF16)


def last_kernel(shares, classes, place, *refs):
    halves, refs = refs[: 2 * shares.planes], refs[2 * shares.planes :]
    emb, g1, g2, gt, gw1, gw2, gw3, gxz, gyz, whole, rest = refs
    each = shares.each
    width, hidden = emb.shape[0], gw2.shape[0]
    core, plane, layer = place[5], place[6], place[7]
    row_core, row_side, rank = place[8], place[0], place[9]
    for k in range(shares.planes):
        for t in range(shares.layers):
            index = (plane ^ k) * shares.layers + (layer ^ t)
            for half, block in ((core, halves[k]), (1 - core, halves[shares.planes + k])):
                whole[half, index] = block[t, 0:each, :]
                rest[half, index] = block[t, each:, :].astype(F32)

    def take(start, ref, lead, lanes):
        for side, index, row, offset, rows in shares.split(start, width if lead is not None else ref.shape[0]):
            block = whole[side, index, row : row + rows, :].astype(F32)
            if lead is not None:
                ref[lead, offset : offset + rows, :] = block
            else:
                ref[offset : offset + rows, lanes] = block

    for name, ref in (("conv1", g1), ("conv2", g2)):
        for tap in range(9):
            take(shares.at[name] + tap * width, ref, tap, None)
    for name, ref in (("w1", gw1), ("w2", gw2)):
        for part in range(hidden // LANES):
            take(shares.at[name] + part * ref.shape[0], ref, None, slice(part * LANES, (part + 1) * LANES))
    at_small, at_yz = shares.small - each, shares.yz - each
    gt[...] = emb[...] * rest[classes // shares.chips, classes % shares.chips, at_small : at_small + 1, :]
    for q in range(classes):
        for part in range(hidden // LANES):
            value = rest[q // shares.chips, q % shares.chips, at_small + part : at_small + part + 1, :]
            gw3[q : q + 1, part * LANES : (part + 1) * LANES] = value
    count = gxz.shape[0]
    begin = pl.multiple_of(row_side * count, count)
    gxz[...] = rest[row_core, pl.ds(begin, count), 0 : shares.xz_rows, :]
    size, per = shares.yz_rows, shares.yz_rows * shares.yz_shares
    for r in range(2):
        for side in range(2):
            for index in range(shares.yz_shares):
                to = (2 * r + side) * per + index * size
                value = rest[side, index, at_yz + r * size : at_yz + (r + 1) * size, :]
                for i in range(1, shares.planes):
                    begin = at_yz + (2 * i + r) * size
                    value = jnp.where(rank == i, rest[side, index, begin : begin + size, :], value)
                gyz[to : to + size, :] = value


def local(
    xy_noisy,
    xz_plane,
    yz_plane,
    labels,
    timestep,
    conv1_weight,
    conv2_weight,
    time_weight,
    w1,
    w2,
    w3,
):
    grid = Grid()
    nrows, ncols, width = xy_noisy.shape
    depth = labels.shape[2]
    hidden, classes = w3.shape
    count = grid.count
    side = grid.iy % count
    emb = time_embedding(timestep, width)
    temb = jnp.dot(emb, time_weight.astype(F32), precision=lax.Precision.HIGHEST)
    flat_one = conv1_weight.reshape(9 * width, width)
    flat_two = conv2_weight.reshape(9 * width, width)
    back_flat = jnp.transpose(conv2_weight[::-1, ::-1], (0, 1, 3, 2)).reshape(9 * width, width)
    w3_wide = jnp.stack(
        [jnp.pad(w3, ((0, 0), (CLASS_ROWS * k, LANES - classes - CLASS_ROWS * k))) for k in range(depth)]
    )
    chunks = nrows // 16
    labels_by_depth = labels.astype(F32).reshape(chunks, -1, depth).transpose(0, 2, 1)

    up = lambda i, j: (i + 1, j)
    down = lambda i, j: (i - 1, j)
    left = lambda i, j: (i, j - 1)
    right = lambda i, j: (i, j + 1)

    def lab(part):
        return jnp.pad(part.astype(BF16), ((0, 0), (0, 0), (0, LANES - depth)))

    slab_count = xz_plane.shape[1] // depth
    start = timestep[0] % slab_count * depth
    xz_local = lax.dynamic_slice_in_dim(xz_plane, start, depth, 1)
    share = xz_local.shape[0]
    yz_half = lax.dynamic_slice(yz_plane, (side * ncols, start, 0), (ncols, depth, width))
    first = grid.move(jnp.concatenate([yz_half, xz_local], axis=0), grid.turned(0))

    def row(features, labels_row, edge):
        edge = jnp.pad(edge[None], ((0, 0), (0, ncols - depth), (0, 0)))
        return jnp.concatenate([features, lab(labels_row), edge])

    above = grid.move(row(xy_noisy[nrows - REACH :], labels[nrows - 1 :], first[ncols + share - 1]), up)
    below = grid.move(row(xy_noisy[:REACH], labels[:1], first[ncols]), down)
    edge_row = jnp.where(side == 0, below[4:, :depth], above[4:, :depth])

    def column(at, where):
        cols = jnp.concatenate(
            [above[:REACH, where], xy_noisy[:, where], below[:REACH, where]], axis=0
        )
        yz = first[at].reshape(depth, 1, width)
        extra = jnp.concatenate(
            [yz[:2], above[3:4, at : at + 1], lab(labels[:, at : at + 1]), below[3:4, at : at + 1], yz[2:]],
            axis=0,
        )
        return jnp.concatenate([jnp.concatenate([cols, extra], axis=1), first[ncols:], edge_row], axis=0)

    before = grid.move(column(ncols - 1, slice(ncols - REACH, ncols)), right)
    after = grid.move(column(0, slice(0, REACH)), left)

    core = grid.ix % 2
    flags = jnp.stack(
        [
            side,
            grid.ix,
            grid.nx - 1 - grid.ix,
            grid.iy,
            grid.ny - 1 - grid.iy,
            core,
            grid.ix // 2 * 2 + grid.iy % 2,
            grid.iy // 2,
            grid.iy // count % 2,
            grid.ix,
        ]
    ).astype(jnp.int32)
    shares = Shares(grid.nx, grid.ny, nrows, ncols, depth, width, hidden)
    planes, layers, chips = shares.planes, shares.layers, shares.chips
    vmem = pl.BlockSpec(memory_space=pltpu.VMEM)
    smem = pl.BlockSpec(memory_space=pltpu.SMEM)
    params = pltpu.CompilerParams(vmem_limit_bytes=VMEM_LIMIT)
    buffer = jax.ShapeDtypeStruct((planes, layers, shares.rows, LANES), BF16)
    own, other = pl.pallas_call(
        functools.partial(main_kernel, classes, shares),
        out_shape=(buffer, buffer),
        in_specs=[smem] + [vmem] * 14,
        out_specs=(vmem, vmem),
        scratch_shapes=[
            pltpu.VMEM((nrows + 6, 32, width), F32),
            pltpu.VMEM((nrows + 4, PITCH, width), F32),
            pltpu.VMEM((nrows + 4, 32, width), F32),
            pltpu.VMEM((nrows + 2, PITCH, width), F32),
            pltpu.VMEM((nrows + 2, PITCH, width), F32),
            pltpu.VMEM((nrows, ncols, width), F32),
            pltpu.VMEM((12 * width, 2 * width), BF16),
            pltpu.VMEM((nrows * ncols, 12 * width), BF16),
            pltpu.VMEM((depth, nrows, width), F32),
            pltpu.VMEM((depth, ncols, width), F32),
            pltpu.VMEM((width, hidden), F32),
            pltpu.VMEM((hidden, hidden), F32),
            pltpu.VMEM((CLASS_ROWS, hidden), F32),
            pltpu.VMEM((depth, nrows, width), F32),
            pltpu.VMEM((depth, ncols, width), F32),
            pltpu.VMEM((nrows * depth, width), F32),
            pltpu.VMEM((2, chips, shares.rows, LANES), F32),
        ],
        compiler_params=params,
        name="tile",
    )(
        flags,
        xy_noisy,
        above,
        below,
        before,
        after,
        labels_by_depth,
        first,
        temb.reshape(1, width),
        flat_one,
        flat_two,
        back_flat,
        w1,
        w2,
        w3_wide,
    )

    swap = lambda i, j: (i ^ 1, j)
    in_plane = lambda k: lambda i, j: (i ^ (k // 2 * 2), j ^ (k % 2))
    in_layer = lambda t: lambda i, j: (i, j ^ (2 * t))

    def kernel(body, count_in, shape, count_out, name, scratch=(), scalars=False):
        return pl.pallas_call(
            body,
            out_shape=(jax.ShapeDtypeStruct(shape, BF16),) * count_out,
            in_specs=[smem] * scalars + [vmem] * count_in,
            out_specs=(vmem,) * count_out,
            scratch_shapes=list(scratch),
            compiler_params=params,
            name=name,
        )

    swapped = grid.move(other, swap)
    blocks = kernel(core_kernel, 2, (layers, shares.rows, LANES), planes, "cores")(own, swapped)
    blocks = [blocks[0]] + [grid.move(blocks[k], in_plane(k)) for k in range(1, planes)]
    body = functools.partial(plane_kernel, shares)
    blocks = kernel(body, planes, (shares.mid_rows, LANES), layers, "planes")(*blocks)
    blocks = [blocks[0]] + [grid.move(blocks[t], in_layer(t)) for t in range(1, layers)]
    scratch = (
        pltpu.VMEM((shares.ranks, shares.xz_slot, LANES), F32),
        pltpu.VMEM((grid.ny, 8, LANES), F32),
        pltpu.VMEM((shares.end_rows - shares.small, LANES), F32),
    )
    body = functools.partial(layer_kernel, shares)
    blocks = kernel(body, layers, (shares.end_rows, LANES), layers, "layers", scratch, True)(flags, *blocks)
    blocks = [blocks[0]] + [grid.move(blocks[t], in_layer(t)) for t in range(1, layers)]
    mine = jnp.stack(blocks)
    halves = [mine] + [grid.move(mine, in_plane(k)) for k in range(1, planes)]
    halves = halves + [grid.move(half, swap) for half in halves]
    g1, g2, gt, gw1, gw2, gw3, gxz, gyz = pl.pallas_call(
        functools.partial(last_kernel, shares, classes),
        out_shape=(
            jax.ShapeDtypeStruct((9, width, width), F32),
            jax.ShapeDtypeStruct((9, width, width), F32),
            jax.ShapeDtypeStruct((width, width), F32),
            jax.ShapeDtypeStruct((width, hidden), F32),
            jax.ShapeDtypeStruct((hidden, hidden), F32),
            jax.ShapeDtypeStruct((classes, hidden), F32),
            jax.ShapeDtypeStruct((chips // 2, shares.xz_rows, width), F32),
            jax.ShapeDtypeStruct((2 * ncols * depth, width), F32),
        ),
        in_specs=[smem] + [vmem] * (2 * planes + 1),
        out_specs=(vmem,) * 8,
        scratch_shapes=[
            pltpu.VMEM((2, chips, shares.each, LANES), BF16),
            pltpu.VMEM((2, chips, shares.end_rows - shares.each, LANES), F32),
        ],
        compiler_params=params,
        name="spread",
    )(
        flags,
        *halves,
        emb.reshape(width, 1),
    )
    shape = (3, 3, width, width)
    return (
        g1.reshape(shape),
        g2.reshape(shape),
        gt,
        gw1,
        gw2,
        gw3.T,
        gxz.reshape(share, depth, width),
        gyz.reshape(2 * ncols, depth, width),
    )


def solution(mesh):
    placed = (
        P("gx", "gy", None),
        P("gy", None, None),
        P("gx", None, None),
        P("gx", "gy", None),
        P(),
        P(),
        P(),
        P(),
        P(),
        P(),
        P(),
    )
    return jax.shard_map(
        local,
        mesh=mesh,
        in_specs=placed,
        out_specs=(P(), P(), P(), P(), P(), P(), P("gy", None, None), P("gx", None, None)),
        check_vma=False,
    )
```

```python
import functools
import math

import jax
import jax.numpy as jnp
from jax import lax
from jax.experimental import pallas as pl
from jax.experimental.pallas import tpu as pltpu
from jax.sharding import PartitionSpec as P

loss_weight = 1.0 / 256.0
BOTH = ("gx", "gy")
LANES = 128
PITCH = 24
REACH = 3
CLASS_ROWS = 32
F32, BF16 = jnp.float32, jnp.bfloat16
VMEM_LIMIT = 48 * 1024 * 1024


def sigmoid(value):
    return 0.5 * jnp.tanh(0.5 * value) + 0.5


def silu_pair(value):
    sig = sigmoid(value)
    out = value * sig
    return out, sig + out - out * sig


def dot(a, b):
    return jnp.dot(a, b, preferred_element_type=F32)


def dot_nt(a, b):
    return lax.dot_general(a, b, (((1,), (1,)), ((), ())), preferred_element_type=F32)


def dot_tn(a, b):
    return lax.dot_general(a, b, (((0,), (0,)), ((), ())), preferred_element_type=F32)


def time_embedding(timestep, width):
    half = width // 2
    freqs = jnp.exp(-math.log(10000.0) * jnp.arange(half, dtype=jnp.float32) / half)
    angle = timestep.astype(jnp.float32)[0] * freqs
    return jnp.concatenate([jnp.cos(angle), jnp.sin(angle)])


class Grid:
    def __init__(self):
        self.nx, self.ny = lax.axis_size("gx"), lax.axis_size("gy")
        self.count = self.ny // self.nx
        self.ix, self.iy = lax.axis_index("gx"), lax.axis_index("gy")

    def move(self, array, target):
        pairs = []
        for i in range(self.nx):
            for j in range(self.ny):
                k, m = target(i, j)
                if 0 <= k < self.nx and 0 <= m < self.ny:
                    pairs.append((i * self.ny + j, k * self.ny + m))
        return lax.ppermute(array, BOTH, pairs)

    def turned(self, shift):
        count = self.count
        return lambda i, j: (j // count, count * i + (j % count + shift) % count)


class Shares:
    def __init__(self, nx, ny, nrows, ncols, depth, width, hidden):
        sizes = (("conv1", 9 * width), ("conv2", 9 * width), ("w1", width * hidden // LANES), ("w2", hidden * hidden // LANES))
        self.at, total = {}, 0
        for name, rows in sizes:
            self.at[name] = total
            total += rows
        self.chips = chips = nx * ny // 2
        self.ranks, self.planes, self.layers = nx // 2, nx, ny // 2
        self.each = -(-total // (2 * chips * 8)) * 8
        self.xz_rows = nrows * depth // chips
        self.yz_rows = max(1, ncols * depth // 2 // chips)
        self.yz_shares = ncols * depth // 2 // self.yz_rows
        self.xz_slot = -(-self.xz_rows // 8) * 8
        even = lambda rows: -(-rows // 8) * 8
        self.xz = self.each
        self.small = self.xz + self.xz_slot
        self.yz = self.small + 2
        self.rows = even(self.yz + self.yz_rows)
        self.mid_small = self.xz + self.ranks * self.xz_slot
        self.mid_yz = self.mid_small + 2
        self.mid_rows = even(self.mid_yz + 2 * self.yz_rows)
        self.end_rows = even(self.yz + ny * self.yz_rows)

    def split(self, start, rows):
        done = 0
        while done < rows:
            share, row = divmod(start + done, self.each)
            step = min(rows - done, self.each - row)
            yield share // self.chips, share % self.chips, row, done, step
            done += step


def main_kernel(
    classes,
    shares,
    place,
    xy,
    above,
    below,
    before,
    after,
    labels,
    first,
    temb,
    conv1,
    conv2,
    back,
    w1,
    w2,
    w3,
    own_out,
    other_out,
    xs,
    hs,
    acts,
    xyds,
    dx,
    das,
    paired,
    patch,
    xzs,
    yzs,
    dw1,
    dw2,
    dw3,
    dxz,
    dyz,
    flat,
    packed,
):
    nrows, ncols, width = xy.shape
    depth = labels.shape[1]
    hidden = w1.shape[1]
    share = nrows // 2
    side, core = place[0], place[5]
    open_up, open_down, open_left, open_right = (place[1] > 0, place[2] > 0, place[3] > 0, place[4] > 0)
    tall = nrows + 2 * REACH

    mid_r, mid_c = slice(REACH, REACH + nrows), slice(REACH, REACH + ncols)
    xs[...] = jnp.zeros_like(xs)
    xs[mid_r, mid_c] = xy[...].astype(F32)
    xs[0:REACH, mid_c] = above[0:REACH].astype(F32)
    xs[REACH + nrows : 2 * REACH + nrows, mid_c] = below[0:REACH].astype(F32)
    xs[:, 0:REACH] = before[0:tall].astype(F32)[:, 0:REACH]
    xs[:, REACH + ncols : 2 * REACH + ncols] = after[0:tall].astype(F32)[:, 0:REACH]

    def gather(source, row, col, rows, cols):
        count = rows * cols
        for a in range(3):
            for b in range(3):
                piece = source[row + a : row + a + rows, col + b : col + b + cols, :]
                tap = (3 * a + b) * width
                patch[0:count, tap : tap + width] = piece.reshape(count, width).astype(BF16)
        return count

    def pair_rows(source, weight, out, rows, cols):
        span, inner = 3 * width, rows // 2
        count = inner * cols
        paired[0 : 3 * span, 0:width] = weight[...]
        paired[3 * span : 4 * span, 0:width] = jnp.zeros((span, width), BF16)
        paired[0:span, width : 2 * width] = jnp.zeros((span, width), BF16)
        paired[span : 4 * span, width : 2 * width] = weight[...]
        for a in range(4):
            for b in range(3):
                piece = source[pl.ds(a, inner, stride=2), b : b + cols, :]
                tap = (3 * a + b) * width
                patch[0:count, tap : tap + width] = piece.reshape(count, width).astype(BF16)
        both = dot(patch[0:count, 0 : 4 * span], paired[...])
        out[pl.ds(0, inner, stride=2)] = both[:, 0:width].reshape(inner, cols, width)
        out[pl.ds(1, inner, stride=2)] = both[:, width : 2 * width].reshape(inner, cols, width)

    pair_rows(xs, conv1, hs, nrows + 4, PITCH)
    h1 = hs[...] + temb[...][None]
    hs[...] = h1
    row = lax.broadcasted_iota(jnp.int32, h1.shape, 0)
    col = lax.broadcasted_iota(jnp.int32, h1.shape, 1)
    low_r = jnp.where(open_up, 0, 2)
    high_r = jnp.where(open_down, nrows + 4, nrows + 2)
    low_c = jnp.where(open_left, 0, 2)
    high_c = jnp.where(open_right, ncols + 4, ncols + 2)
    inside = (row >= low_r) & (row < high_r) & (col >= low_c) & (col < high_c)
    a1 = jnp.where(inside, h1 * sigmoid(h1), 0.0)
    acts[...] = jnp.zeros_like(acts)
    acts[:, 0:PITCH] = a1.astype(BF16).astype(F32)
    pair_rows(acts, conv2, xyds, nrows + 2, PITCH)
    xyds[...] = xyds[...].astype(BF16).astype(F32)

    rows_before = before[tall : tall + share + 1].astype(F32)
    rows_after = after[tall : tall + share + 1].astype(F32)
    mine = first[...].astype(F32)
    edge_above, edge_below = above[4].astype(F32), below[4].astype(F32)
    same_at = pl.ds(pl.multiple_of(side * share, share), share)
    second_at = pl.ds(pl.multiple_of((1 - side) * share, share), share)
    xz_above, xz_below = [], []
    for k in range(depth):
        second = jnp.where(side == 0, rows_after[:, k, :], rows_before[:, k, :])
        yzs[k] = mine[0:ncols, k, :]
        xzs[k, same_at, :] = mine[ncols:, k, :]
        xzs[k, second_at, :] = second[0:share]
        xz_above.append(jnp.where(side == 0, second[share:], edge_above[k : k + 1]))
        xz_below.append(jnp.where(side == 0, edge_below[k : k + 1], second[share:]))

    def decode(feat, label):
        pixels = feat.shape[0] // depth
        u1 = dot(feat, w1[...])
        g1, s1 = silu_pair(u1)
        g1 = g1.astype(BF16)
        u2 = dot(g1, w2[...])
        g2, s2 = silu_pair(u2)
        g2 = g2.astype(BF16)
        logits = dot(g2[0:pixels], w3[0])
        for k in range(1, depth):
            logits = logits + dot(g2[k * pixels : (k + 1) * pixels], w3[k])
        turned = logits.T
        outs = []
        for k in range(depth):
            part = turned[k * CLASS_ROWS : (k + 1) * CLASS_ROWS]
            lane = lax.broadcasted_iota(jnp.int32, part.shape, 0)
            part = jnp.where(lane < classes, part, -jnp.inf)
            power = jnp.exp(part - jnp.max(part, axis=0, keepdims=True))
            prob = power / jnp.sum(power, axis=0, keepdims=True)
            onehot = jnp.where(lane.astype(F32) == label[k : k + 1], 1.0, 0.0)
            outs.append(loss_weight * (prob - onehot))
        turned = jnp.concatenate(outs, axis=0)
        dlogits = turned.T.astype(BF16)
        dg2 = jnp.concatenate([dot_nt(dlogits, w3[k]) for k in range(depth)], axis=0)
        du2 = (dg2 * s2).astype(BF16)
        du1 = (dot_nt(du2, w2[...]) * s1).astype(BF16)
        return g1, g2, turned.astype(BF16), du2, du1, dot_nt(du1, w1[...])

    dw1[...] = jnp.zeros_like(dw1)
    dw2[...] = jnp.zeros_like(dw2)
    dw3[...] = jnp.zeros_like(dw3)
    dyz[...] = jnp.zeros_like(dyz)
    dx[...] = jnp.zeros_like(dx)
    chunk = nrows // labels.shape[0]
    size = chunk * ncols

    def step(index, carry):
        r0 = pl.multiple_of(index * chunk, chunk)
        tile = xyds[pl.ds(r0 + 1, chunk), 1 : ncols + 1, :]
        feats = []
        for k in range(depth):
            xz_k = xzs[k, pl.ds(r0, chunk), :]
            feat = tile + xz_k[:, None, :] + yzs[k][None]
            feats.append(feat.reshape(size, width).astype(BF16))
        feat = jnp.concatenate(feats, axis=0)
        g1, g2, dlogits, du2, du1, dfeat = decode(feat, labels[index])
        for k in range(depth):
            dw3[...] += dot(dlogits[k * CLASS_ROWS : (k + 1) * CLASS_ROWS], g2[k * size : (k + 1) * size])
        dw2[...] += dot_tn(g1, du2)
        dw1[...] += dot_tn(feat, du1)
        total = jnp.zeros((chunk, ncols, width), F32)
        for k in range(depth):
            piece = dfeat[k * size : (k + 1) * size].reshape(chunk, ncols, width)
            total = total + piece
            dxz[k, pl.ds(r0, chunk), :] = jnp.sum(piece, axis=1)
            dyz[k] += jnp.sum(piece, axis=0)
        dx[pl.ds(r0 + 1, chunk), 1 : ncols + 1, :] = total.astype(BF16).astype(F32)
        return carry

    lax.fori_loop(0, nrows // chunk, step, 0, unroll=True)

    lab_before = before[2 : nrows + 4, 3, :].astype(F32)
    lab_after = after[2 : nrows + 4, 3, :].astype(F32)
    lab_up = above[3].astype(F32)
    lab_down = below[3].astype(F32)
    tail = jnp.zeros((PITCH - ncols - 2, LANES), F32)
    span = 2 * PITCH + 2 * nrows
    fill = -span % LANES
    lab_rim = jnp.concatenate(
        [
            lab_before[0:1],
            lab_up,
            lab_after[0:1],
            tail,
            lab_before[nrows + 1 : nrows + 2],
            lab_down,
            lab_after[nrows + 1 : nrows + 2],
            tail,
            lab_before[1 : nrows + 1],
            lab_after[1 : nrows + 1],
            jnp.zeros((fill, LANES), F32),
        ],
        axis=0,
    )
    rim_at = (0, 1, nrows + 2 * REACH - 2, nrows + 2 * REACH - 1)
    feats = []
    zero_tail = jnp.zeros((PITCH - ncols - 2, width), F32)
    for k in range(depth):
        yz_before = before[rim_at[k], 3:4, :].astype(F32)
        yz_after = after[rim_at[k], 3:4, :].astype(F32)
        yz_row = jnp.concatenate([yz_before, yzs[k], yz_after, zero_tail], axis=0)
        feats.append(xyds[0] + xz_above[k] + yz_row)
        feats.append(xyds[nrows + 1] + xz_below[k] + yz_row)
        feats.append(xyds[1 : nrows + 1, 0, :] + xzs[k] + yz_before)
        feats.append(xyds[1 : nrows + 1, ncols + 1, :] + xzs[k] + yz_after)
        feats.append(jnp.zeros((fill, width), F32))
    rim = decode(jnp.concatenate(feats, axis=0).astype(BF16), lab_rim.T[0:8])[-1]
    whole_span = span + fill
    rim_sum = rim[0:span]
    for k in range(1, depth):
        rim_sum = rim_sum + rim[k * whole_span : k * whole_span + span]
    rim_sum = rim_sum.astype(BF16).astype(F32)
    rcol = lax.broadcasted_iota(jnp.int32, (PITCH, width), 0)
    keep = (rcol >= jnp.where(open_left, 0, 1)) & (rcol < jnp.where(open_right, ncols + 2, ncols + 1))
    dx[0] = jnp.where(keep & open_up, rim_sum[0:PITCH], 0.0)
    dx[nrows + 1] = jnp.where(keep & open_down, rim_sum[PITCH : 2 * PITCH], 0.0)
    west = rim_sum[2 * PITCH : 2 * PITCH + nrows]
    east = rim_sum[2 * PITCH + nrows : span]
    dx[1 : nrows + 1, 0, :] = jnp.where(open_left, west, 0.0)
    dx[1 : nrows + 1, ncols + 1, :] = jnp.where(open_right, east, 0.0)

    def put(start, block):
        for half, index, row, offset, rows in shares.split(start, block.shape[0]):
            packed[half, index, row : row + rows, :] = block[offset : offset + rows]

    def weight_gradient(start, dout):
        grad = dot_tn(dout, patch[0 : nrows * ncols])
        for tap in range(9):
            put(start + tap * width, grad[:, tap * width : (tap + 1) * width].T)

    packed[...] = jnp.zeros_like(packed)

    n3 = gather(acts, 1, 1, nrows, ncols)
    dxyd = dx[1 : nrows + 1, 1 : ncols + 1, :].reshape(n3, width).astype(BF16)
    weight_gradient(shares.at["conv2"], dxyd)
    pair_rows(dx, back, das, nrows, ncols)
    da1 = das[...].reshape(n3, width)
    _, slope = silu_pair(hs[2 : nrows + 2, 2 : ncols + 2, :].reshape(n3, width))
    dh1 = (da1 * slope).astype(BF16)
    gather(xs, 2, 2, nrows, ncols)
    weight_gradient(shares.at["conv1"], dh1)

    for name, ref in (("w1", dw1), ("w2", dw2)):
        rows = ref.shape[0]
        for half in range(hidden // LANES):
            put(shares.at[name] + half * rows, ref[:, half * LANES : (half + 1) * LANES])
    for q in range(classes):
        where = packed.at[q // shares.chips, q % shares.chips]
        for half in range(hidden // LANES):
            row = shares.small + half
            where[row : row + 1, :] = dw3[q : q + 1, half * LANES : (half + 1) * LANES]
    time_row = jnp.sum(dh1.astype(F32), axis=0, keepdims=True)
    packed[classes // shares.chips, classes % shares.chips, shares.small : shares.small + 1, :] = time_row
    for k in range(depth):
        flat[pl.ds(k, ncols, stride=depth), :] = dyz[k]
    for half in range(2):
        for index in range(shares.yz_shares):
            begin = half * ncols * depth // 2 + index * shares.yz_rows
            packed[half, index, shares.yz : shares.yz + shares.yz_rows, :] = flat[begin : begin + shares.yz_rows]
    for k in range(depth):
        flat[pl.ds(k, nrows, stride=depth), :] = dxz[k]
    for index in range(shares.chips):
        begin = index * shares.xz_rows
        packed[core, index, shares.xz : shares.xz + shares.xz_rows, :] = flat[begin : begin + shares.xz_rows]
    plane, layer = place[6], place[7]
    for k in range(shares.planes):
        for t in range(shares.layers):
            index = (plane ^ k) * shares.layers + (layer ^ t)
            own_out[k, t] = packed[core, index].astype(BF16)
            other_out[k, t] = packed[1 - core, index].astype(BF16)


def core_kernel(own, other, *outs):
    for k, out in enumerate(outs):
        out[...] = (own[k].astype(F32) + other[k].astype(F32)).astype(BF16)


def plane_kernel(shares, *refs):
    blocks, outs = refs[: shares.planes], refs[shares.planes :]
    size = shares.yz_rows
    for t, out in enumerate(outs):
        got = [block[t].astype(F32) for block in blocks]
        total = sum(got[1:], got[0])
        pieces = [total[: shares.each]]
        for rank in range(shares.ranks):
            pair = got[2 * rank] + got[2 * rank + 1]
            pieces.append(pair[shares.xz : shares.small])
        pieces.append(total[shares.small : shares.yz])
        for column in range(2):
            part = sum(got[column + 2 :: 2], got[column])
            pieces.append(part[shares.yz : shares.yz + size])
        rest = shares.mid_rows - shares.mid_yz - 2 * size
        if rest:
            pieces.append(jnp.zeros((rest, LANES), F32))
        out[...] = jnp.concatenate(pieces, axis=0).astype(BF16)


def layer_kernel(shares, place, *refs):
    layers, size = shares.layers, shares.yz_rows
    blocks, outs = refs[:layers], refs[layers : 2 * layers]
    by_row, by_col, tail = refs[2 * layers :]
    plane, layer = place[6], place[7]
    rank, column = plane // 2, plane % 2
    got = [block[...].astype(F32) for block in blocks]
    total = sum(got[1:], got[0])
    for r in range(shares.ranks):
        begin = shares.xz + r * shares.xz_slot
        by_row[rank ^ r] = total[begin : begin + shares.xz_slot]
    for t in range(layers):
        for c in range(2):
            begin = shares.mid_yz + c * size
            by_col[2 * (layer ^ t) + (column ^ c), 0:size, :] = got[t][begin : begin + size]
    tail[...] = jnp.zeros_like(tail)
    tail[0:2, :] = total[shares.mid_small : shares.mid_yz]
    for j in range(2 * layers):
        tail[2 + j * size : 2 + (j + 1) * size, :] = by_col[j, 0:size, :]
    for t, out in enumerate(outs):
        pieces = [total[: shares.each], by_row[(layer ^ t) // 2], tail[...]]
        out[...] = jnp.concatenate(pieces, axis=0).astype(BF16)


def last_kernel(shares, classes, place, *refs):
    halves, refs = refs[: 2 * shares.planes], refs[2 * shares.planes :]
    emb, g1, g2, gt, gw1, gw2, gw3, gxz, gyz, whole, rest = refs
    each = shares.each
    width, hidden = emb.shape[0], gw2.shape[0]
    core, plane, layer = place[5], place[6], place[7]
    row_core, row_side, rank = place[8], place[0], place[9]
    for k in range(shares.planes):
        for t in range(shares.layers):
            index = (plane ^ k) * shares.layers + (layer ^ t)
            for half, block in ((core, halves[k]), (1 - core, halves[shares.planes + k])):
                value = block[t].astype(F32)
                whole[half, index] = value[0:each].astype(BF16)
                rest[half, index] = value[each:]

    def take(start, ref, lead, lanes):
        for side, index, row, offset, rows in shares.split(start, width if lead is not None else ref.shape[0]):
            block = whole[side, index, row : row + rows, :].astype(F32)
            if lead is not None:
                ref[lead, offset : offset + rows, :] = block
            else:
                ref[offset : offset + rows, lanes] = block

    for name, ref in (("conv1", g1), ("conv2", g2)):
        for tap in range(9):
            take(shares.at[name] + tap * width, ref, tap, None)
    for name, ref in (("w1", gw1), ("w2", gw2)):
        for part in range(hidden // LANES):
            take(shares.at[name] + part * ref.shape[0], ref, None, slice(part * LANES, (part + 1) * LANES))
    at_small, at_yz = shares.small - each, shares.yz - each
    gt[...] = emb[...] * rest[classes // shares.chips, classes % shares.chips, at_small : at_small + 1, :]
    for q in range(classes):
        for part in range(hidden // LANES):
            value = rest[q // shares.chips, q % shares.chips, at_small + part : at_small + part + 1, :]
            gw3[q : q + 1, part * LANES : (part + 1) * LANES] = value
    count = gxz.shape[0]
    begin = pl.multiple_of(row_side * count, count)
    gxz[...] = rest[row_core, pl.ds(begin, count), 0 : shares.xz_rows, :]
    size, per = shares.yz_rows, shares.yz_rows * shares.yz_shares
    for r in range(2):
        for side in range(2):
            for index in range(shares.yz_shares):
                to = (2 * r + side) * per + index * size
                value = rest[side, index, at_yz + r * size : at_yz + (r + 1) * size, :]
                for i in range(1, shares.planes):
                    begin = at_yz + (2 * i + r) * size
                    value = jnp.where(rank == i, rest[side, index, begin : begin + size, :], value)
                gyz[to : to + size, :] = value


def local(
    xy_noisy,
    xz_plane,
    yz_plane,
    labels,
    timestep,
    conv1_weight,
    conv2_weight,
    time_weight,
    w1,
    w2,
    w3,
):
    grid = Grid()
    nrows, ncols, width = xy_noisy.shape
    depth = labels.shape[2]
    hidden, classes = w3.shape
    count = grid.count
    side = grid.iy % count
    flat_one = conv1_weight.reshape(9 * width, width)
    flat_two = conv2_weight.reshape(9 * width, width)

    up = lambda i, j: (i + 1, j)
    down = lambda i, j: (i - 1, j)
    left = lambda i, j: (i, j - 1)
    right = lambda i, j: (i, j + 1)

    def lab(part):
        return jnp.pad(part.astype(BF16), ((0, 0), (0, 0), (0, LANES - depth)))

    slab_count = xz_plane.shape[1] // depth
    start = timestep[0] % slab_count * depth
    xz_local = lax.dynamic_slice_in_dim(xz_plane, start, depth, 1)
    share = xz_local.shape[0]
    yz_half = lax.dynamic_slice(yz_plane, (side * ncols, start, 0), (ncols, depth, width))
    first = grid.move(jnp.concatenate([yz_half, xz_local], axis=0), grid.turned(0))

    def row(features, labels_row, edge):
        edge = jnp.pad(edge[None], ((0, 0), (0, ncols - depth), (0, 0)))
        return jnp.concatenate([features, lab(labels_row), edge])

    above = grid.move(row(xy_noisy[nrows - REACH :], labels[nrows - 1 :], first[ncols + share - 1]), up)
    below = grid.move(row(xy_noisy[:REACH], labels[:1], first[ncols]), down)
    above, late_conv2, late_time, late_w3, late_labels, late_step = lax.optimization_barrier(
        (above, conv2_weight, time_weight, w3, labels, timestep)
    )
    edge_row = jnp.where(side == 0, below[4:, :depth], above[4:, :depth])

    def column(at, where):
        cols = jnp.concatenate(
            [above[:REACH, where], xy_noisy[:, where], below[:REACH, where]], axis=0
        )
        yz = first[at].reshape(depth, 1, width)
        extra = jnp.concatenate(
            [yz[:2], above[3:4, at : at + 1], lab(labels[:, at : at + 1]), below[3:4, at : at + 1], yz[2:]],
            axis=0,
        )
        return jnp.concatenate([jnp.concatenate([cols, extra], axis=1), first[ncols:], edge_row], axis=0)

    before = grid.move(column(ncols - 1, slice(ncols - REACH, ncols)), right)
    after = grid.move(column(0, slice(0, REACH)), left)

    emb = time_embedding(late_step, width)
    temb = jnp.dot(emb, late_time.astype(F32), precision=lax.Precision.HIGHEST)
    back_flat = jnp.transpose(late_conv2[::-1, ::-1], (0, 1, 3, 2)).reshape(9 * width, width)
    w3_wide = jnp.stack(
        [jnp.pad(late_w3, ((0, 0), (CLASS_ROWS * k, LANES - classes - CLASS_ROWS * k))) for k in range(depth)]
    )
    chunks = nrows // 16
    labels_by_depth = late_labels.astype(F32).reshape(chunks, -1, depth).transpose(0, 2, 1)

    core = grid.ix % 2
    flags = jnp.stack(
        [
            side,
            grid.ix,
            grid.nx - 1 - grid.ix,
            grid.iy,
            grid.ny - 1 - grid.iy,
            core,
            grid.ix // 2 * 2 + grid.iy % 2,
            grid.iy // 2,
            grid.iy // count % 2,
            grid.ix,
        ]
    ).astype(jnp.int32)
    shares = Shares(grid.nx, grid.ny, nrows, ncols, depth, width, hidden)
    planes, layers, chips = shares.planes, shares.layers, shares.chips
    vmem = pl.BlockSpec(memory_space=pltpu.VMEM)
    smem = pl.BlockSpec(memory_space=pltpu.SMEM)
    params = pltpu.CompilerParams(vmem_limit_bytes=VMEM_LIMIT)
    buffer = jax.ShapeDtypeStruct((planes, layers, shares.rows, LANES), BF16)
    own, other = pl.pallas_call(
        functools.partial(main_kernel, classes, shares),
        out_shape=(buffer, buffer),
        in_specs=[smem] + [vmem] * 14,
        out_specs=(vmem, vmem),
        scratch_shapes=[
            pltpu.VMEM((nrows + 6, 32, width), F32),
            pltpu.VMEM((nrows + 4, PITCH, width), F32),
            pltpu.VMEM((nrows + 4, 32, width), F32),
            pltpu.VMEM((nrows + 2, PITCH, width), F32),
            pltpu.VMEM((nrows + 2, PITCH, width), F32),
            pltpu.VMEM((nrows, ncols, width), F32),
            pltpu.VMEM((12 * width, 2 * width), BF16),
            pltpu.VMEM((nrows * ncols, 12 * width), BF16),
            pltpu.VMEM((depth, nrows, width), F32),
            pltpu.VMEM((depth, ncols, width), F32),
            pltpu.VMEM((width, hidden), F32),
            pltpu.VMEM((hidden, hidden), F32),
            pltpu.VMEM((CLASS_ROWS, hidden), F32),
            pltpu.VMEM((depth, nrows, width), F32),
            pltpu.VMEM((depth, ncols, width), F32),
            pltpu.VMEM((nrows * depth, width), F32),
            pltpu.VMEM((2, chips, shares.rows, LANES), F32),
        ],
        compiler_params=params,
        name="tile",
    )(
        flags,
        xy_noisy,
        above,
        below,
        before,
        after,
        labels_by_depth,
        first,
        temb.reshape(1, width),
        flat_one,
        flat_two,
        back_flat,
        w1,
        w2,
        w3_wide,
    )

    swap = lambda i, j: (i ^ 1, j)
    in_plane = lambda k: lambda i, j: (i ^ (k // 2 * 2), j ^ (k % 2))
    in_layer = lambda t: lambda i, j: (i, j ^ (2 * t))

    def kernel(body, count_in, shape, count_out, name, scratch=(), scalars=False):
        return pl.pallas_call(
            body,
            out_shape=(jax.ShapeDtypeStruct(shape, BF16),) * count_out,
            in_specs=[smem] * scalars + [vmem] * count_in,
            out_specs=(vmem,) * count_out,
            scratch_shapes=list(scratch),
            compiler_params=params,
            name=name,
        )

    swapped = grid.move(other, swap)
    blocks = kernel(core_kernel, 2, (layers, shares.rows, LANES), planes, "cores")(own, swapped)
    blocks = [blocks[0]] + [grid.move(blocks[k], in_plane(k)) for k in range(1, planes)]
    body = functools.partial(plane_kernel, shares)
    blocks = kernel(body, planes, (shares.mid_rows, LANES), layers, "planes")(*blocks)
    blocks = [blocks[0]] + [grid.move(blocks[t], in_layer(t)) for t in range(1, layers)]
    scratch = (
        pltpu.VMEM((shares.ranks, shares.xz_slot, LANES), F32),
        pltpu.VMEM((grid.ny, 8, LANES), F32),
        pltpu.VMEM((shares.end_rows - shares.small, LANES), F32),
    )
    body = functools.partial(layer_kernel, shares)
    blocks = kernel(body, layers, (shares.end_rows, LANES), layers, "layers", scratch, True)(flags, *blocks)
    blocks = [blocks[0]] + [grid.move(blocks[t], in_layer(t)) for t in range(1, layers)]
    mine = jnp.stack(blocks)
    halves = [mine] + [grid.move(mine, in_plane(k)) for k in range(1, planes)]
    halves = halves + [grid.move(half, swap) for half in halves]
    g1, g2, gt, gw1, gw2, gw3, gxz, gyz = pl.pallas_call(
        functools.partial(last_kernel, shares, classes),
        out_shape=(
            jax.ShapeDtypeStruct((9, width, width), F32),
            jax.ShapeDtypeStruct((9, width, width), F32),
            jax.ShapeDtypeStruct((width, width), F32),
            jax.ShapeDtypeStruct((width, hidden), F32),
            jax.ShapeDtypeStruct((hidden, hidden), F32),
            jax.ShapeDtypeStruct((classes, hidden), F32),
            jax.ShapeDtypeStruct((chips // 2, shares.xz_rows, width), F32),
            jax.ShapeDtypeStruct((2 * ncols * depth, width), F32),
        ),
        in_specs=[smem] + [vmem] * (2 * planes + 1),
        out_specs=(vmem,) * 8,
        scratch_shapes=[
            pltpu.VMEM((2, chips, shares.each, LANES), BF16),
            pltpu.VMEM((2, chips, shares.end_rows - shares.each, LANES), F32),
        ],
        compiler_params=params,
        name="spread",
    )(
        flags,
        *halves,
        emb.reshape(width, 1),
    )
    shape = (3, 3, width, width)
    return (
        g1.reshape(shape),
        g2.reshape(shape),
        gt,
        gw1,
        gw2,
        gw3.T,
        gxz.reshape(share, depth, width),
        gyz.reshape(2 * ncols, depth, width),
    )


def solution(mesh):
    placed = (
        P("gx", "gy", None),
        P("gy", None, None),
        P("gx", None, None),
        P("gx", "gy", None),
        P(),
        P(),
        P(),
        P(),
        P(),
        P(),
        P(),
    )
    return jax.shard_map(
        local,
        mesh=mesh,
        in_specs=placed,
        out_specs=(P(), P(), P(), P(), P(), P(), P("gy", None, None), P("gx", None, None)),
        check_vma=False,
    )
```

```python
import functools
import math

import jax
import jax.numpy as jnp
from jax import lax
from jax.experimental import pallas as pl
from jax.experimental.pallas import tpu as pltpu
from jax.sharding import PartitionSpec as P

loss_weight = 1.0 / 256.0
BOTH = ("gx", "gy")
LANES = 128
PITCH = 24
REACH = 3
CLASS_ROWS = 32
F32, BF16 = jnp.float32, jnp.bfloat16
VMEM_LIMIT = 48 * 1024 * 1024


def sigmoid(value):
    return 0.5 * jnp.tanh(0.5 * value) + 0.5


def silu_pair(value):
    sig = sigmoid(value)
    out = value * sig
    return out, sig + out - out * sig


def dot(a, b):
    return jnp.dot(a, b, preferred_element_type=F32)


def dot_nt(a, b):
    return lax.dot_general(a, b, (((1,), (1,)), ((), ())), preferred_element_type=F32)


def dot_tn(a, b):
    return lax.dot_general(a, b, (((0,), (0,)), ((), ())), preferred_element_type=F32)


def time_embedding(timestep, width):
    half = width // 2
    freqs = jnp.exp(-math.log(10000.0) * jnp.arange(half, dtype=jnp.float32) / half)
    angle = timestep.astype(jnp.float32)[0] * freqs
    return jnp.concatenate([jnp.cos(angle), jnp.sin(angle)])


class Grid:
    def __init__(self):
        self.nx, self.ny = lax.axis_size("gx"), lax.axis_size("gy")
        self.count = self.ny // self.nx
        self.ix, self.iy = lax.axis_index("gx"), lax.axis_index("gy")

    def move(self, array, target):
        pairs = []
        for i in range(self.nx):
            for j in range(self.ny):
                k, m = target(i, j)
                if 0 <= k < self.nx and 0 <= m < self.ny:
                    pairs.append((i * self.ny + j, k * self.ny + m))
        return lax.ppermute(array, BOTH, pairs)

    def turned(self, shift):
        count = self.count
        return lambda i, j: (j // count, count * i + (j % count + shift) % count)


class Shares:
    def __init__(self, nx, ny, nrows, ncols, depth, width, hidden):
        sizes = (("conv1", 9 * width), ("conv2", 9 * width), ("w1", width * hidden // LANES), ("w2", hidden * hidden // LANES))
        self.at, total = {}, 0
        for name, rows in sizes:
            self.at[name] = total
            total += rows
        self.chips = chips = nx * ny // 2
        self.ranks, self.planes, self.layers = nx // 2, nx, ny // 2
        self.each = -(-total // (2 * chips * 8)) * 8
        self.xz_rows = nrows * depth // chips
        self.yz_rows = max(1, ncols * depth // 2 // chips)
        self.yz_shares = ncols * depth // 2 // self.yz_rows
        self.xz_slot = -(-self.xz_rows // 8) * 8
        even = lambda rows: -(-rows // 8) * 8
        self.xz = self.each
        self.small = self.xz + self.xz_slot
        self.yz = self.small + 2
        self.rows = even(self.yz + self.yz_rows)
        self.mid_small = self.xz + self.ranks * self.xz_slot
        self.mid_yz = self.mid_small + 2
        self.mid_rows = even(self.mid_yz + 2 * self.yz_rows)
        self.end_rows = even(self.yz + ny * self.yz_rows)

    def split(self, start, rows):
        done = 0
        while done < rows:
            share, row = divmod(start + done, self.each)
            step = min(rows - done, self.each - row)
            yield share // self.chips, share % self.chips, row, done, step
            done += step


def main_kernel(
    classes,
    shares,
    place,
    xy,
    above,
    below,
    before,
    after,
    labels,
    first,
    temb,
    conv1,
    conv2,
    back,
    w1,
    w2,
    w3,
    own_out,
    other_out,
    xs,
    hs,
    acts,
    xyds,
    dx,
    das,
    paired,
    patch,
    xzs,
    yzs,
    dw1,
    dw2,
    dw3,
    dxz,
    dyz,
    flat,
    packed,
):
    nrows, ncols, width = xy.shape
    depth = labels.shape[1]
    hidden = w1.shape[1]
    share = nrows // 2
    side, core = place[0], place[5]
    open_up, open_down, open_left, open_right = (place[1] > 0, place[2] > 0, place[3] > 0, place[4] > 0)
    tall = nrows + 2 * REACH

    mid_r, mid_c = slice(REACH, REACH + nrows), slice(REACH, REACH + ncols)
    xs[...] = jnp.zeros_like(xs)
    xs[mid_r, mid_c] = xy[...].astype(F32)
    xs[0:REACH, mid_c] = above[0:REACH].astype(F32)
    xs[REACH + nrows : 2 * REACH + nrows, mid_c] = below[0:REACH].astype(F32)
    xs[:, 0:REACH] = before[0:tall].astype(F32)[:, 0:REACH]
    xs[:, REACH + ncols : 2 * REACH + ncols] = after[0:tall].astype(F32)[:, 0:REACH]

    def gather(source, row, col, rows, cols):
        count = rows * cols
        for a in range(3):
            for b in range(3):
                piece = source[row + a : row + a + rows, col + b : col + b + cols, :]
                tap = (3 * a + b) * width
                patch[0:count, tap : tap + width] = piece.reshape(count, width).astype(BF16)
        return count

    def pair_rows(source, weight, out, rows, cols):
        span, inner = 3 * width, rows // 2
        count = inner * cols
        paired[0 : 3 * span, 0:width] = weight[...]
        paired[3 * span : 4 * span, 0:width] = jnp.zeros((span, width), BF16)
        paired[0:span, width : 2 * width] = jnp.zeros((span, width), BF16)
        paired[span : 4 * span, width : 2 * width] = weight[...]
        for a in range(4):
            for b in range(3):
                piece = source[pl.ds(a, inner, stride=2), b : b + cols, :]
                tap = (3 * a + b) * width
                patch[0:count, tap : tap + width] = piece.reshape(count, width).astype(BF16)
        both = dot(patch[0:count, 0 : 4 * span], paired[...])
        out[pl.ds(0, inner, stride=2)] = both[:, 0:width].reshape(inner, cols, width)
        out[pl.ds(1, inner, stride=2)] = both[:, width : 2 * width].reshape(inner, cols, width)

    pair_rows(xs, conv1, hs, nrows + 4, PITCH)
    h1 = hs[...] + temb[...][None]
    hs[...] = h1
    row = lax.broadcasted_iota(jnp.int32, h1.shape, 0)
    col = lax.broadcasted_iota(jnp.int32, h1.shape, 1)
    low_r = jnp.where(open_up, 0, 2)
    high_r = jnp.where(open_down, nrows + 4, nrows + 2)
    low_c = jnp.where(open_left, 0, 2)
    high_c = jnp.where(open_right, ncols + 4, ncols + 2)
    inside = (row >= low_r) & (row < high_r) & (col >= low_c) & (col < high_c)
    a1 = jnp.where(inside, h1 * sigmoid(h1), 0.0)
    acts[...] = jnp.zeros_like(acts)
    acts[:, 0:PITCH] = a1.astype(BF16).astype(F32)
    pair_rows(acts, conv2, xyds, nrows + 2, PITCH)
    xyds[...] = xyds[...].astype(BF16).astype(F32)

    rows_before = before[tall : tall + share + 1].astype(F32)
    rows_after = after[tall : tall + share + 1].astype(F32)
    mine = first[...].astype(F32)
    edge_above, edge_below = above[4].astype(F32), below[4].astype(F32)
    same_at = pl.ds(pl.multiple_of(side * share, share), share)
    second_at = pl.ds(pl.multiple_of((1 - side) * share, share), share)
    xz_above, xz_below = [], []
    for k in range(depth):
        second = jnp.where(side == 0, rows_after[:, k, :], rows_before[:, k, :])
        yzs[k] = mine[0:ncols, k, :]
        xzs[k, same_at, :] = mine[ncols:, k, :]
        xzs[k, second_at, :] = second[0:share]
        xz_above.append(jnp.where(side == 0, second[share:], edge_above[k : k + 1]))
        xz_below.append(jnp.where(side == 0, edge_below[k : k + 1], second[share:]))

    def decode(feat, label):
        pixels = feat.shape[0] // depth
        u1 = dot(feat, w1[...])
        g1, s1 = silu_pair(u1)
        g1 = g1.astype(BF16)
        u2 = dot(g1, w2[...])
        g2, s2 = silu_pair(u2)
        g2 = g2.astype(BF16)
        logits = dot(g2[0:pixels], w3[0])
        for k in range(1, depth):
            logits = logits + dot(g2[k * pixels : (k + 1) * pixels], w3[k])
        turned = logits.T
        outs = []
        for k in range(depth):
            part = turned[k * CLASS_ROWS : (k + 1) * CLASS_ROWS]
            lane = lax.broadcasted_iota(jnp.int32, part.shape, 0)
            part = jnp.where(lane < classes, part, -jnp.inf)
            power = jnp.exp(part - jnp.max(part, axis=0, keepdims=True))
            prob = power / jnp.sum(power, axis=0, keepdims=True)
            onehot = jnp.where(lane.astype(F32) == label[k : k + 1], 1.0, 0.0)
            outs.append(loss_weight * (prob - onehot))
        turned = jnp.concatenate(outs, axis=0)
        dlogits = turned.T.astype(BF16)
        dg2 = jnp.concatenate([dot_nt(dlogits, w3[k]) for k in range(depth)], axis=0)
        du2 = (dg2 * s2).astype(BF16)
        du1 = (dot_nt(du2, w2[...]) * s1).astype(BF16)
        return g1, g2, turned.astype(BF16), du2, du1, dot_nt(du1, w1[...])

    dw1[...] = jnp.zeros_like(dw1)
    dw2[...] = jnp.zeros_like(dw2)
    dw3[...] = jnp.zeros_like(dw3)
    dyz[...] = jnp.zeros_like(dyz)
    dx[...] = jnp.zeros_like(dx)
    chunk = nrows // labels.shape[0]
    size = chunk * ncols

    def step(index, carry):
        r0 = pl.multiple_of(index * chunk, chunk)
        tile = xyds[pl.ds(r0 + 1, chunk), 1 : ncols + 1, :]
        feats = []
        for k in range(depth):
            xz_k = xzs[k, pl.ds(r0, chunk), :]
            feat = tile + xz_k[:, None, :] + yzs[k][None]
            feats.append(feat.reshape(size, width).astype(BF16))
        feat = jnp.concatenate(feats, axis=0)
        g1, g2, dlogits, du2, du1, dfeat = decode(feat, labels[index])
        for k in range(depth):
            dw3[...] += dot(dlogits[k * CLASS_ROWS : (k + 1) * CLASS_ROWS], g2[k * size : (k + 1) * size])
        dw2[...] += dot_tn(g1, du2)
        dw1[...] += dot_tn(feat, du1)
        total = jnp.zeros((chunk, ncols, width), F32)
        for k in range(depth):
            piece = dfeat[k * size : (k + 1) * size].reshape(chunk, ncols, width)
            total = total + piece
            dxz[k, pl.ds(r0, chunk), :] = jnp.sum(piece, axis=1)
            dyz[k] += jnp.sum(piece, axis=0)
        dx[pl.ds(r0 + 1, chunk), 1 : ncols + 1, :] = total.astype(BF16).astype(F32)
        return carry

    lax.fori_loop(0, nrows // chunk, step, 0, unroll=True)

    lab_before = before[2 : nrows + 4, 3, :].astype(F32)
    lab_after = after[2 : nrows + 4, 3, :].astype(F32)
    lab_up = above[3].astype(F32)
    lab_down = below[3].astype(F32)
    tail = jnp.zeros((PITCH - ncols - 2, LANES), F32)
    span = 2 * PITCH + 2 * nrows
    fill = -span % LANES
    lab_rim = jnp.concatenate(
        [
            lab_before[0:1],
            lab_up,
            lab_after[0:1],
            tail,
            lab_before[nrows + 1 : nrows + 2],
            lab_down,
            lab_after[nrows + 1 : nrows + 2],
            tail,
            lab_before[1 : nrows + 1],
            lab_after[1 : nrows + 1],
            jnp.zeros((fill, LANES), F32),
        ],
        axis=0,
    )
    rim_at = (0, 1, nrows + 2 * REACH - 2, nrows + 2 * REACH - 1)
    feats = []
    zero_tail = jnp.zeros((PITCH - ncols - 2, width), F32)
    for k in range(depth):
        yz_before = before[rim_at[k], 3:4, :].astype(F32)
        yz_after = after[rim_at[k], 3:4, :].astype(F32)
        yz_row = jnp.concatenate([yz_before, yzs[k], yz_after, zero_tail], axis=0)
        feats.append(xyds[0] + xz_above[k] + yz_row)
        feats.append(xyds[nrows + 1] + xz_below[k] + yz_row)
        feats.append(xyds[1 : nrows + 1, 0, :] + xzs[k] + yz_before)
        feats.append(xyds[1 : nrows + 1, ncols + 1, :] + xzs[k] + yz_after)
        feats.append(jnp.zeros((fill, width), F32))
    rim = decode(jnp.concatenate(feats, axis=0).astype(BF16), lab_rim.T[0:8])[-1]
    whole_span = span + fill
    rim_sum = rim[0:span]
    for k in range(1, depth):
        rim_sum = rim_sum + rim[k * whole_span : k * whole_span + span]
    rim_sum = rim_sum.astype(BF16).astype(F32)
    rcol = lax.broadcasted_iota(jnp.int32, (PITCH, width), 0)
    keep = (rcol >= jnp.where(open_left, 0, 1)) & (rcol < jnp.where(open_right, ncols + 2, ncols + 1))
    dx[0] = jnp.where(keep & open_up, rim_sum[0:PITCH], 0.0)
    dx[nrows + 1] = jnp.where(keep & open_down, rim_sum[PITCH : 2 * PITCH], 0.0)
    west = rim_sum[2 * PITCH : 2 * PITCH + nrows]
    east = rim_sum[2 * PITCH + nrows : span]
    dx[1 : nrows + 1, 0, :] = jnp.where(open_left, west, 0.0)
    dx[1 : nrows + 1, ncols + 1, :] = jnp.where(open_right, east, 0.0)

    def put(start, block):
        for half, index, row, offset, rows in shares.split(start, block.shape[0]):
            packed[half, index, row : row + rows, :] = block[offset : offset + rows]

    def weight_gradient(start, dout):
        put(start, dot_tn(patch[0 : nrows * ncols, 0 : 9 * width], dout))

    packed[...] = jnp.zeros_like(packed)

    n3 = gather(acts, 1, 1, nrows, ncols)
    dxyd = dx[1 : nrows + 1, 1 : ncols + 1, :].reshape(n3, width).astype(BF16)
    weight_gradient(shares.at["conv2"], dxyd)
    pair_rows(dx, back, das, nrows, ncols)
    da1 = das[...].reshape(n3, width)
    _, slope = silu_pair(hs[2 : nrows + 2, 2 : ncols + 2, :].reshape(n3, width))
    dh1 = (da1 * slope).astype(BF16)
    gather(xs, 2, 2, nrows, ncols)
    weight_gradient(shares.at["conv1"], dh1)

    for name, ref in (("w1", dw1), ("w2", dw2)):
        rows = ref.shape[0]
        for half in range(hidden // LANES):
            put(shares.at[name] + half * rows, ref[:, half * LANES : (half + 1) * LANES])
    for q in range(classes):
        where = packed.at[q // shares.chips, q % shares.chips]
        for half in range(hidden // LANES):
            row = shares.small + half
            where[row : row + 1, :] = dw3[q : q + 1, half * LANES : (half + 1) * LANES]
    time_row = jnp.sum(dh1.astype(F32), axis=0, keepdims=True)
    packed[classes // shares.chips, classes % shares.chips, shares.small : shares.small + 1, :] = time_row
    for k in range(depth):
        flat[pl.ds(k, ncols, stride=depth), :] = dyz[k]
    for half in range(2):
        for index in range(shares.yz_shares):
            begin = half * ncols * depth // 2 + index * shares.yz_rows
            packed[half, index, shares.yz : shares.yz + shares.yz_rows, :] = flat[begin : begin + shares.yz_rows]
    for k in range(depth):
        flat[pl.ds(k, nrows, stride=depth), :] = dxz[k]
    for index in range(shares.chips):
        begin = index * shares.xz_rows
        packed[core, index, shares.xz : shares.xz + shares.xz_rows, :] = flat[begin : begin + shares.xz_rows]
    plane, layer = place[6], place[7]
    for k in range(shares.planes):
        for t in range(shares.layers):
            index = (plane ^ k) * shares.layers + (layer ^ t)
            own_out[k, t] = packed[core, index].astype(BF16)
            other_out[k, t] = packed[1 - core, index].astype(BF16)


def core_kernel(own, other, *outs):
    for k, out in enumerate(outs):
        out[...] = (own[k].astype(F32) + other[k].astype(F32)).astype(BF16)


def plane_kernel(shares, *refs):
    blocks, outs = refs[: shares.planes], refs[shares.planes :]
    size = shares.yz_rows
    for t, out in enumerate(outs):
        got = [block[t].astype(F32) for block in blocks]
        total = sum(got[1:], got[0])
        pieces = [total[: shares.each]]
        for rank in range(shares.ranks):
            pair = got[2 * rank] + got[2 * rank + 1]
            pieces.append(pair[shares.xz : shares.small])
        pieces.append(total[shares.small : shares.yz])
        for column in range(2):
            part = sum(got[column + 2 :: 2], got[column])
            pieces.append(part[shares.yz : shares.yz + size])
        rest = shares.mid_rows - shares.mid_yz - 2 * size
        if rest:
            pieces.append(jnp.zeros((rest, LANES), F32))
        out[...] = jnp.concatenate(pieces, axis=0).astype(BF16)


def layer_kernel(shares, place, *refs):
    layers, size = shares.layers, shares.yz_rows
    blocks, outs = refs[:layers], refs[layers : 2 * layers]
    by_row, by_col, tail = refs[2 * layers :]
    plane, layer = place[6], place[7]
    rank, column = plane // 2, plane % 2
    got = [block[...].astype(F32) for block in blocks]
    total = sum(got[1:], got[0])
    for r in range(shares.ranks):
        begin = shares.xz + r * shares.xz_slot
        by_row[rank ^ r] = total[begin : begin + shares.xz_slot]
    for t in range(layers):
        for c in range(2):
            begin = shares.mid_yz + c * size
            by_col[2 * (layer ^ t) + (column ^ c), 0:size, :] = got[t][begin : begin + size]
    tail[...] = jnp.zeros_like(tail)
    tail[0:2, :] = total[shares.mid_small : shares.mid_yz]
    for j in range(2 * layers):
        tail[2 + j * size : 2 + (j + 1) * size, :] = by_col[j, 0:size, :]
    for t, out in enumerate(outs):
        pieces = [total[: shares.each], by_row[(layer ^ t) // 2], tail[...]]
        out[...] = jnp.concatenate(pieces, axis=0).astype(BF16)


def last_kernel(shares, classes, place, *refs):
    halves, refs = refs[: 2 * shares.planes], refs[2 * shares.planes :]
    emb, g1, g2, gt, gw1, gw2, gw3, gxz, gyz, whole, rest = refs
    each = shares.each
    width, hidden = emb.shape[0], gw2.shape[0]
    core, plane, layer = place[5], place[6], place[7]
    row_core, row_side, rank = place[8], place[0], place[9]
    for k in range(shares.planes):
        for t in range(shares.layers):
            index = (plane ^ k) * shares.layers + (layer ^ t)
            for half, block in ((core, halves[k]), (1 - core, halves[shares.planes + k])):
                value = block[t].astype(F32)
                whole[half, index] = value[0:each].astype(BF16)
                rest[half, index] = value[each:]

    def take(start, ref, lead, lanes):
        for side, index, row, offset, rows in shares.split(start, width if lead is not None else ref.shape[0]):
            block = whole[side, index, row : row + rows, :].astype(F32)
            if lead is not None:
                ref[lead, offset : offset + rows, :] = block
            else:
                ref[offset : offset + rows, lanes] = block

    for name, ref in (("conv1", g1), ("conv2", g2)):
        for tap in range(9):
            take(shares.at[name] + tap * width, ref, tap, None)
    for name, ref in (("w1", gw1), ("w2", gw2)):
        for part in range(hidden // LANES):
            take(shares.at[name] + part * ref.shape[0], ref, None, slice(part * LANES, (part + 1) * LANES))
    at_small, at_yz = shares.small - each, shares.yz - each
    gt[...] = emb[...] * rest[classes // shares.chips, classes % shares.chips, at_small : at_small + 1, :]
    for q in range(classes):
        for part in range(hidden // LANES):
            value = rest[q // shares.chips, q % shares.chips, at_small + part : at_small + part + 1, :]
            gw3[q : q + 1, part * LANES : (part + 1) * LANES] = value
    count = gxz.shape[0]
    begin = pl.multiple_of(row_side * count, count)
    gxz[...] = rest[row_core, pl.ds(begin, count), 0 : shares.xz_rows, :]
    size, per = shares.yz_rows, shares.yz_rows * shares.yz_shares
    for r in range(2):
        for side in range(2):
            for index in range(shares.yz_shares):
                to = (2 * r + side) * per + index * size
                value = rest[side, index, at_yz + r * size : at_yz + (r + 1) * size, :]
                for i in range(1, shares.planes):
                    begin = at_yz + (2 * i + r) * size
                    value = jnp.where(rank == i, rest[side, index, begin : begin + size, :], value)
                gyz[to : to + size, :] = value


def local(
    xy_noisy,
    xz_plane,
    yz_plane,
    labels,
    timestep,
    conv1_weight,
    conv2_weight,
    time_weight,
    w1,
    w2,
    w3,
):
    grid = Grid()
    nrows, ncols, width = xy_noisy.shape
    depth = labels.shape[2]
    hidden, classes = w3.shape
    count = grid.count
    side = grid.iy % count
    flat_one = conv1_weight.reshape(9 * width, width)
    flat_two = conv2_weight.reshape(9 * width, width)

    up = lambda i, j: (i + 1, j)
    down = lambda i, j: (i - 1, j)
    left = lambda i, j: (i, j - 1)
    right = lambda i, j: (i, j + 1)

    def lab(part):
        return jnp.pad(part.astype(BF16), ((0, 0), (0, 0), (0, LANES - depth)))

    slab_count = xz_plane.shape[1] // depth
    start = timestep[0] % slab_count * depth
    xz_local = lax.dynamic_slice_in_dim(xz_plane, start, depth, 1)
    share = xz_local.shape[0]
    yz_half = lax.dynamic_slice(yz_plane, (side * ncols, start, 0), (ncols, depth, width))
    first = grid.move(jnp.concatenate([yz_half, xz_local], axis=0), grid.turned(0))

    def row(features, labels_row, edge):
        edge = jnp.pad(edge[None], ((0, 0), (0, ncols - depth), (0, 0)))
        return jnp.concatenate([features, lab(labels_row), edge])

    above = grid.move(row(xy_noisy[nrows - REACH :], labels[nrows - 1 :], first[ncols + share - 1]), up)
    below = grid.move(row(xy_noisy[:REACH], labels[:1], first[ncols]), down)
    above, late_conv2, late_time, late_w3, late_labels, late_step = lax.optimization_barrier(
        (above, conv2_weight, time_weight, w3, labels, timestep)
    )
    edge_row = jnp.where(side == 0, below[4:, :depth], above[4:, :depth])

    def column(at, where):
        cols = jnp.concatenate(
            [above[:REACH, where], xy_noisy[:, where], below[:REACH, where]], axis=0
        )
        yz = first[at].reshape(depth, 1, width)
        extra = jnp.concatenate(
            [yz[:2], above[3:4, at : at + 1], lab(labels[:, at : at + 1]), below[3:4, at : at + 1], yz[2:]],
            axis=0,
        )
        return jnp.concatenate([jnp.concatenate([cols, extra], axis=1), first[ncols:], edge_row], axis=0)

    before = grid.move(column(ncols - 1, slice(ncols - REACH, ncols)), right)
    after = grid.move(column(0, slice(0, REACH)), left)

    emb = time_embedding(late_step, width)
    temb = jnp.dot(emb, late_time.astype(F32), precision=lax.Precision.HIGHEST)
    back_flat = jnp.transpose(late_conv2[::-1, ::-1], (0, 1, 3, 2)).reshape(9 * width, width)
    w3_wide = jnp.stack(
        [jnp.pad(late_w3, ((0, 0), (CLASS_ROWS * k, LANES - classes - CLASS_ROWS * k))) for k in range(depth)]
    )
    chunks = nrows // 32
    labels_by_depth = late_labels.astype(F32).reshape(chunks, -1, depth).transpose(0, 2, 1)

    core = grid.ix % 2
    flags = jnp.stack(
        [
            side,
            grid.ix,
            grid.nx - 1 - grid.ix,
            grid.iy,
            grid.ny - 1 - grid.iy,
            core,
            grid.ix // 2 * 2 + grid.iy % 2,
            grid.iy // 2,
            grid.iy // count % 2,
            grid.ix,
        ]
    ).astype(jnp.int32)
    shares = Shares(grid.nx, grid.ny, nrows, ncols, depth, width, hidden)
    planes, layers, chips = shares.planes, shares.layers, shares.chips
    vmem = pl.BlockSpec(memory_space=pltpu.VMEM)
    smem = pl.BlockSpec(memory_space=pltpu.SMEM)
    params = pltpu.CompilerParams(vmem_limit_bytes=VMEM_LIMIT)
    buffer = jax.ShapeDtypeStruct((planes, layers, shares.rows, LANES), BF16)
    own, other = pl.pallas_call(
        functools.partial(main_kernel, classes, shares),
        out_shape=(buffer, buffer),
        in_specs=[smem] + [vmem] * 14,
        out_specs=(vmem, vmem),
        scratch_shapes=[
            pltpu.VMEM((nrows + 6, 32, width), F32),
            pltpu.VMEM((nrows + 4, PITCH, width), F32),
            pltpu.VMEM((nrows + 4, 32, width), F32),
            pltpu.VMEM((nrows + 2, PITCH, width), F32),
            pltpu.VMEM((nrows + 2, PITCH, width), F32),
            pltpu.VMEM((nrows, ncols, width), F32),
            pltpu.VMEM((12 * width, 2 * width), BF16),
            pltpu.VMEM((nrows * ncols, 12 * width), BF16),
            pltpu.VMEM((depth, nrows, width), F32),
            pltpu.VMEM((depth, ncols, width), F32),
            pltpu.VMEM((width, hidden), F32),
            pltpu.VMEM((hidden, hidden), F32),
            pltpu.VMEM((CLASS_ROWS, hidden), F32),
            pltpu.VMEM((depth, nrows, width), F32),
            pltpu.VMEM((depth, ncols, width), F32),
            pltpu.VMEM((nrows * depth, width), F32),
            pltpu.VMEM((2, chips, shares.rows, LANES), F32),
        ],
        compiler_params=params,
        name="tile",
    )(
        flags,
        xy_noisy,
        above,
        below,
        before,
        after,
        labels_by_depth,
        first,
        temb.reshape(1, width),
        flat_one,
        flat_two,
        back_flat,
        w1,
        w2,
        w3_wide,
    )

    swap = lambda i, j: (i ^ 1, j)
    in_plane = lambda k: lambda i, j: (i ^ (k // 2 * 2), j ^ (k % 2))
    in_layer = lambda t: lambda i, j: (i, j ^ (2 * t))

    def kernel(body, count_in, shape, count_out, name, scratch=(), scalars=False):
        return pl.pallas_call(
            body,
            out_shape=(jax.ShapeDtypeStruct(shape, BF16),) * count_out,
            in_specs=[smem] * scalars + [vmem] * count_in,
            out_specs=(vmem,) * count_out,
            scratch_shapes=list(scratch),
            compiler_params=params,
            name=name,
        )

    swapped = grid.move(other, swap)
    blocks = kernel(core_kernel, 2, (layers, shares.rows, LANES), planes, "cores")(own, swapped)
    blocks = [blocks[0]] + [grid.move(blocks[k], in_plane(k)) for k in range(1, planes)]
    body = functools.partial(plane_kernel, shares)
    blocks = kernel(body, planes, (shares.mid_rows, LANES), layers, "planes")(*blocks)
    blocks = [blocks[0]] + [grid.move(blocks[t], in_layer(t)) for t in range(1, layers)]
    scratch = (
        pltpu.VMEM((shares.ranks, shares.xz_slot, LANES), F32),
        pltpu.VMEM((grid.ny, 8, LANES), F32),
        pltpu.VMEM((shares.end_rows - shares.small, LANES), F32),
    )
    body = functools.partial(layer_kernel, shares)
    blocks = kernel(body, layers, (shares.end_rows, LANES), layers, "layers", scratch, True)(flags, *blocks)
    blocks = [blocks[0]] + [grid.move(blocks[t], in_layer(t)) for t in range(1, layers)]
    mine = jnp.stack(blocks)
    halves = [mine] + [grid.move(mine, in_plane(k)) for k in range(1, planes)]
    halves = halves + [grid.move(half, swap) for half in halves]
    g1, g2, gt, gw1, gw2, gw3, gxz, gyz = pl.pallas_call(
        functools.partial(last_kernel, shares, classes),
        out_shape=(
            jax.ShapeDtypeStruct((9, width, width), F32),
            jax.ShapeDtypeStruct((9, width, width), F32),
            jax.ShapeDtypeStruct((width, width), F32),
            jax.ShapeDtypeStruct((width, hidden), F32),
            jax.ShapeDtypeStruct((hidden, hidden), F32),
            jax.ShapeDtypeStruct((classes, hidden), F32),
            jax.ShapeDtypeStruct((chips // 2, shares.xz_rows, width), F32),
            jax.ShapeDtypeStruct((2 * ncols * depth, width), F32),
        ),
        in_specs=[smem] + [vmem] * (2 * planes + 1),
        out_specs=(vmem,) * 8,
        scratch_shapes=[
            pltpu.VMEM((2, chips, shares.each, LANES), BF16),
            pltpu.VMEM((2, chips, shares.end_rows - shares.each, LANES), F32),
        ],
        compiler_params=params,
        name="spread",
    )(
        flags,
        *halves,
        emb.reshape(width, 1),
    )
    shape = (3, 3, width, width)
    return (
        g1.reshape(shape),
        g2.reshape(shape),
        gt,
        gw1,
        gw2,
        gw3.T,
        gxz.reshape(share, depth, width),
        gyz.reshape(2 * ncols, depth, width),
    )


def solution(mesh):
    placed = (
        P("gx", "gy", None),
        P("gy", None, None),
        P("gx", None, None),
        P("gx", "gy", None),
        P(),
        P(),
        P(),
        P(),
        P(),
        P(),
        P(),
    )
    return jax.shard_map(
        local,
        mesh=mesh,
        in_specs=placed,
        out_specs=(P(), P(), P(), P(), P(), P(), P("gy", None, None), P("gx", None, None)),
        check_vma=False,
    )
```
